128 devices in a mesh: pre: 8 (over x, core), req: 16 (over y, z).
Axes of the slice: x: 4, y: 4, z: 4, core: 2. Of those that a mesh axis runs over, the one named last changes fastest.
Arguments:
- prefix_kv: bfloat16 [16, 16384, 2048], P('pre', 'req'), may hold values from -9 to 9
- prefix_len: int32 [16], replicated, may hold values from 1 to 16384, 131072 in all
- prefix_of: int32 [256, 1], P('req'), may hold values from 0 to 15; in each aligned block of 16 rows (0 to 15, 16 to 31, ...) at most 2 rows name the same one
- suffix_len: int32 [256], P('req'), may hold values from 1 to 1024, 196608 in all
- suffix_kv: bfloat16 [256, 1024, 2048], P('req', None, 'pre'), may hold values from -9 to 9
- queries: bfloat16 [256, 4, 8192], P('req', None, 'pre'), may hold values from -60 to 60
- new_kv: bfloat16 [256, 4, 2048], P('req', None, 'pre'), may hold values from -12 to 12
Outputs:
- attended: bfloat16 [256, 4, 8192], P('req', None, 'pre')
The draws below stay inside these ranges and needn't reach their ends.
Inputs may be any that keep to these rules, and one draw needn't show every extreme that they name: `prefix_len`: some prefix is 16384 positions long. `prefix_of`: within the rows of one index of req (aligned blocks of 16 requests) no prefix is named by more than 2 requests, and some block reaches 2. `suffix_len`: some request uses all 1024 positions.
All inputs are finite; a program needn't handle non-finite values. No bound on the sum of `suffix_len` on one device may be relied on, other than what follows from the above.
Results may differ from the reference program's by a relative error of at most 0.014.
Values may be sent and summed in bfloat16 or wider, within the bound.
No kernel may reach another device: no remote copies, remote signals or barrier semaphores. Data moves between devices by JAX's collectives and lax.ppermute only.
A program may use at most 128 MiB of HBM per device.

```python
import math
import jax
import jax.numpy as jnp
import numpy as np
from jax import lax

H = 64
KVH = 8
HD = 128
PLEN = 16384
SLEN = 1024
REQ_DEV = 16
STEPS = 4
PREFIXES = 16
REQUESTS = 256
MOST = 2


def base_queries(key):
    inner = jax.random.fold_in(key, 11)
    return 1.7 * jax.random.normal(inner, (REQUESTS, STEPS, KVH, H // KVH, HD), jnp.float32)


def draw_queries(key, part):
    base = base_queries(key)
    values = jnp.clip(base, -12.0, 12.0)
    return values.reshape(REQUESTS, STEPS, H * HD).astype(jnp.bfloat16)


def draw_new_kv(key, part):
    base = base_queries(key)
    key = jax.random.fold_in(key, 2)
    first, second = jax.random.split(key)
    head_mean = jnp.mean(base, axis=3)
    keys_part = jnp.clip(2.7 * head_mean + 0.5 * jax.random.normal(first, (REQUESTS, STEPS, KVH, HD), jnp.float32), -12.0, 12.0)
    values_part = jnp.clip(1.5 * jax.random.normal(second, (REQUESTS, STEPS, KVH, HD), jnp.float32), -9.0, 9.0)
    stacked = jnp.stack([keys_part, values_part], axis=3)
    return stacked.reshape(REQUESTS, STEPS, KVH * 2 * HD).astype(jnp.bfloat16)


def block_levels(key, extent, cuts, smallest, high):
    loudness, own = 1.0, jax.random.fold_in(key, 6)
    for position, parts in cuts:
        heights = jnp.exp(jax.random.uniform(jax.random.fold_in(own, position), (parts,), jnp.float32, smallest / len(cuts), high / len(cuts)))
        loudness = loudness * jnp.repeat(heights, extent[position] // parts).reshape([-1 if axis == position else 1 for axis in range(len(extent))])
    return loudness


def length_profile(count, total, most, skew):
    loads = [(1 << 20) // math.isqrt(standing ** skew) + 1 for standing in range(2, count + 1)]
    spare, counts = total - most - (count - 1), [1] * (count - 1)
    while spare > 0:
        candidates = [i for i in range(count - 1) if counts[i] < most]
        whole, remaining = sum([loads[i] for i in candidates]), spare
        for i in candidates:
            extra = min(most - counts[i], max(1, remaining * loads[i] // whole), spare)
            counts[i] = counts[i] + extra
            spare = spare - extra
    return np.array([most] + counts)


def ragged_sizes(rng, count, total, limit, skew):
    if count == 2:
        one = jax.random.randint(rng, (), max(1, total - limit), min(limit, total - 1) + 1)
        return jnp.stack([one, total - one])
    sizes = jnp.asarray(length_profile(count, total, limit, skew), jnp.int32)
    pairs = (count - 1) // 2
    donor, sink = sizes[1:1 + 2 * pairs:2], sizes[2:2 + 2 * pairs:2]
    slack = jnp.minimum(donor - 1, limit - sink)
    passed = jax.random.randint(jax.random.fold_in(rng, 1), (pairs,), 0, 1 << 20) % (slack + 1)
    sizes = sizes.at[1:1 + 2 * pairs:2].set(donor - passed).at[2:2 + 2 * pairs:2].set(sink + passed)
    return sizes[jax.random.permutation(jax.random.fold_in(rng, 2), count)]


def routed_block(rng, own, number, rows, amount, top, limit, lean):
    sequence = jax.random.permutation(rng, amount)
    heavy_load, common = shares(amount, rows * top, limit, lean, True), shares(amount, rows * top, limit, lean, False)
    places = jnp.arange(amount)

    def named(sizes, offset_by):
        used = int((sizes > 0).sum())
        fixed = max(1, used // 4)
        moved = fixed + (places - fixed + offset_by * (used - fixed)) % max(1, amount - fixed)
        return jnp.zeros((amount,), jnp.int32).at[sequence[jnp.where(places < fixed, places, moved)]].set(jnp.asarray(sizes, jnp.int32))

    sizes = jnp.where(number % 4 == 0, named(heavy_load, number // 4), named(common, number - number // 4 - 1))
    mixed = jax.random.permutation(jax.random.fold_in(own, 3), amount)
    donor, sink = mixed[0:amount // 2 * 2:2], mixed[1:amount // 2 * 2:2]
    margin = jnp.minimum(sizes[donor] - 1, limit - sizes[sink]) // 2
    margin = jnp.where((donor == sequence[0]) | (sink == sequence[0]) | (sizes[sink] == 0), 0, jnp.maximum(margin, 0))
    moved = jax.random.randint(jax.random.fold_in(own, 4), (amount // 2,), 0, 1 << 20) % (margin + 1)
    sizes = sizes.at[donor].add(-moved).at[sink].add(moved)
    items = jnp.searchsorted(jnp.cumsum(sizes), jnp.arange(rows * top), side="right").astype(jnp.int32)
    table = items.reshape(top, rows).T
    table = table[jax.random.permutation(jax.random.fold_in(own, 1), rows)]
    offset_by = jax.random.randint(jax.random.fold_in(own, 2), (rows, 1), 0, top)
    return jnp.take_along_axis(table, (jnp.arange(top)[None, :] + offset_by) % top, axis=1)


def shares(number_of, total, bound, skew, full):
    portions = [(1 << 20) // math.isqrt(grade ** skew) + 1 for grade in range(1, number_of + 1)]
    largest = bound if full else min(bound, max(-(-total // number_of), total * portions[0] // sum(portions)))
    least = 1 if total - largest >= number_of - 1 else 0
    counts, spare = [largest] + [least] * (number_of - 1), total - largest - least * (number_of - 1)
    while spare > 0:
        candidates = [i for i in range(1, number_of) if counts[i] < largest] or [i for i in range(1, number_of) if counts[i] < bound]
        mass, left = sum([portions[i] for i in candidates]), spare
        for i in candidates:
            more = min(bound - counts[i], max(1, left * portions[i] // mass), spare)
            counts[i] = counts[i] + more
            spare = spare - more
    return np.array(counts)


def normal_values(own_key, extent, deviation, limit, shards=(), kind=jnp.bfloat16):
    loudness = block_levels(own_key, extent, shards, -0.22, 0.18) if shards else 1.0
    result = jax.random.normal(own_key, extent, jnp.float32) * deviation * loudness
    return jnp.minimum(jnp.maximum(result, -limit), limit).astype(kind)


def setup_inputs(seed: int = 0) -> dict:
    seeds = jax.random.split(jax.random.key(seed), 8)
    prefix_kv = normal_values(seeds[0], (PREFIXES, PLEN, KVH * 2 * HD), 1.5, 9.0, ((0, 8), (1, 16)))
    prefix_len = ragged_sizes(seeds[1], PREFIXES, PREFIXES * PLEN // 2, PLEN, 2).astype(jnp.int32)
    prefix_of_keys = jax.random.split(jax.random.fold_in(seeds[2], 1), REQUESTS // REQ_DEV)
    prefix_of_turns = jax.random.permutation(jax.random.fold_in(seeds[2], 3), REQUESTS // REQ_DEV)
    prefix_of = jax.vmap(lambda own, number: routed_block(jax.random.fold_in(seeds[2], 2), own, number, REQ_DEV, PREFIXES, 1, MOST, 2))(prefix_of_keys, prefix_of_turns).reshape((REQUESTS, 1))
    suffix_len = ragged_sizes(seeds[3], REQUESTS, REQUESTS * SLEN * 3 // 4, SLEN, 1).astype(jnp.int32)
    suffix_kv = normal_values(seeds[4], (REQUESTS, SLEN, KVH * 2 * HD), 1.5, 9.0, ((0, 16), (2, 8)))
    queries = draw_queries(jax.random.fold_in(seeds[7], 71), 0)
    new_kv = draw_new_kv(jax.random.fold_in(seeds[7], 71), 0)
    return dict(prefix_kv=prefix_kv, prefix_len=prefix_len, prefix_of=prefix_of, suffix_len=suffix_len, suffix_kv=suffix_kv, queries=queries, new_kv=new_kv)


NEG_FILL = -1e+30

def rounded(values):
    narrow = values.astype(jnp.bfloat16)
    narrow = lax.optimization_barrier(narrow)
    return narrow.astype(jnp.float32)

def reference(prefix_kv, prefix_len, prefix_of, suffix_len, suffix_kv, queries, new_kv):
    group_size = H // KVH
    inv_root = 1.0 / math.sqrt(HD)

    def one_request(index):
        owner = prefix_of[index, 0]
        prefix_heads = lax.dynamic_index_in_dim(prefix_kv, owner, 0, keepdims=False).reshape(PLEN, KVH, 2, HD).astype(jnp.float32)
        used_prefix = lax.dynamic_index_in_dim(prefix_len, owner, 0, keepdims=False)
        query_rows = lax.dynamic_index_in_dim(queries, index, 0, keepdims=False).reshape(STEPS, KVH, group_size, HD).astype(jnp.float32)
        cache_heads = lax.dynamic_index_in_dim(suffix_kv, index, 0, keepdims=False).reshape(SLEN, KVH, 2, HD).astype(jnp.float32)
        fresh_heads = lax.dynamic_index_in_dim(new_kv, index, 0, keepdims=False).reshape(STEPS, KVH, 2, HD).astype(jnp.float32)
        used_cache = lax.dynamic_index_in_dim(suffix_len, index, 0, keepdims=False)
        prefix_usable = (jnp.arange(PLEN, dtype=jnp.int32) < used_prefix)[None, None, None, :]
        cache_usable = (jnp.arange(SLEN, dtype=jnp.int32) < used_cache)[None, None, None, :]
        step_iota = jnp.arange(STEPS, dtype=jnp.int32)
        fresh_usable = (step_iota[None, :] <= step_iota[:, None])[:, None, None, :]
        prefix_scores = jnp.einsum('skgd,lkd->skgl', query_rows, prefix_heads[:, :, 0]) * inv_root
        cache_scores = jnp.einsum('skgd,lkd->skgl', query_rows, cache_heads[:, :, 0]) * inv_root
        fresh_scores = jnp.einsum('skgd,tkd->skgt', query_rows, fresh_heads[:, :, 0]) * inv_root
        prefix_scores = jnp.where(prefix_usable, prefix_scores, NEG_FILL)
        cache_scores = jnp.where(cache_usable, cache_scores, NEG_FILL)
        fresh_scores = jnp.where(fresh_usable, fresh_scores, NEG_FILL)
        row_top = jnp.maximum(jnp.maximum(lax.optimization_barrier(jnp.max(prefix_scores, axis=-1)), lax.optimization_barrier(jnp.max(cache_scores, axis=-1))), lax.optimization_barrier(jnp.max(fresh_scores, axis=-1)))
        prefix_w = rounded(jnp.where(prefix_usable, jnp.exp(prefix_scores - row_top[..., None]), 0.0))
        cache_w = rounded(jnp.where(cache_usable, jnp.exp(cache_scores - row_top[..., None]), 0.0))
        fresh_w = rounded(jnp.where(fresh_usable, jnp.exp(fresh_scores - row_top[..., None]), 0.0))
        numerator = jnp.einsum('skgl,lkd->skgd', prefix_w, prefix_heads[:, :, 1])
        numerator = numerator + jnp.einsum('skgl,lkd->skgd', cache_w, cache_heads[:, :, 1])
        numerator = numerator + jnp.einsum('skgt,tkd->skgd', fresh_w, fresh_heads[:, :, 1])
        denominator = lax.optimization_barrier(jnp.sum(prefix_w, axis=-1)) + lax.optimization_barrier(jnp.sum(cache_w, axis=-1)) + lax.optimization_barrier(jnp.sum(fresh_w, axis=-1))
        return (numerator / denominator[..., None]).astype(jnp.bfloat16).reshape(STEPS, H * HD)
    return lax.map(one_request, jnp.arange(REQUESTS, dtype=jnp.int32))
```

```python
import functools
import math

import jax
import jax.numpy as jnp
from jax import lax
from jax.experimental import pallas as pl
from jax.experimental.pallas import tpu as pltpu
from jax.sharding import PartitionSpec as P

HD = 128
GROUP = 8
STEPS = 4
ROWS = STEPS * GROUP
NEG = -1e30
ROOT = 1.0 / math.sqrt(HD)
LOG2E = math.log2(math.e)
LINE = 272
LAST = 144
BF = jnp.bfloat16
F32 = jnp.float32


def params(mb=48):
    return pltpu.CompilerParams(vmem_limit_bytes=mb * 1024 * 1024)


def code_of(i):
    x, core = i >> 1, i & 1
    return core | (((x ^ (x >> 1)) & 1) << 1) | ((x >> 1) << 2)


def index_of(code):
    core, low, high = code & 1, (code >> 1) & 1, (code >> 2) & 1
    x = (high << 1) | (low ^ high)
    return (x << 1) | core


def pre_pairs(rel):
    return [(i, index_of(code_of(i) ^ rel)) for i in range(8)]


def req_pairs(dim):
    flip = (1, 4, 3, 12)[dim]
    return [(j, j ^ flip) for j in range(16)]


def split3(x):
    hi = x.astype(BF).astype(F32)
    mid = (x - hi).astype(BF).astype(F32)
    low = (x - hi - mid).astype(BF).astype(F32)
    return hi, mid, low


def pack_kernel(req_ref, q_ref, *out_refs):
    zero = jnp.zeros((ROWS, HD), BF)
    for rel in range(8):
        for part in range(4):
            r = req_ref[rel * 4 + part]
            rows = q_ref[jnp.maximum(r, 0)]
            out_refs[rel][0, 0, part * ROWS:(part + 1) * ROWS, :] = jnp.where(r >= 0, rows, zero)


def pack(req_of, q_rows):
    return pl.pallas_call(
        pack_kernel,
        out_shape=[jax.ShapeDtypeStruct((1, 1, 128, HD), BF)] * 8,
        in_specs=[pl.BlockSpec(memory_space=pltpu.SMEM), pl.BlockSpec(memory_space=pltpu.VMEM)],
        out_specs=[pl.BlockSpec(memory_space=pltpu.VMEM)] * 8,
        compiler_params=params(),
        name="pack_slots",
    )(req_of, q_rows)


def prefix_kernel(head_ref, use_ref, q_ref, kv_ref, o_ref, lse_ref):
    step = pl.program_id(0)
    m, h = step // 2, step % 2
    usable = use_ref[m]
    base = pl.multiple_of(m * 128 + h * 64, 64)
    positions = kv_ref.shape[1]
    blocks = q_ref.shape[0]
    per = 2
    row_id = lax.broadcasted_iota(jnp.int32, (64, HD), 0)
    lane_id = lax.broadcasted_iota(jnp.int32, (64, HD), 1)
    diag = (lane_id - row_id == h * 64)[None]

    @pl.when(h == 0)
    def _():
        lse_ref[m] = jnp.zeros((blocks, HD), F32)

    def run(masked):
        k = kv_ref[0, :, :HD]
        v1 = jnp.concatenate([kv_ref[0, :, HD:], jnp.ones((positions, HD), BF)], axis=1)
        for c in range(0, blocks, per):
            q = q_ref[c:c + per, 0].reshape(per * 64, HD)
            s = lax.dot_general(q, k, (((1,), (1,)), ((), ())), preferred_element_type=F32)
            if masked:
                pos = lax.broadcasted_iota(jnp.int32, s.shape, 1)
                s = jnp.where(pos < usable, s, NEG)
            top = jnp.max(s, axis=1, keepdims=True)
            p = jnp.exp2((s - top) * (ROOT * LOG2E)).astype(BF)
            r = jnp.dot(p, v1, preferred_element_type=F32)
            den = r[:, HD:]
            o = r[:, :HD] / den
            lse = top * ROOT + jnp.log(den)
            o_ref[c:c + per, pl.ds(base, 64), :] = o.reshape(per, 64, HD).astype(BF)
            flat = jnp.sum(jnp.where(diag, lse.reshape(per, 64, HD), 0.0), axis=1)
            lse_ref[m, c:c + per, :] = lse_ref[m, c:c + per, :] + flat

    @pl.when(usable >= positions)
    def _():
        run(False)

    @pl.when((usable > 0) & (usable < positions))
    def _():
        run(True)

    @pl.when(usable <= 0)
    def _():
        o_ref[:, pl.ds(base, 64), :] = jnp.zeros((blocks, 64, HD), BF)
        lse_ref[m] = jnp.full((blocks, HD), NEG, F32)

    @pl.when(step == 3)
    def _():
        o_ref[:, 256:LINE, :] = lse_rows([lse_ref[0][:, None, :], lse_ref[1][:, None, :]])


def lse_rows(tops):
    shape = (tops[0].shape[0], 16, HD)
    row = lax.broadcasted_iota(jnp.int32, shape, 1)
    out = jnp.zeros(shape, F32)
    at = 0
    for top in tops:
        for piece in split3(top):
            out = jnp.where(row == at, jnp.broadcast_to(piece, shape), out)
            at += 1
    return out.astype(BF)


def prefix_attention(head_of, usable, q, prefix_kv, quarter):
    blocks = q.shape[0]
    positions = prefix_kv.shape[1]
    grid_spec = pltpu.PrefetchScalarGridSpec(
        num_scalar_prefetch=2,
        grid=(4,),
        in_specs=[
            pl.BlockSpec((blocks, 1, 64, HD), lambda s, head, use: (0, s % 2, s // 2, 0)),
            pl.BlockSpec(
                (1, positions, 2 * HD), lambda s, head, use: (s // 2, 0, head[2 * quarter + s % 2])
            ),
        ],
        out_specs=pl.BlockSpec((blocks, LINE, HD), lambda s, head, use: (0, 0, 0)),
        scratch_shapes=[pltpu.VMEM((2, blocks, HD), F32)],
    )
    rows = blocks * 64 * 4
    return pl.pallas_call(
        prefix_kernel,
        out_shape=jax.ShapeDtypeStruct((blocks, LINE, HD), BF),
        grid_spec=grid_spec,
        compiler_params=params(),
        cost_estimate=pl.CostEstimate(
            flops=rows * positions * 128 * 8, bytes_accessed=4 << 20, transcendentals=rows * positions
        ),
        name="prefix_attention",
    )(head_of, usable, q, prefix_kv)


def blend_weights(la, lb):
    top = jnp.maximum(la, lb)
    ea, eb = jnp.exp(la - top), jnp.exp(lb - top)
    total = ea + eb
    return ea / total, top + jnp.log(total)


def spread(w):
    return jnp.broadcast_to(w, (HD, HD)).T


def read_lse(rows, m):
    return rows[3 * m:3 * m + 1] + rows[3 * m + 1:3 * m + 2] + rows[3 * m + 2:3 * m + 3]


def merge_line(a_ref, b_ref, idx):
    ra = a_ref[idx, 256:LINE, :].astype(F32)
    rb = b_ref[idx, 256:LINE, :].astype(F32)
    datas, tops = [], []
    for m in range(2):
        wa, lse = blend_weights(read_lse(ra, m), read_lse(rb, m))
        oa = a_ref[idx, m * 128:(m + 1) * 128, :].astype(F32)
        ob = b_ref[idx, m * 128:(m + 1) * 128, :].astype(F32)
        datas.append(ob + spread(wa) * (oa - ob))
        tops.append(lse)
    return datas, tops


def merge_kernel(a_ref, b_ref, keep_ref, send_ref):
    half = keep_ref.shape[0]
    for out_ref, first in ((send_ref, half), (keep_ref, 0)):
        for b in range(half):
            datas, tops = merge_line(a_ref, b_ref, first + b)
            for m in range(2):
                out_ref[b, m * 128:(m + 1) * 128, :] = datas[m].astype(BF)
            out_ref[b, 256:LINE, :] = lse_rows([t[None] for t in tops])[0]


def merge(mine, received):
    blocks = mine.shape[0]
    half = blocks // 2
    one = jax.ShapeDtypeStruct((half, LINE, HD), BF)
    return pl.pallas_call(
        merge_kernel,
        out_shape=[one, one],
        in_specs=[pl.BlockSpec(memory_space=pltpu.VMEM)] * 2,
        out_specs=[pl.BlockSpec(memory_space=pltpu.VMEM)] * 2,
        compiler_params=params(),
        cost_estimate=pl.CostEstimate(
            flops=blocks * 256 * 128 * 6, bytes_accessed=blocks * LINE * HD * 6, transcendentals=0
        ),
        name="merge_step",
    )(mine, received)


def last_kernel(a_ref, b_ref, *out_refs):
    datas, tops = merge_line(a_ref, b_ref, 0)
    lane = lax.broadcasted_iota(jnp.int32, (1, HD), 1)
    low = lane < 64
    wide = [jnp.broadcast_to(t, (8, HD)) for t in tops]
    rolled = [pltpu.roll(t, 64, 1)[0:1] for t in wide]
    joined = (
        jnp.where(low, tops[0], rolled[1]),
        jnp.where(low, rolled[0], tops[1]),
    )
    for h in range(2):
        for m in range(2):
            out_refs[h][m * 64:(m + 1) * 64, :] = datas[m][h * 64:(h + 1) * 64].astype(BF)
        out_refs[h][128:LAST, :] = lse_rows([joined[h][None]])[0]


def merge_last(mine, received):
    one = jax.ShapeDtypeStruct((LAST, HD), BF)
    return pl.pallas_call(
        last_kernel,
        out_shape=[one, one],
        in_specs=[pl.BlockSpec(memory_space=pltpu.VMEM)] * 2,
        out_specs=[pl.BlockSpec(memory_space=pltpu.VMEM)] * 2,
        compiler_params=params(),
        name="merge_last",
    )(mine, received)


def suffix_kernel(len_ref, q_ref, kv_ref, new_ref, o_ref, lse_ref):
    per = q_ref.shape[0]
    positions = kv_ref.shape[1]
    step_id = lax.broadcasted_iota(jnp.int32, (ROWS, 1), 0) // GROUP
    pos = lax.broadcasted_iota(jnp.int32, (ROWS, positions), 1)
    ones = jnp.ones((positions, HD), BF)
    for e in range(per):
        used = len_ref[pl.program_id(0) * per + e]
        q = q_ref[e]
        qf = q.astype(F32)
        fresh = new_ref[e].astype(F32)
        s = lax.dot_general(
            q, kv_ref[e, :, :HD], (((1,), (1,)), ((), ())), preferred_element_type=F32
        )
        s = jnp.where(pos < used, s, NEG)
        top = jnp.max(s, axis=1, keepdims=True)
        extra = []
        for t in range(STEPS):
            f = jnp.sum(qf * fresh[t:t + 1, :HD], axis=1, keepdims=True)
            f = jnp.where(step_id >= t, f, NEG)
            extra.append(f)
            top = jnp.maximum(top, f)
        p = jnp.exp2((s - top) * (ROOT * LOG2E)).astype(BF)
        r = jnp.dot(
            p, jnp.concatenate([kv_ref[e, :, HD:], ones], axis=1), preferred_element_type=F32
        )
        num, den = r[:, :HD], r[:, HD:]
        for t in range(STEPS):
            w = jnp.exp2((extra[t] - top) * (ROOT * LOG2E))
            num = num + w * fresh[t:t + 1, HD:]
            den = den + w
        o_ref[e] = num / den
        lse_ref[e] = top * ROOT + jnp.log(den)


def suffix_attention(suffix_len, q_rows, suffix_kv, new_kv):
    count = q_rows.shape[0]
    positions = suffix_kv.shape[1]
    per = 4
    one = jax.ShapeDtypeStruct((count, ROWS, HD), F32)
    grid_spec = pltpu.PrefetchScalarGridSpec(
        num_scalar_prefetch=1,
        grid=(count // per,),
        in_specs=[
            pl.BlockSpec((per, ROWS, HD), lambda s, n: (s, 0, 0)),
            pl.BlockSpec((per, positions, 2 * HD), lambda s, n: (s, 0, 0)),
            pl.BlockSpec((per, STEPS, 2 * HD), lambda s, n: (s, 0, 0)),
        ],
        out_specs=[pl.BlockSpec((per, ROWS, HD), lambda s, n: (s, 0, 0))] * 2,
    )
    return pl.pallas_call(
        suffix_kernel,
        out_shape=[one, one],
        grid_spec=grid_spec,
        compiler_params=params(),
        cost_estimate=pl.CostEstimate(
            flops=count * 256 * positions * 128 * 4,
            bytes_accessed=9 << 20,
            transcendentals=count * ROWS * positions,
        ),
        name="suffix_attention",
    )(suffix_len, q_rows, suffix_kv, new_kv)


def final_kernel(rel_ref, off_ref, o_ref, lse_ref, *rest):
    parts, out_ref, data_ref, top_ref = rest[:8], rest[8], rest[9], rest[10]
    for t in range(8):
        data_ref[t] = parts[t][0:128, :].astype(F32)
        rows = parts[t][128:LAST, :].astype(F32)
        top_ref[t] = spread(read_lse(rows, 0))
    for r in range(o_ref.shape[0]):
        at = pl.ds(pl.multiple_of(off_ref[r], ROWS), ROWS)
        op, lp = data_ref[rel_ref[r], at, :], top_ref[rel_ref[r], at, :]
        w, _ = blend_weights(lp, lse_ref[r])
        ol = o_ref[r]
        out_ref[r] = (ol + w * (op - ol)).astype(BF)


def finish(rel, off, o_local, lse_local, parts):
    return pl.pallas_call(
        final_kernel,
        out_shape=jax.ShapeDtypeStruct(o_local.shape, BF),
        in_specs=[pl.BlockSpec(memory_space=pltpu.SMEM)] * 2
        + [pl.BlockSpec(memory_space=pltpu.VMEM)] * 10,
        out_specs=pl.BlockSpec(memory_space=pltpu.VMEM),
        scratch_shapes=[pltpu.VMEM((8, HD, HD), F32), pltpu.VMEM((8, HD, HD), F32)],
        compiler_params=params(),
        name="finish",
    )(rel, off, o_local, lse_local, *parts)


def on_device(prefix_kv, prefix_len, prefix_of, suffix_len, suffix_kv, queries, new_kv):
    mine, block = lax.axis_index("pre"), lax.axis_index("req")
    code = code_of(mine)
    shard = prefix_kv.shape[1]
    count = queries.shape[0]

    owners = prefix_of[:, 0]
    ids = jnp.arange(count, dtype=jnp.int32)
    earlier = (owners[None, :] == owners[:, None]) & (ids[None, :] < ids[:, None])
    rank = jnp.sum(earlier.astype(jnp.int32), axis=1)
    rel = code_of(owners >> 1) ^ code
    part = (owners & 1) * 2 + rank
    slot = rel * 4 + part
    match = slot[None, :] == jnp.arange(32, dtype=jnp.int32)[:, None]
    req_of = jnp.max(jnp.where(match, ids[None, :], -1), axis=1)
    head_of = index_of(code ^ jnp.arange(8, dtype=jnp.int32))
    own_len = lax.dynamic_slice_in_dim(prefix_len, mine * 2, 2, 0)
    usable = jnp.clip(own_len - block * shard, 0, shard)

    q_rows = queries.reshape(count, ROWS, HD)
    packed = pack(req_of, q_rows)
    heads = [packed[0]] + [lax.ppermute(packed[t], "pre", pre_pairs(t)) for t in range(1, 8)]
    o_local, lse_local = suffix_attention(suffix_len, q_rows, suffix_kv, new_kv)

    have = [jnp.concatenate([heads[2 * k], heads[2 * k + 1]], axis=1) for k in range(4)]
    for t in range(3):
        got = [lax.ppermute(have[k], "req", req_pairs((k + t) % 4)) for k in range(4)]
        have = [jnp.concatenate([have[k], got[k]], axis=0) for k in range(4)]
    far = [lax.ppermute(have[k], "req", req_pairs((k + 3) % 4)) for k in range(4)]
    keep = [prefix_attention(head_of, usable, have[k], prefix_kv, k) for k in range(4)]
    send = [prefix_attention(head_of, usable, far[k], prefix_kv, k) for k in range(4)]
    for t in range(3, 0, -1):
        got = [lax.ppermute(send[k], "req", req_pairs((k + t) % 4)) for k in range(4)]
        both = [merge(keep[k], got[k]) for k in range(4)]
        keep, send = [b[0] for b in both], [b[1] for b in both]
    got = [lax.ppermute(send[k], "req", req_pairs(k)) for k in range(4)]
    tiles = []
    for k in range(4):
        tiles += merge_last(keep[k], got[k])
    back = [tiles[0]] + [lax.ppermute(tiles[t], "pre", pre_pairs(t)) for t in range(1, 8)]
    out = finish(rel, part * ROWS, o_local, lse_local, back)
    return out.reshape(queries.shape)


def solution(mesh):
    placed = (
        P("pre", "req", None),
        P(),
        P("req", None),
        P("req"),
        P("req", None, "pre"),
        P("req", None, "pre"),
        P("req", None, "pre"),
    )
    return jax.shard_map(
        on_device, mesh=mesh, in_specs=placed, out_specs=P("req", None, "pre"), check_vma=False
    )
```

```python
import functools
import math

import jax
import jax.numpy as jnp
from jax import lax
from jax.experimental import pallas as pl
from jax.experimental.pallas import tpu as pltpu
from jax.sharding import PartitionSpec as P

HD = 128
GROUP = 8
STEPS = 4
ROWS = STEPS * GROUP
NEG = -1e30
ROOT = 1.0 / math.sqrt(HD)
LOG2E = math.log2(math.e)
LINE = 528
LAST = 144
BF = jnp.bfloat16
F32 = jnp.float32


def params(mb=32):
    return pltpu.CompilerParams(vmem_limit_bytes=mb * 1024 * 1024)


def code_of(i):
    x, core = i >> 1, i & 1
    return core | (((x ^ (x >> 1)) & 1) << 1) | ((x >> 1) << 2)


def index_of(code):
    core, low, high = code & 1, (code >> 1) & 1, (code >> 2) & 1
    x = (high << 1) | (low ^ high)
    return (x << 1) | core


def pre_pairs(rel):
    return [(i, index_of(code_of(i) ^ rel)) for i in range(8)]


def req_pairs(half, turn):
    pairs = []
    for i in range(8):
        flip = (1, 4, 3, 12)[(2 * (i & 1) + half + turn) % 4]
        pairs += [(i * 16 + j, i * 16 + (j ^ flip)) for j in range(16)]
    return pairs


def over_req(x, half, turn):
    return lax.ppermute(x, ("pre", "req"), req_pairs(half, turn))


def split3(x):
    hi = x.astype(BF).astype(F32)
    mid = (x - hi).astype(BF).astype(F32)
    low = (x - hi - mid).astype(BF).astype(F32)
    return hi, mid, low


def pack_kernel(code_ref, of_ref, q_ref, rows_ref, *rest):
    out_refs, wide_ref, seen_ref, req_ref = rest[:8], rest[8], rest[9], rest[10]
    count = q_ref.shape[0]
    code = code_ref[0]
    for p in range(16):
        seen_ref[p] = 0
    for slot in range(32):
        req_ref[slot] = -1
    for r in range(count):
        p = of_ref[r]
        rank = seen_ref[p]
        seen_ref[p] = rank + 1
        req_ref[(code_of(p >> 1) ^ code) * 4 + (p & 1) * 2 + rank] = r
    for g in range(GROUP):
        wide_ref[:, pl.ds(g, STEPS, GROUP), :] = q_ref[:, :, g * HD:(g + 1) * HD].astype(F32)
    rows_ref[...] = wide_ref[...].astype(BF)
    zero = jnp.zeros((ROWS, HD), BF)
    for rel in range(8):
        for part in range(4):
            r = req_ref[rel * 4 + part]
            rows = rows_ref[jnp.maximum(r, 0)]
            out_refs[rel][0, 0, part * ROWS:(part + 1) * ROWS, :] = jnp.where(r >= 0, rows, zero)


def pack(code, owners, queries):
    count = queries.shape[0]
    return pl.pallas_call(
        pack_kernel,
        out_shape=[jax.ShapeDtypeStruct((count, ROWS, HD), BF)]
        + [jax.ShapeDtypeStruct((1, 1, 128, HD), BF)] * 8,
        in_specs=[pl.BlockSpec(memory_space=pltpu.SMEM)] * 2
        + [pl.BlockSpec(memory_space=pltpu.VMEM)],
        out_specs=[pl.BlockSpec(memory_space=pltpu.VMEM)] * 9,
        scratch_shapes=[
            pltpu.VMEM((count, ROWS, HD), F32),
            pltpu.SMEM((16,), jnp.int32),
            pltpu.SMEM((32,), jnp.int32),
        ],
        compiler_params=params(),
        name="pack_slots",
    )(code, owners, queries)


def join_kernel(a_ref, b_ref, after_ref, out_ref):
    half = a_ref.shape[0]
    out_ref[:half] = a_ref[...]
    out_ref[half:] = b_ref[...]


def join(a, b, after):
    return pl.pallas_call(
        join_kernel,
        out_shape=jax.ShapeDtypeStruct((2 * a.shape[0],) + a.shape[1:], BF),
        in_specs=[pl.BlockSpec(memory_space=pltpu.VMEM)] * 2 + [pl.BlockSpec(memory_space=pl.ANY)],
        out_specs=pl.BlockSpec(memory_space=pltpu.VMEM),
        compiler_params=params(),
        name="join",
    )(a, b, after)


def prefix_kernel(head_ref, use_ref, q_ref, kv_ref, o_ref, lse_ref):
    step = pl.program_id(0)
    m, h = step // 4, step % 4
    usable = use_ref[m]
    base = pl.multiple_of(m * 256 + h * 64, 64)
    tile = step // 2
    side = h % 2
    positions = kv_ref.shape[1]
    blocks = q_ref.shape[0]
    row_id = lax.broadcasted_iota(jnp.int32, (64, HD), 0)
    lane_id = lax.broadcasted_iota(jnp.int32, (64, HD), 1)
    diag = (lane_id - row_id == side * 64)[None]

    @pl.when(side == 0)
    def _():
        lse_ref[tile] = jnp.zeros((blocks, HD), F32)

    def run(masked):
        k = kv_ref[0, :, :HD]
        v1 = jnp.concatenate([kv_ref[0, :, HD:], jnp.ones((positions, HD), BF)], axis=1)
        q = q_ref[:, 0].reshape(blocks * 64, HD)
        s = lax.dot_general(q, k, (((1,), (1,)), ((), ())), preferred_element_type=F32)
        if masked:
            pos = lax.broadcasted_iota(jnp.int32, s.shape, 1)
            s = jnp.where(pos < usable, s, NEG)
        top = jnp.max(s, axis=1, keepdims=True)
        p = jnp.exp2((s - top) * (ROOT * LOG2E)).astype(BF)
        r = jnp.dot(p, v1, preferred_element_type=F32)
        den = r[:, HD:]
        o = r[:, :HD] / den
        lse = top * ROOT + jnp.log(den)
        o_ref[:, pl.ds(base, 64), :] = o.reshape(blocks, 64, HD).astype(BF)
        lse_ref[tile] += jnp.sum(jnp.where(diag, lse.reshape(blocks, 64, HD), 0.0), axis=1)

    @pl.when(usable >= positions)
    def _():
        run(False)

    @pl.when((usable > 0) & (usable < positions))
    def _():
        run(True)

    @pl.when(usable <= 0)
    def _():
        o_ref[:, pl.ds(base, 64), :] = jnp.zeros((blocks, 64, HD), BF)
        lse_ref[tile] = jnp.full((blocks, HD), NEG, F32)

    @pl.when(step == 7)
    def _():
        o_ref[:, 512:LINE, :] = lse_rows([lse_ref[i][:, None, :] for i in range(4)])


def lse_rows(tops):
    shape = (tops[0].shape[0], 16, HD)
    row = lax.broadcasted_iota(jnp.int32, shape, 1)
    out = jnp.zeros(shape, F32)
    at = 0
    for top in tops:
        for piece in split3(top):
            out = jnp.where(row == at, jnp.broadcast_to(piece, shape), out)
            at += 1
    return out.astype(BF)


def prefix_attention(head_of, usable, q, prefix_kv, half):
    blocks = q.shape[0]
    positions = prefix_kv.shape[1]
    grid_spec = pltpu.PrefetchScalarGridSpec(
        num_scalar_prefetch=2,
        grid=(8,),
        in_specs=[
            pl.BlockSpec((blocks, 1, 64, HD), lambda s, head, use: (0, s % 4, s // 4, 0)),
            pl.BlockSpec(
                (1, positions, 2 * HD), lambda s, head, use: (s // 4, 0, head[4 * half + s % 4])
            ),
        ],
        out_specs=pl.BlockSpec((blocks, LINE, HD), lambda s, head, use: (0, 0, 0)),
        scratch_shapes=[pltpu.VMEM((4, blocks, HD), F32)],
    )
    rows = blocks * 64 * 8
    return pl.pallas_call(
        prefix_kernel,
        out_shape=jax.ShapeDtypeStruct((blocks, LINE, HD), BF),
        grid_spec=grid_spec,
        compiler_params=params(),
        cost_estimate=pl.CostEstimate(
            flops=rows * positions * 128 * 8, bytes_accessed=8 << 20, transcendentals=rows * positions
        ),
        name="prefix_attention",
    )(head_of, usable, q, prefix_kv)


def blend_weights(la, lb):
    top = jnp.maximum(la, lb)
    ea, eb = jnp.exp(la - top), jnp.exp(lb - top)
    total = ea + eb
    return ea / total, top + jnp.log(total)


def spread(w):
    return jnp.broadcast_to(w, (HD, HD)).T


def read_lse(rows, m):
    return rows[3 * m:3 * m + 1] + rows[3 * m + 1:3 * m + 2] + rows[3 * m + 2:3 * m + 3]


def merge_line(a_ref, b_ref, idx):
    ra = a_ref[idx, 512:LINE, :].astype(F32)
    rb = b_ref[idx, 512:LINE, :].astype(F32)
    datas, tops = [], []
    for m in range(4):
        wa, lse = blend_weights(read_lse(ra, m), read_lse(rb, m))
        oa = a_ref[idx, m * 128:(m + 1) * 128, :].astype(F32)
        ob = b_ref[idx, m * 128:(m + 1) * 128, :].astype(F32)
        datas.append(ob + spread(wa) * (oa - ob))
        tops.append(lse)
    return datas, tops


def merge_kernel(a_ref, b_ref, keep_ref, send_ref):
    half = keep_ref.shape[0]
    for out_ref, first in ((send_ref, half), (keep_ref, 0)):
        for b in range(half):
            datas, tops = merge_line(a_ref, b_ref, first + b)
            for m in range(4):
                out_ref[b, m * 128:(m + 1) * 128, :] = datas[m].astype(BF)
            out_ref[b, 512:LINE, :] = lse_rows([t[None] for t in tops])[0]


def merge(mine, received):
    blocks = mine.shape[0]
    half = blocks // 2
    one = jax.ShapeDtypeStruct((half, LINE, HD), BF)
    return pl.pallas_call(
        merge_kernel,
        out_shape=[one, one],
        in_specs=[pl.BlockSpec(memory_space=pltpu.VMEM)] * 2,
        out_specs=[pl.BlockSpec(memory_space=pltpu.VMEM)] * 2,
        compiler_params=params(),
        cost_estimate=pl.CostEstimate(
            flops=blocks * 512 * 128 * 6, bytes_accessed=blocks * LINE * HD * 6, transcendentals=0
        ),
        name="merge_step",
    )(mine, received)


def last_kernel(a_ref, b_ref, *out_refs):
    datas, tops = merge_line(a_ref, b_ref, 0)
    low = lax.broadcasted_iota(jnp.int32, (1, HD), 1) < 64
    rolled = [pltpu.roll(jnp.broadcast_to(t, (8, HD)), 64, 1)[0:1] for t in tops]
    for h in range(4):
        pair, side = h // 2, h % 2
        if side == 0:
            joined = jnp.where(low, tops[pair], rolled[2 + pair])
        else:
            joined = jnp.where(low, rolled[pair], tops[2 + pair])
        for m in range(2):
            rows = datas[2 * m + pair][side * 64:(side + 1) * 64]
            out_refs[h][m * 64:(m + 1) * 64, :] = rows.astype(BF)
        out_refs[h][128:LAST, :] = lse_rows([joined[None]])[0]


def merge_last(mine, received):
    one = jax.ShapeDtypeStruct((LAST, HD), BF)
    return pl.pallas_call(
        last_kernel,
        out_shape=[one] * 4,
        in_specs=[pl.BlockSpec(memory_space=pltpu.VMEM)] * 2,
        out_specs=[pl.BlockSpec(memory_space=pltpu.VMEM)] * 4,
        compiler_params=params(),
        name="merge_last",
    )(mine, received)


def suffix_kernel(first, len_ref, q_ref, kv_ref, new_ref, o_ref, lse_ref):
    per = q_ref.shape[0]
    positions = kv_ref.shape[1]
    step_id = lax.broadcasted_iota(jnp.int32, (ROWS, 1), 0) // GROUP
    pos = lax.broadcasted_iota(jnp.int32, (ROWS, positions), 1)
    ones = jnp.ones((positions, HD), BF)
    for e in range(per):
        used = len_ref[first + pl.program_id(0) * per + e]
        q = q_ref[e]
        qf = q.astype(F32)
        fresh = new_ref[e].astype(F32)
        s = lax.dot_general(
            q, kv_ref[e, :, :HD], (((1,), (1,)), ((), ())), preferred_element_type=F32
        )
        s = jnp.where(pos < used, s, NEG)
        top = jnp.max(s, axis=1, keepdims=True)
        extra = []
        for t in range(STEPS):
            f = jnp.sum(qf * fresh[t:t + 1, :HD], axis=1, keepdims=True)
            f = jnp.where(step_id >= t, f, NEG)
            extra.append(f)
            top = jnp.maximum(top, f)
        p = jnp.exp2((s - top) * (ROOT * LOG2E)).astype(BF)
        r = jnp.dot(
            p, jnp.concatenate([kv_ref[e, :, HD:], ones], axis=1), preferred_element_type=F32
        )
        num, den = r[:, :HD], r[:, HD:]
        for t in range(STEPS):
            w = jnp.exp2((extra[t] - top) * (ROOT * LOG2E))
            num = num + w * fresh[t:t + 1, HD:]
            den = den + w
        o_ref[e] = num / den
        lse_ref[e] = top * ROOT + jnp.log(den)


def suffix_attention(suffix_len, q_rows, suffix_kv, new_kv, first, count):
    positions = suffix_kv.shape[1]
    per = 4
    skip = first // per
    one = jax.ShapeDtypeStruct((count, ROWS, HD), F32)
    grid_spec = pltpu.PrefetchScalarGridSpec(
        num_scalar_prefetch=1,
        grid=(count // per,),
        in_specs=[
            pl.BlockSpec((per, ROWS, HD), lambda s, n: (s + skip, 0, 0)),
            pl.BlockSpec((per, positions, 2 * HD), lambda s, n: (s + skip, 0, 0)),
            pl.BlockSpec((per, STEPS, 2 * HD), lambda s, n: (s + skip, 0, 0)),
        ],
        out_specs=[pl.BlockSpec((per, ROWS, HD), lambda s, n: (s, 0, 0))] * 2,
    )
    return pl.pallas_call(
        functools.partial(suffix_kernel, first),
        out_shape=[one, one],
        grid_spec=grid_spec,
        compiler_params=params(),
        cost_estimate=pl.CostEstimate(
            flops=count * 256 * positions * 128 * 4,
            bytes_accessed=count << 19,
            transcendentals=count * ROWS * positions,
        ),
        name="suffix_attention",
    )(suffix_len, q_rows, suffix_kv, new_kv)


def final_kernel(rel_ref, off_ref, oa_ref, la_ref, ob_ref, lb_ref, *rest):
    parts, out_ref, data_ref, top_ref, wide_ref = rest[:8], rest[8], rest[9], rest[10], rest[11]
    for t in range(8):
        data_ref[t] = parts[t][0:128, :].astype(F32)
        rows = parts[t][128:LAST, :].astype(F32)
        top_ref[t] = spread(read_lse(rows, 0))
    each = oa_ref.shape[0]
    for r in range(2 * each):
        o_ref, l_ref = (oa_ref, la_ref) if r < each else (ob_ref, lb_ref)
        at = pl.ds(pl.multiple_of(off_ref[r], ROWS), ROWS)
        op, lp = data_ref[rel_ref[r], at, :], top_ref[rel_ref[r], at, :]
        w, _ = blend_weights(lp, l_ref[r % each])
        ol = o_ref[r % each]
        wide_ref[r] = ol + w * (op - ol)
    for g in range(GROUP):
        out_ref[:, :, g * HD:(g + 1) * HD] = wide_ref[:, pl.ds(g, STEPS, GROUP), :].astype(BF)


def finish(rel, off, local, parts):
    count = rel.shape[0]
    return pl.pallas_call(
        final_kernel,
        out_shape=jax.ShapeDtypeStruct((count, STEPS, GROUP * HD), BF),
        in_specs=[pl.BlockSpec(memory_space=pltpu.SMEM)] * 2
        + [pl.BlockSpec(memory_space=pltpu.VMEM)] * 12,
        out_specs=pl.BlockSpec(memory_space=pltpu.VMEM),
        scratch_shapes=[
            pltpu.VMEM((8, HD, HD), F32),
            pltpu.VMEM((8, HD, HD), F32),
            pltpu.VMEM((count, ROWS, HD), F32),
        ],
        compiler_params=params(),
        name="finish",
    )(rel, off, *local, *parts)


def on_device(prefix_kv, prefix_len, prefix_of, suffix_len, suffix_kv, queries, new_kv):
    mine, block = lax.axis_index("pre"), lax.axis_index("req")
    code = code_of(mine)
    shard = prefix_kv.shape[1]
    count = queries.shape[0]

    owners = prefix_of[:, 0]
    ids = jnp.arange(count, dtype=jnp.int32)
    earlier = (owners[None, :] == owners[:, None]) & (ids[None, :] < ids[:, None])
    rank = jnp.sum(earlier.astype(jnp.int32), axis=1)
    rel = code_of(owners >> 1) ^ code
    part = (owners & 1) * 2 + rank
    head_of = index_of(code ^ jnp.arange(8, dtype=jnp.int32))
    own_len = lax.dynamic_slice_in_dim(prefix_len, mine * 2, 2, 0)
    usable = jnp.clip(own_len - block * shard, 0, shard)

    q_rows, *packed = pack(jnp.reshape(code, (1,)), owners, queries)
    heads = [packed[0]] + [lax.ppermute(packed[t], "pre", pre_pairs(t)) for t in range(1, 8)]
    local = []
    for first in (0, count // 2):
        local += suffix_attention(suffix_len, q_rows, suffix_kv, new_kv, first, count // 2)

    have = [jnp.concatenate(heads[4 * a:4 * a + 4], axis=1) for a in range(2)]
    for t in range(3):
        got = [over_req(have[a], a, t) for a in range(2)]
        if t == 0:
            have = [jnp.concatenate([have[a], got[a]], axis=0) for a in range(2)]
        else:
            have = [join(have[a], got[a], local[2 * t - 2]) for a in range(2)]
    far = [over_req(have[a], a, 3) for a in range(2)]
    keep = [prefix_attention(head_of, usable, have[a], prefix_kv, a) for a in range(2)]
    send = [prefix_attention(head_of, usable, far[a], prefix_kv, a) for a in range(2)]
    for t in range(3, 0, -1):
        got = [over_req(send[a], a, t) for a in range(2)]
        both = [merge(keep[a], got[a]) for a in range(2)]
        keep, send = [b[0] for b in both], [b[1] for b in both]
    got = [over_req(send[a], a, 0) for a in range(2)]
    tiles = []
    for a in range(2):
        tiles += merge_last(keep[a], got[a])
    back = [tiles[0]] + [lax.ppermute(tiles[t], "pre", pre_pairs(t)) for t in range(1, 8)]
    return finish(rel, part * ROWS, local, back)


def solution(mesh):
    placed = (
        P("pre", "req", None),
        P(),
        P("req", None),
        P("req"),
        P("req", None, "pre"),
        P("req", None, "pre"),
        P("req", None, "pre"),
    )
    return jax.shard_map(
        on_device, mesh=mesh, in_specs=placed, out_specs=P("req", None, "pre"), check_vma=False
    )
```

```python
import functools
import math

import jax
import jax.numpy as jnp
from jax import lax
from jax.experimental import pallas as pl
from jax.experimental.pallas import tpu as pltpu
from jax.sharding import PartitionSpec as P

HD = 128
GROUP = 8
STEPS = 4
ROWS = STEPS * GROUP
NEG = -1e30
ROOT = 1.0 / math.sqrt(HD)
LOG2E = math.log2(math.e)
EMPTY = 128.0
LAST = 144
BF = jnp.bfloat16
F32 = jnp.float32


def params(mb=48):
    return pltpu.CompilerParams(vmem_limit_bytes=mb * 1024 * 1024)


def code_of(i):
    x, core = i >> 1, i & 1
    return core | (((x ^ (x >> 1)) & 1) << 1) | ((x >> 1) << 2)


def index_of(code):
    core, low, high = code & 1, (code >> 1) & 1, (code >> 2) & 1
    x = (high << 1) | (low ^ high)
    return (x << 1) | core


def pre_pairs(rel):
    return [(i, index_of(code_of(i) ^ rel)) for i in range(8)]


def req_pairs(turn_of_core):
    pairs = []
    for i in range(8):
        flip = (1, 4, 3, 12)[turn_of_core[i & 1] % 4]
        pairs += [(i * 16 + j, i * 16 + (j ^ flip)) for j in range(16)]
    return pairs


def half_step(x, half, turn):
    pairs = req_pairs([half + turn, 2 + half + turn])
    return lax.ppermute(x, ("pre", "req"), pairs)


def quarter_step(x, half, side, turn):
    turn = turn if side == 0 else 5 - turn
    return half_step(x, half, turn)


def split3(x):
    hi = x.astype(BF).astype(F32)
    mid = (x - hi).astype(BF).astype(F32)
    low = (x - hi - mid).astype(BF).astype(F32)
    return hi, mid, low


def pack_kernel(code_ref, of_ref, q_ref, rows_ref, *rest):
    out_refs, wide_ref, seen_ref, req_ref = rest[:8], rest[8], rest[9], rest[10]
    count = q_ref.shape[0]
    code = code_ref[0]
    for p in range(16):
        seen_ref[p] = 0
    for slot in range(32):
        req_ref[slot] = -1
    for r in range(count):
        p = of_ref[r]
        rank = seen_ref[p]
        seen_ref[p] = rank + 1
        req_ref[(code_of(p >> 1) ^ code) * 4 + (p & 1) * 2 + rank] = r
    for g in range(GROUP):
        wide_ref[:, pl.ds(g, STEPS, GROUP), :] = q_ref[:, :, g * HD:(g + 1) * HD].astype(F32)
    rows_ref[...] = wide_ref[...].astype(BF)
    nobody = jnp.full((ROWS, HD), EMPTY, BF)
    for rel in range(8):
        for part in range(4):
            r = req_ref[rel * 4 + part]
            rows = rows_ref[jnp.maximum(r, 0)]
            out_refs[rel][0, 0, part * ROWS:(part + 1) * ROWS, :] = jnp.where(r >= 0, rows, nobody)


def pack(code, owners, queries):
    count = queries.shape[0]
    return pl.pallas_call(
        pack_kernel,
        out_shape=[jax.ShapeDtypeStruct((count, ROWS, HD), BF)]
        + [jax.ShapeDtypeStruct((1, 1, 128, HD), BF)] * 8,
        in_specs=[pl.BlockSpec(memory_space=pltpu.SMEM)] * 2
        + [pl.BlockSpec(memory_space=pltpu.VMEM)],
        out_specs=[pl.BlockSpec(memory_space=pltpu.VMEM)] * 9,
        scratch_shapes=[
            pltpu.VMEM((count, ROWS, HD), F32),
            pltpu.SMEM((16,), jnp.int32),
            pltpu.SMEM((32,), jnp.int32),
        ],
        compiler_params=params(),
        name="pack_slots",
    )(code, owners, queries)


def join_kernel(cuts, a_ref, b_ref, *rest):
    half = a_ref.shape[0]
    out_refs = rest[-cuts:]
    width = a_ref.shape[1] // cuts
    for c in range(cuts):
        out_refs[c][:half] = a_ref[:, c * width:(c + 1) * width]
        out_refs[c][half:] = b_ref[:, c * width:(c + 1) * width]


def join(a, b, cuts=1, after=None):
    extra = [] if after is None else [after]
    shape = (2 * a.shape[0], a.shape[1] // cuts) + a.shape[2:]
    return pl.pallas_call(
        functools.partial(join_kernel, cuts),
        out_shape=[jax.ShapeDtypeStruct(shape, BF)] * cuts,
        in_specs=[pl.BlockSpec(memory_space=pltpu.VMEM)] * 2
        + [pl.BlockSpec(memory_space=pl.ANY)] * len(extra),
        out_specs=[pl.BlockSpec(memory_space=pltpu.VMEM)] * cuts,
        compiler_params=params(),
        name="join",
    )(a, b, *extra)


def prefix_kernel(count, first, head_ref, use_ref, *rest):
    q_refs, kv_hbm, out_refs = rest[:count], rest[count], rest[count + 1:2 * count + 1]
    q_all, kv_all, o_all, sa_ref, sb_ref, bias_ref, lse_ref, item_ref, many_ref, sems = rest[
        2 * count + 1:
    ]
    heads = 2 * count
    positions = kv_all.shape[1]
    blocks = q_all.shape[1]
    rows = blocks * ROWS

    def fetch(m, h):
        at = pl.multiple_of(head_ref[2 * first + h] * (2 * HD), 2 * HD)
        return pltpu.make_async_copy(
            kv_hbm.at[m, :, pl.ds(at, 2 * HD)], kv_all.at[m * heads + h], sems.at[m * heads + h]
        )

    def live(m, rank):
        at = (m * 2 + rank) * ROWS
        mark = jnp.min(q_refs[0][:, 0, at:at + 16, :].astype(F32))
        return (use_ref[m] > 0) & (mark < 100.0)

    many_ref[0] = 0
    for m in range(2):
        for rank in range(2):
            on = live(m, rank)

            @pl.when(on)
            def _():
                n = many_ref[0]
                for h in range(heads):
                    item_ref[n + h] = (m * 2 + rank) * heads + h
                    if rank == 0:
                        fetch(m, h).start()
                many_ref[0] = n + heads

            @pl.when(jnp.logical_not(on))
            def _():
                for side in range(2):
                    at = m * 128 + side * 64 + rank * ROWS
                    o_all[:, :, at:at + ROWS, :] = jnp.zeros((count, blocks, ROWS, HD), BF)

    for m in range(2):
        pos = lax.broadcasted_iota(jnp.int32, (8, positions), 1)
        bias_ref[m] = jnp.where(pos < use_ref[m], 0.0, NEG)
    lse_ref[...] = jnp.full(lse_ref.shape, NEG, F32)
    for c in range(count):
        for side in range(2):
            q_all[2 * c + side] = q_refs[c][:, side]
    n = many_ref[0]
    shift = heads.bit_length() - 1

    def decode(i):
        code = item_ref[jnp.minimum(i, n - 1)]
        h, which = code & (heads - 1), code >> shift
        return h, which, which >> 1, which & 1

    def score(i, s_ref):
        h, which, m, rank = decode(i)

        @pl.when((rank == 0) & (i < n))
        def _():
            fetch(m, h).wait()

        q = q_all[h, :, pl.ds(pl.multiple_of(which * ROWS, ROWS), ROWS), :].reshape(rows, HD)
        k = kv_all[m * heads + h, :, :HD]
        s = lax.dot_general(q, k, (((1,), (1,)), ((), ())), preferred_element_type=F32)
        s = s.reshape(rows // 8, 8, positions) + bias_ref[m][None]
        s_ref[...] = s.reshape(rows, positions)

    def weigh(i, s_ref):
        h, which, m, rank = decode(i)
        c, side = h >> 1, h & 1
        s = s_ref[...]
        top = jnp.max(s, axis=1, keepdims=True)
        p = jnp.exp2((s - top) * (ROOT * LOG2E)).astype(BF)
        v = kv_all[m * heads + h, :, HD:]
        v1 = jnp.concatenate([v, jnp.ones((positions, HD), BF)], axis=1)
        r = jnp.dot(p, v1, preferred_element_type=F32)
        den = r[:, HD:]
        o = r[:, :HD] / den
        lse = top * ROOT + jnp.log(den)
        at = pl.multiple_of(m * 128 + side * 64 + rank * ROWS, ROWS)
        o_all[c, :, pl.ds(at, ROWS), :] = o.reshape(blocks, ROWS, HD).astype(BF)
        part = side * 2 + rank
        row_id = lax.broadcasted_iota(jnp.int32, (ROWS, HD), 0)
        lane_id = lax.broadcasted_iota(jnp.int32, (ROWS, HD), 1)
        diag = (lane_id - row_id == part * ROWS)[None]
        flat = jnp.sum(jnp.where(diag, lse.reshape(blocks, ROWS, HD), 0.0), axis=1)
        lanes = lax.broadcasted_iota(jnp.int32, (blocks, HD), 1) >> 5
        old = lse_ref[c * 2 + m]
        lse_ref[c * 2 + m] = jnp.where(lanes == part, flat, old)

    @pl.when(n > 0)
    def _():
        score(0, sa_ref)

        def body(j, carry):
            score(2 * j + 1, sb_ref)
            weigh(2 * j, sa_ref)
            score(2 * j + 2, sa_ref)
            weigh(2 * j + 1, sb_ref)
            return carry

        lax.fori_loop(0, (n + 1) // 2, body, 0)

    for c in range(count):
        out_refs[c][:, :256, :] = o_all[c]
        out_refs[c][:, 256:, :] = lse_rows([lse_ref[2 * c + m][:, None, :] for m in range(2)])


def lse_rows(tops):
    shape = (tops[0].shape[0], 16, HD)
    row = lax.broadcasted_iota(jnp.int32, shape, 1)
    out = jnp.zeros(shape, F32)
    at = 0
    for top in tops:
        for piece in split3(top):
            out = jnp.where(row == at, jnp.broadcast_to(piece, shape), out)
            at += 1
    return out.astype(BF)


def prefix_attention(head_of, usable, qs, prefix_kv, first):
    count = len(qs)
    heads = 2 * count
    blocks = qs[0].shape[0]
    positions = prefix_kv.shape[1]
    rows = blocks * ROWS
    work = rows * positions * heads * 3
    return pl.pallas_call(
        functools.partial(prefix_kernel, count, first),
        out_shape=[jax.ShapeDtypeStruct((blocks, 272, HD), BF)] * count,
        in_specs=[pl.BlockSpec(memory_space=pltpu.SMEM)] * 2
        + [pl.BlockSpec(memory_space=pltpu.VMEM)] * count
        + [pl.BlockSpec(memory_space=pl.ANY)],
        out_specs=[pl.BlockSpec(memory_space=pltpu.VMEM)] * count,
        scratch_shapes=[
            pltpu.VMEM((heads, blocks, 128, HD), BF),
            pltpu.VMEM((2 * heads, positions, 2 * HD), BF),
            pltpu.VMEM((count, blocks, 256, HD), BF),
            pltpu.VMEM((rows, positions), F32),
            pltpu.VMEM((rows, positions), F32),
            pltpu.VMEM((2, 8, positions), F32),
            pltpu.VMEM((heads, blocks, HD), F32),
            pltpu.SMEM((4 * heads,), jnp.int32),
            pltpu.SMEM((1,), jnp.int32),
            pltpu.SemaphoreType.DMA((2 * heads,)),
        ],
        compiler_params=params(),
        cost_estimate=pl.CostEstimate(
            flops=work * 512, bytes_accessed=heads << 20, transcendentals=work
        ),
        name="prefix_attention",
    )(head_of, usable, *qs, prefix_kv)


def blend_weights(la, lb):
    top = jnp.maximum(la, lb)
    ea, eb = jnp.exp(la - top), jnp.exp(lb - top)
    total = ea + eb
    return ea / total, top + jnp.log(total)


def spread(w):
    return jnp.broadcast_to(w, (HD, HD)).T


def read_lse(rows, m):
    return rows[3 * m:3 * m + 1] + rows[3 * m + 1:3 * m + 2] + rows[3 * m + 2:3 * m + 3]


def merge_line(a_ref, b_ref, idx):
    tiles = a_ref.shape[1] // 128
    ra = a_ref[idx, tiles * 128:, :].astype(F32)
    rb = b_ref[idx, tiles * 128:, :].astype(F32)
    datas, tops = [], []
    for m in range(tiles):
        wa, lse = blend_weights(read_lse(ra, m), read_lse(rb, m))
        oa = a_ref[idx, m * 128:(m + 1) * 128, :].astype(F32)
        ob = b_ref[idx, m * 128:(m + 1) * 128, :].astype(F32)
        datas.append(ob + spread(wa) * (oa - ob))
        tops.append(lse)
    return datas, tops


def merge_kernel(*refs):
    pairs, (keep_ref, send_ref) = refs[:-2], refs[-2:]
    half = keep_ref.shape[0]
    for out_ref, first in ((send_ref, half), (keep_ref, 0)):
        for b in range(half):
            merged = [
                merge_line(pairs[2 * c], pairs[2 * c + 1], first + b) for c in range(len(pairs) // 2)
            ]
            datas = [d for row in zip(*[x[0] for x in merged]) for d in row]
            tops = [t for row in zip(*[x[1] for x in merged]) for t in row]
            tiles = len(datas)
            for m in range(tiles):
                out_ref[b, m * 128:(m + 1) * 128, :] = datas[m].astype(BF)
            out_ref[b, tiles * 128:, :] = lse_rows([t[None] for t in tops])[0]


def merge(*pairs):
    blocks, line = pairs[0].shape[:2]
    tiles = (line // 128) * (len(pairs) // 2)
    one = jax.ShapeDtypeStruct((blocks // 2, tiles * 128 + 16, HD), BF)
    return pl.pallas_call(
        merge_kernel,
        out_shape=[one, one],
        in_specs=[pl.BlockSpec(memory_space=pltpu.VMEM)] * len(pairs),
        out_specs=[pl.BlockSpec(memory_space=pltpu.VMEM)] * 2,
        compiler_params=params(),
        cost_estimate=pl.CostEstimate(
            flops=blocks * tiles * 128 * 128 * 6,
            bytes_accessed=blocks * tiles * 128 * HD * 6,
            transcendentals=0,
        ),
        name="merge_step",
    )(*pairs)


def last_kernel(a_ref, b_ref, *out_refs):
    datas, tops = merge_line(a_ref, b_ref, 0)
    low = lax.broadcasted_iota(jnp.int32, (1, HD), 1) < 64
    rolled = [pltpu.roll(jnp.broadcast_to(t, (8, HD)), 64, 1)[0:1] for t in tops]
    for h in range(4):
        pair, side = h // 2, h % 2
        if side == 0:
            joined = jnp.where(low, tops[pair], rolled[2 + pair])
        else:
            joined = jnp.where(low, rolled[pair], tops[2 + pair])
        for m in range(2):
            rows = datas[2 * m + pair][side * 64:(side + 1) * 64]
            out_refs[h][m * 64:(m + 1) * 64, :] = rows.astype(BF)
        out_refs[h][128:LAST, :] = lse_rows([joined[None]])[0]


def merge_last(mine, received):
    one = jax.ShapeDtypeStruct((LAST, HD), BF)
    return pl.pallas_call(
        last_kernel,
        out_shape=[one] * 4,
        in_specs=[pl.BlockSpec(memory_space=pltpu.VMEM)] * 2,
        out_specs=[pl.BlockSpec(memory_space=pltpu.VMEM)] * 4,
        compiler_params=params(),
        name="merge_last",
    )(mine, received)


def suffix_kernel(first, len_ref, q_ref, kv_ref, new_ref, o_ref, lse_ref):
    per = q_ref.shape[0]
    positions = kv_ref.shape[1]
    step_id = lax.broadcasted_iota(jnp.int32, (ROWS, 1), 0) // GROUP
    pos = lax.broadcasted_iota(jnp.int32, (ROWS, positions), 1)
    ones = jnp.ones((positions, HD), BF)
    for e in range(per):
        used = len_ref[first + pl.program_id(0) * per + e]
        q = q_ref[e]
        qf = q.astype(F32)
        fresh = new_ref[e].astype(F32)
        s = lax.dot_general(
            q, kv_ref[e, :, :HD], (((1,), (1,)), ((), ())), preferred_element_type=F32
        )
        s = jnp.where(pos < used, s, NEG)
        top = jnp.max(s, axis=1, keepdims=True)
        extra = []
        for t in range(STEPS):
            f = jnp.sum(qf * fresh[t:t + 1, :HD], axis=1, keepdims=True)
            f = jnp.where(step_id >= t, f, NEG)
            extra.append(f)
            top = jnp.maximum(top, f)
        p = jnp.exp2((s - top) * (ROOT * LOG2E)).astype(BF)
        r = jnp.dot(
            p, jnp.concatenate([kv_ref[e, :, HD:], ones], axis=1), preferred_element_type=F32
        )
        num, den = r[:, :HD], r[:, HD:]
        for t in range(STEPS):
            w = jnp.exp2((extra[t] - top) * (ROOT * LOG2E))
            num = num + w * fresh[t:t + 1, HD:]
            den = den + w
        o_ref[e] = num / den
        lse_ref[e] = top * ROOT + jnp.log(den)


def suffix_attention(suffix_len, q_rows, suffix_kv, new_kv, first, count):
    positions = suffix_kv.shape[1]
    per = 4
    skip = first // per
    one = jax.ShapeDtypeStruct((count, ROWS, HD), F32)
    grid_spec = pltpu.PrefetchScalarGridSpec(
        num_scalar_prefetch=1,
        grid=(count // per,),
        in_specs=[
            pl.BlockSpec((per, ROWS, HD), lambda s, n: (s + skip, 0, 0)),
            pl.BlockSpec((per, positions, 2 * HD), lambda s, n: (s + skip, 0, 0)),
            pl.BlockSpec((per, STEPS, 2 * HD), lambda s, n: (s + skip, 0, 0)),
        ],
        out_specs=[pl.BlockSpec((per, ROWS, HD), lambda s, n: (s, 0, 0))] * 2,
    )
    return pl.pallas_call(
        functools.partial(suffix_kernel, first),
        out_shape=[one, one],
        grid_spec=grid_spec,
        compiler_params=params(),
        cost_estimate=pl.CostEstimate(
            flops=count * 256 * positions * 128 * 4,
            bytes_accessed=count << 19,
            transcendentals=count * ROWS * positions,
        ),
        name="suffix_attention",
    )(suffix_len, q_rows, suffix_kv, new_kv)


def final_kernel(rel_ref, off_ref, oa_ref, la_ref, ob_ref, lb_ref, *rest):
    parts, out_ref, data_ref, top_ref, wide_ref = rest[:8], rest[8], rest[9], rest[10], rest[11]
    for t in range(8):
        data_ref[t] = parts[t][0:128, :].astype(F32)
        rows = parts[t][128:LAST, :].astype(F32)
        top_ref[t] = spread(read_lse(rows, 0))
    each = oa_ref.shape[0]
    for r in range(2 * each):
        o_ref, l_ref = (oa_ref, la_ref) if r < each else (ob_ref, lb_ref)
        at = pl.ds(pl.multiple_of(off_ref[r], ROWS), ROWS)
        op, lp = data_ref[rel_ref[r], at, :], top_ref[rel_ref[r], at, :]
        w, _ = blend_weights(lp, l_ref[r % each])
        ol = o_ref[r % each]
        wide_ref[r] = ol + w * (op - ol)
    for g in range(GROUP):
        out_ref[:, :, g * HD:(g + 1) * HD] = wide_ref[:, pl.ds(g, STEPS, GROUP), :].astype(BF)


def finish(rel, off, local, parts):
    count = rel.shape[0]
    return pl.pallas_call(
        final_kernel,
        out_shape=jax.ShapeDtypeStruct((count, STEPS, GROUP * HD), BF),
        in_specs=[pl.BlockSpec(memory_space=pltpu.SMEM)] * 2
        + [pl.BlockSpec(memory_space=pltpu.VMEM)] * 12,
        out_specs=pl.BlockSpec(memory_space=pltpu.VMEM),
        scratch_shapes=[
            pltpu.VMEM((8, HD, HD), F32),
            pltpu.VMEM((8, HD, HD), F32),
            pltpu.VMEM((count, ROWS, HD), F32),
        ],
        compiler_params=params(),
        name="finish",
    )(rel, off, *local, *parts)


def on_device(prefix_kv, prefix_len, prefix_of, suffix_len, suffix_kv, queries, new_kv):
    mine, block = lax.axis_index("pre"), lax.axis_index("req")
    code = code_of(mine)
    shard = prefix_kv.shape[1]
    count = queries.shape[0]

    owners = prefix_of[:, 0]
    ids = jnp.arange(count, dtype=jnp.int32)
    earlier = (owners[None, :] == owners[:, None]) & (ids[None, :] < ids[:, None])
    rank = jnp.sum(earlier.astype(jnp.int32), axis=1)
    rel = code_of(owners >> 1) ^ code
    part = (owners & 1) * 2 + rank
    head_of = index_of(code ^ jnp.arange(8, dtype=jnp.int32))
    own_len = lax.dynamic_slice_in_dim(prefix_len, mine * 2, 2, 0)
    usable = jnp.clip(own_len - block * shard, 0, shard)

    q_rows, *packed = pack(jnp.reshape(code, (1,)), owners, queries)
    heads = [packed[0]] + [lax.ppermute(packed[t], "pre", pre_pairs(t)) for t in range(1, 8)]
    local = []
    for first in (0, count // 2):
        local += suffix_attention(suffix_len, q_rows, suffix_kv, new_kv, first, count // 2)

    both = [(a, side) for a in range(2) for side in range(2)]
    have = [jnp.concatenate(heads[4 * a:4 * a + 4], axis=1) for a in range(2)]
    got = [half_step(have[a], a, 0) for a in range(2)]
    have = [join(have[a], got[a], 1, local[0])[0] for a in range(2)]
    got = [half_step(have[a], a, 1) for a in range(2)]
    near = [x for a in range(2) for x in join(have[a], got[a], 2, local[2])]
    got = [quarter_step(near[k], *both[k], 2) for k in range(4)]
    near = [join(near[k], got[k])[0] for k in range(4)]
    far = [quarter_step(near[k], *both[k], 3) for k in range(4)]
    keep = prefix_attention(head_of, usable, near, prefix_kv, 0)
    send = []
    for a in range(2):
        send += prefix_attention(head_of, usable, far[2 * a:2 * a + 2], prefix_kv, 2 * a)
    got = [quarter_step(send[k], *both[k], 3) for k in range(4)]
    parts = [merge(keep[k], got[k]) for k in range(4)]
    keep, send = [p[0] for p in parts], [p[1] for p in parts]
    got = [quarter_step(send[k], *both[k], 2) for k in range(4)]
    parts = [merge(keep[2 * a], got[2 * a], keep[2 * a + 1], got[2 * a + 1]) for a in range(2)]
    keep, send = [p[0] for p in parts], [p[1] for p in parts]
    got = [half_step(send[a], a, 1) for a in range(2)]
    parts = [merge(keep[a], got[a]) for a in range(2)]
    keep, send = [p[0] for p in parts], [p[1] for p in parts]
    got = [half_step(send[a], a, 0) for a in range(2)]
    tiles = []
    for a in range(2):
        tiles += merge_last(keep[a], got[a])
    back = [tiles[0]] + [lax.ppermute(tiles[t], "pre", pre_pairs(t)) for t in range(1, 8)]
    return finish(rel, part * ROWS, local, back)


def solution(mesh):
    placed = (
        P("pre", "req", None),
        P(),
        P("req", None),
        P("req"),
        P("req", None, "pre"),
        P("req", None, "pre"),
        P("req", None, "pre"),
    )
    return jax.shard_map(
        on_device, mesh=mesh, in_specs=placed, out_specs=P("req", None, "pre"), check_vma=False
    )
```

```python
import functools
import math

import jax
import jax.numpy as jnp
from jax import lax
from jax.experimental import pallas as pl
from jax.experimental.pallas import tpu as pltpu
from jax.sharding import PartitionSpec as P

HD = 128
GROUP = 8
STEPS = 4
ROWS = STEPS * GROUP
NEG = -1e30
ROOT = 1.0 / math.sqrt(HD)
LOG2E = math.log2(math.e)
EMPTY = 128.0
LAST = 144
BF = jnp.bfloat16
F32 = jnp.float32


def params(mb=48):
    return pltpu.CompilerParams(vmem_limit_bytes=mb * 1024 * 1024)


def code_of(i):
    x, core = i >> 1, i & 1
    return core | (((x ^ (x >> 1)) & 1) << 1) | ((x >> 1) << 2)


def index_of(code):
    core, low, high = code & 1, (code >> 1) & 1, (code >> 2) & 1
    x = (high << 1) | (low ^ high)
    return (x << 1) | core


def pre_pairs(rel):
    return [(i, index_of(code_of(i) ^ rel)) for i in range(8)]


def req_pairs(turn_of_core):
    pairs = []
    for i in range(8):
        flip = (1, 4, 3, 12)[turn_of_core[i & 1] % 4]
        pairs += [(i * 16 + j, i * 16 + (j ^ flip)) for j in range(16)]
    return pairs


def half_step(x, half, turn):
    pairs = req_pairs([half + turn, 2 + half + turn])
    return lax.ppermute(x, ("pre", "req"), pairs)


def quarter_step(x, half, side, turn):
    turn = turn if side == 0 else 5 - turn
    return half_step(x, half, turn)


def split3(x):
    hi = x.astype(BF).astype(F32)
    mid = (x - hi).astype(BF).astype(F32)
    low = (x - hi - mid).astype(BF).astype(F32)
    return hi, mid, low


def pack_kernel(code_ref, of_ref, q_ref, rows_ref, *rest):
    out_refs, wide_ref, seen_ref, req_ref = rest[:8], rest[8], rest[9], rest[10]
    count = q_ref.shape[0]
    code = code_ref[0]
    for p in range(16):
        seen_ref[p] = 0
    for slot in range(32):
        req_ref[slot] = -1
    for r in range(count):
        p = of_ref[r]
        rank = seen_ref[p]
        seen_ref[p] = rank + 1
        req_ref[(code_of(p >> 1) ^ code) * 4 + (p & 1) * 2 + rank] = r
    for g in range(GROUP):
        wide_ref[:, pl.ds(g, STEPS, GROUP), :] = q_ref[:, :, g * HD:(g + 1) * HD].astype(F32)
    rows_ref[...] = wide_ref[...].astype(BF)
    nobody = jnp.full((ROWS, HD), EMPTY, BF)
    for rel in range(8):
        for part in range(4):
            r = req_ref[rel * 4 + part]
            rows = rows_ref[jnp.maximum(r, 0)]
            out_refs[rel][0, 0, part * ROWS:(part + 1) * ROWS, :] = jnp.where(r >= 0, rows, nobody)


def pack(code, owners, queries):
    count = queries.shape[0]
    return pl.pallas_call(
        pack_kernel,
        out_shape=[jax.ShapeDtypeStruct((count, ROWS, HD), BF)]
        + [jax.ShapeDtypeStruct((1, 1, 128, HD), BF)] * 8,
        in_specs=[pl.BlockSpec(memory_space=pltpu.SMEM)] * 2
        + [pl.BlockSpec(memory_space=pltpu.VMEM)],
        out_specs=[pl.BlockSpec(memory_space=pltpu.VMEM)] * 9,
        scratch_shapes=[
            pltpu.VMEM((count, ROWS, HD), F32),
            pltpu.SMEM((16,), jnp.int32),
            pltpu.SMEM((32,), jnp.int32),
        ],
        compiler_params=params(),
        name="pack_slots",
    )(code, owners, queries)


def join_kernel(cuts, a_ref, b_ref, *rest):
    half = a_ref.shape[0]
    out_refs = rest[-cuts:]
    width = a_ref.shape[1] // cuts
    for c in range(cuts):
        out_refs[c][:half] = a_ref[:, c * width:(c + 1) * width]
        out_refs[c][half:] = b_ref[:, c * width:(c + 1) * width]


def join(a, b, cuts=1, after=None):
    extra = [] if after is None else [after]
    shape = (2 * a.shape[0], a.shape[1] // cuts) + a.shape[2:]
    return pl.pallas_call(
        functools.partial(join_kernel, cuts),
        out_shape=[jax.ShapeDtypeStruct(shape, BF)] * cuts,
        in_specs=[pl.BlockSpec(memory_space=pltpu.VMEM)] * 2
        + [pl.BlockSpec(memory_space=pl.ANY)] * len(extra),
        out_specs=[pl.BlockSpec(memory_space=pltpu.VMEM)] * cuts,
        compiler_params=params(),
        name="join",
    )(a, b, *extra)


def prefix_kernel(count, first, extra, head_ref, use_ref, *rest):
    q_refs, kv_hbm = rest[:count], rest[count]
    rest = rest[count + 1 + extra:]
    out_refs = rest[:count]
    q_all, kv_all, o_all, sa_ref, sb_ref, bias_ref, lse_ref, most_ref, item_ref, many_ref, sems = (
        rest[count:]
    )
    heads = 2 * count
    positions = kv_all.shape[1]
    blocks = q_all.shape[1]
    rows = blocks * ROWS

    def fetch(m, h):
        at = pl.multiple_of(head_ref[2 * first + h] * (2 * HD), 2 * HD)
        return pltpu.make_async_copy(
            kv_hbm.at[m, :, pl.ds(at, 2 * HD)], kv_all.at[m * heads + h], sems.at[m * heads + h]
        )

    marks = [
        jnp.min(q_refs[0][:, 0, w * ROWS:w * ROWS + 16, :].astype(F32)) < 100.0 for w in range(4)
    ]
    live = [(use_ref[w // 2] > 0) & marks[w] for w in range(4)]

    many_ref[0] = 0
    for m in range(2):
        for rank in range(2):
            on = live[m * 2 + rank]

            @pl.when(on)
            def _():
                n = many_ref[0]
                for h in range(heads):
                    item_ref[n + h] = (m * 2 + rank) * heads + h
                    if rank == 0:
                        fetch(m, h).start()
                many_ref[0] = n + heads

            @pl.when(jnp.logical_not(on))
            def _():
                for side in range(2):
                    at = m * 128 + side * 64 + rank * ROWS
                    o_all[:, :, at:at + ROWS, :] = jnp.zeros((count, blocks, ROWS, HD), BF)

    for m in range(2):
        pos = lax.broadcasted_iota(jnp.int32, (8, positions), 1)
        bias_ref[m] = jnp.where(pos < use_ref[m], 0.0, NEG)
    lse_ref[...] = jnp.full(lse_ref.shape, NEG, F32)
    most_ref[...] = jnp.zeros(most_ref.shape, F32)
    for c in range(count):
        for side in range(2):
            q_all[2 * c + side] = q_refs[c][:, side]
    n = many_ref[0]
    shift = heads.bit_length() - 1

    def decode(i):
        code = item_ref[jnp.minimum(i, n - 1)]
        h, which = code & (heads - 1), code >> shift
        return h, which, which >> 1, which & 1

    def score(i, s_ref, exact):
        h, which, m, rank = decode(i)

        if not exact:

            @pl.when((rank == 0) & (i < n))
            def _():
                fetch(m, h).wait()

        q = q_all[h, :, pl.ds(pl.multiple_of(which * ROWS, ROWS), ROWS), :].reshape(rows, HD)
        k = kv_all[m * heads + h, :, :HD]
        s = lax.dot_general(q, k, (((1,), (1,)), ((), ())), preferred_element_type=F32)
        s = s.reshape(rows // 8, 8, positions) + bias_ref[m][None]
        s_ref[...] = s.reshape(rows, positions)

    def weigh(i, s_ref, exact):
        h, which, m, rank = decode(i)
        c, side = h >> 1, h & 1
        s = s_ref[...]
        top = jnp.max(s if exact else s[:, :HD], axis=1, keepdims=True)
        p = jnp.exp2((s - top) * (ROOT * LOG2E)).astype(BF)
        v = kv_all[m * heads + h, :, HD:]
        v1 = jnp.concatenate([v, jnp.ones((positions, HD), BF)], axis=1)
        r = jnp.dot(p, v1, preferred_element_type=F32)
        den = r[:, HD:]
        most_ref[...] = jnp.maximum(most_ref[...], jnp.max(den.reshape(rows // 8, 8, HD), axis=0))
        o = r[:, :HD] / den
        lse = top * ROOT + jnp.log(den)
        at = pl.multiple_of(m * 128 + side * 64 + rank * ROWS, ROWS)
        o_all[c, :, pl.ds(at, ROWS), :] = o.reshape(blocks, ROWS, HD).astype(BF)
        part = side * 2 + rank
        row_id = lax.broadcasted_iota(jnp.int32, (ROWS, HD), 0)
        lane_id = lax.broadcasted_iota(jnp.int32, (ROWS, HD), 1)
        diag = (lane_id - row_id == part * ROWS)[None]
        flat = jnp.sum(jnp.where(diag, lse.reshape(blocks, ROWS, HD), 0.0), axis=1)
        lanes = lax.broadcasted_iota(jnp.int32, (blocks, HD), 1) >> 5
        old = lse_ref[c * 2 + m]
        lse_ref[c * 2 + m] = jnp.where(lanes == part, flat, old)

    def run(exact):
        score(0, sa_ref, exact)

        def body(j, carry):
            score(2 * j + 1, sb_ref, exact)
            weigh(2 * j, sa_ref, exact)
            score(2 * j + 2, sa_ref, exact)
            weigh(2 * j + 1, sb_ref, exact)
            return carry

        lax.fori_loop(0, (n + 1) // 2, body, 0)

    @pl.when(n > 0)
    def _():
        run(False)

        @pl.when(jnp.max(most_ref[...]) > 1e30)
        def _():
            run(True)

    for c in range(count):
        out_refs[c][:, :256, :] = o_all[c]
        out_refs[c][:, 256:, :] = lse_rows([lse_ref[2 * c + m][:, None, :] for m in range(2)])


def lse_rows(tops):
    shape = (tops[0].shape[0], 16, HD)
    row = lax.broadcasted_iota(jnp.int32, shape, 1)
    out = jnp.zeros(shape, F32)
    at = 0
    for top in tops:
        for piece in split3(top):
            out = jnp.where(row == at, jnp.broadcast_to(piece, shape), out)
            at += 1
    return out.astype(BF)


def prefix_attention(head_of, usable, qs, prefix_kv, first, after=None):
    count = len(qs)
    extra = [] if after is None else [after]
    heads = 2 * count
    blocks = qs[0].shape[0]
    positions = prefix_kv.shape[1]
    rows = blocks * ROWS
    work = rows * positions * heads * 3
    return pl.pallas_call(
        functools.partial(prefix_kernel, count, first, len(extra)),
        out_shape=[jax.ShapeDtypeStruct((blocks, 272, HD), BF)] * count,
        in_specs=[pl.BlockSpec(memory_space=pltpu.SMEM)] * 2
        + [pl.BlockSpec(memory_space=pltpu.VMEM)] * count
        + [pl.BlockSpec(memory_space=pl.ANY)] * (1 + len(extra)),
        out_specs=[pl.BlockSpec(memory_space=pltpu.VMEM)] * count,
        scratch_shapes=[
            pltpu.VMEM((heads, blocks, 128, HD), BF),
            pltpu.VMEM((2 * heads, positions, 2 * HD), BF),
            pltpu.VMEM((count, blocks, 256, HD), BF),
            pltpu.VMEM((rows, positions), F32),
            pltpu.VMEM((rows, positions), F32),
            pltpu.VMEM((2, 8, positions), F32),
            pltpu.VMEM((heads, blocks, HD), F32),
            pltpu.VMEM((8, HD), F32),
            pltpu.SMEM((4 * heads,), jnp.int32),
            pltpu.SMEM((1,), jnp.int32),
            pltpu.SemaphoreType.DMA((2 * heads,)),
        ],
        compiler_params=params(),
        cost_estimate=pl.CostEstimate(
            flops=work * 512, bytes_accessed=heads << 20, transcendentals=work
        ),
        name="prefix_attention",
    )(head_of, usable, *qs, prefix_kv, *extra)


def blend_weights(la, lb):
    top = jnp.maximum(la, lb)
    ea, eb = jnp.exp(la - top), jnp.exp(lb - top)
    total = ea + eb
    return ea / total, top + jnp.log(total)


def spread(w):
    return jnp.broadcast_to(w, (HD, HD)).T


def read_lse(rows, m):
    return rows[3 * m:3 * m + 1] + rows[3 * m + 1:3 * m + 2] + rows[3 * m + 2:3 * m + 3]


def merge_line(a_ref, b_ref, idx):
    tiles = a_ref.shape[1] // 128
    ra = a_ref[idx, tiles * 128:, :].astype(F32)
    rb = b_ref[idx, tiles * 128:, :].astype(F32)
    datas, tops = [], []
    for m in range(tiles):
        wa, lse = blend_weights(read_lse(ra, m), read_lse(rb, m))
        oa = a_ref[idx, m * 128:(m + 1) * 128, :].astype(F32)
        ob = b_ref[idx, m * 128:(m + 1) * 128, :].astype(F32)
        datas.append(ob + spread(wa) * (oa - ob))
        tops.append(lse)
    return datas, tops


def merge_kernel(extra, *refs):
    pairs, (keep_ref, send_ref) = refs[:-2 - extra], refs[-2:]
    half = keep_ref.shape[0]
    for out_ref, first in ((send_ref, half), (keep_ref, 0)):
        for b in range(half):
            merged = [
                merge_line(pairs[2 * c], pairs[2 * c + 1], first + b) for c in range(len(pairs) // 2)
            ]
            datas = [d for row in zip(*[x[0] for x in merged]) for d in row]
            tops = [t for row in zip(*[x[1] for x in merged]) for t in row]
            tiles = len(datas)
            for m in range(tiles):
                out_ref[b, m * 128:(m + 1) * 128, :] = datas[m].astype(BF)
            out_ref[b, tiles * 128:, :] = lse_rows([t[None] for t in tops])[0]


def merge(*pairs, after=None):
    extra = [] if after is None else [after]
    blocks, line = pairs[0].shape[:2]
    tiles = (line // 128) * (len(pairs) // 2)
    one = jax.ShapeDtypeStruct((blocks // 2, tiles * 128 + 16, HD), BF)
    return pl.pallas_call(
        functools.partial(merge_kernel, len(extra)),
        out_shape=[one, one],
        in_specs=[pl.BlockSpec(memory_space=pltpu.VMEM)] * len(pairs)
        + [pl.BlockSpec(memory_space=pl.ANY)] * len(extra),
        out_specs=[pl.BlockSpec(memory_space=pltpu.VMEM)] * 2,
        compiler_params=params(),
        cost_estimate=pl.CostEstimate(
            flops=blocks * tiles * 128 * 128 * 6,
            bytes_accessed=blocks * tiles * 128 * HD * 6,
            transcendentals=0,
        ),
        name="merge_step",
    )(*pairs, *extra)


def last_kernel(a_ref, b_ref, *out_refs):
    datas, tops = merge_line(a_ref, b_ref, 0)
    low = lax.broadcasted_iota(jnp.int32, (1, HD), 1) < 64
    rolled = [pltpu.roll(jnp.broadcast_to(t, (8, HD)), 64, 1)[0:1] for t in tops]
    for h in range(4):
        pair, side = h // 2, h % 2
        if side == 0:
            joined = jnp.where(low, tops[pair], rolled[2 + pair])
        else:
            joined = jnp.where(low, rolled[pair], tops[2 + pair])
        for m in range(2):
            rows = datas[2 * m + pair][side * 64:(side + 1) * 64]
            out_refs[h][m * 64:(m + 1) * 64, :] = rows.astype(BF)
        out_refs[h][128:LAST, :] = lse_rows([joined[None]])[0]


def merge_last(mine, received):
    one = jax.ShapeDtypeStruct((LAST, HD), BF)
    return pl.pallas_call(
        last_kernel,
        out_shape=[one] * 4,
        in_specs=[pl.BlockSpec(memory_space=pltpu.VMEM)] * 2,
        out_specs=[pl.BlockSpec(memory_space=pltpu.VMEM)] * 4,
        compiler_params=params(),
        name="merge_last",
    )(mine, received)


def suffix_kernel(first, len_ref, q_ref, kv_ref, new_ref, o_ref, lse_ref):
    per = q_ref.shape[0]
    positions = kv_ref.shape[1]
    step_id = lax.broadcasted_iota(jnp.int32, (ROWS, 1), 0) // GROUP
    pos = lax.broadcasted_iota(jnp.int32, (ROWS, positions), 1)
    ones = jnp.ones((positions, HD), BF)
    for e in range(per):
        used = len_ref[first + pl.program_id(0) * per + e]
        q = q_ref[e]
        qf = q.astype(F32)
        fresh = new_ref[e].astype(F32)
        s = lax.dot_general(
            q, kv_ref[e, :, :HD], (((1,), (1,)), ((), ())), preferred_element_type=F32
        )
        s = jnp.where(pos < used, s, NEG)
        top = jnp.max(s, axis=1, keepdims=True)
        extra = []
        for t in range(STEPS):
            f = jnp.sum(qf * fresh[t:t + 1, :HD], axis=1, keepdims=True)
            f = jnp.where(step_id >= t, f, NEG)
            extra.append(f)
            top = jnp.maximum(top, f)
        p = jnp.exp2((s - top) * (ROOT * LOG2E)).astype(BF)
        r = jnp.dot(
            p, jnp.concatenate([kv_ref[e, :, HD:], ones], axis=1), preferred_element_type=F32
        )
        num, den = r[:, :HD], r[:, HD:]
        for t in range(STEPS):
            w = jnp.exp2((extra[t] - top) * (ROOT * LOG2E))
            num = num + w * fresh[t:t + 1, HD:]
            den = den + w
        o_ref[e] = num / den
        lse_ref[e] = top * ROOT + jnp.log(den)


def suffix_attention(suffix_len, q_rows, suffix_kv, new_kv, first, count):
    positions = suffix_kv.shape[1]
    per = 4
    skip = first // per
    one = jax.ShapeDtypeStruct((count, ROWS, HD), F32)
    grid_spec = pltpu.PrefetchScalarGridSpec(
        num_scalar_prefetch=1,
        grid=(count // per,),
        in_specs=[
            pl.BlockSpec((per, ROWS, HD), lambda s, n: (s + skip, 0, 0)),
            pl.BlockSpec((per, positions, 2 * HD), lambda s, n: (s + skip, 0, 0)),
            pl.BlockSpec((per, STEPS, 2 * HD), lambda s, n: (s + skip, 0, 0)),
        ],
        out_specs=[pl.BlockSpec((per, ROWS, HD), lambda s, n: (s, 0, 0))] * 2,
    )
    return pl.pallas_call(
        functools.partial(suffix_kernel, first),
        out_shape=[one, one],
        grid_spec=grid_spec,
        compiler_params=params(),
        cost_estimate=pl.CostEstimate(
            flops=count * 256 * positions * 128 * 4,
            bytes_accessed=count << 19,
            transcendentals=count * ROWS * positions,
        ),
        name="suffix_attention",
    )(suffix_len, q_rows, suffix_kv, new_kv)


def final_kernel(rel_ref, off_ref, oa_ref, la_ref, ob_ref, lb_ref, *rest):
    parts, out_ref, data_ref, top_ref, wide_ref = rest[:8], rest[8], rest[9], rest[10], rest[11]
    for t in range(8):
        data_ref[t] = parts[t][0:128, :].astype(F32)
        rows = parts[t][128:LAST, :].astype(F32)
        top_ref[t] = spread(read_lse(rows, 0))
    each = oa_ref.shape[0]
    for r in range(2 * each):
        o_ref, l_ref = (oa_ref, la_ref) if r < each else (ob_ref, lb_ref)
        at = pl.ds(pl.multiple_of(off_ref[r], ROWS), ROWS)
        op, lp = data_ref[rel_ref[r], at, :], top_ref[rel_ref[r], at, :]
        w, _ = blend_weights(lp, l_ref[r % each])
        ol = o_ref[r % each]
        wide_ref[r] = ol + w * (op - ol)
    for g in range(GROUP):
        out_ref[:, :, g * HD:(g + 1) * HD] = wide_ref[:, pl.ds(g, STEPS, GROUP), :].astype(BF)


def finish(rel, off, local, parts):
    count = rel.shape[0]
    return pl.pallas_call(
        final_kernel,
        out_shape=jax.ShapeDtypeStruct((count, STEPS, GROUP * HD), BF),
        in_specs=[pl.BlockSpec(memory_space=pltpu.SMEM)] * 2
        + [pl.BlockSpec(memory_space=pltpu.VMEM)] * 12,
        out_specs=pl.BlockSpec(memory_space=pltpu.VMEM),
        scratch_shapes=[
            pltpu.VMEM((8, HD, HD), F32),
            pltpu.VMEM((8, HD, HD), F32),
            pltpu.VMEM((count, ROWS, HD), F32),
        ],
        compiler_params=params(),
        name="finish",
    )(rel, off, *local, *parts)


def on_device(prefix_kv, prefix_len, prefix_of, suffix_len, suffix_kv, queries, new_kv):
    mine, block = lax.axis_index("pre"), lax.axis_index("req")
    code = code_of(mine)
    shard = prefix_kv.shape[1]
    count = queries.shape[0]

    owners = prefix_of[:, 0]
    ids = jnp.arange(count, dtype=jnp.int32)
    earlier = (owners[None, :] == owners[:, None]) & (ids[None, :] < ids[:, None])
    rank = jnp.sum(earlier.astype(jnp.int32), axis=1)
    rel = code_of(owners >> 1) ^ code
    part = (owners & 1) * 2 + rank
    head_of = index_of(code ^ jnp.arange(8, dtype=jnp.int32))
    own_len = lax.dynamic_slice_in_dim(prefix_len, mine * 2, 2, 0)
    usable = jnp.clip(own_len - block * shard, 0, shard)

    q_rows, *packed = pack(jnp.reshape(code, (1,)), owners, queries)
    heads = [packed[0]] + [lax.ppermute(packed[t], "pre", pre_pairs(t)) for t in range(1, 8)]
    local = []
    for first in (0, count // 2):
        local += suffix_attention(suffix_len, q_rows, suffix_kv, new_kv, first, count // 2)

    both = [(a, side) for a in range(2) for side in range(2)]
    have = [jnp.concatenate(heads[4 * a:4 * a + 4], axis=1) for a in range(2)]
    got = [half_step(have[a], a, 0) for a in range(2)]
    have = [join(have[a], got[a])[0] for a in range(2)]
    got = [half_step(have[a], a, 1) for a in range(2)]
    near = [x for a in range(2) for x in join(have[a], got[a], 2, local[0])]
    got = [quarter_step(near[k], *both[k], 2) for k in range(4)]
    near = [join(near[k], got[k])[0] for k in range(4)]
    far = [quarter_step(near[k], *both[k], 3) for k in range(4)]
    keep = prefix_attention(head_of, usable, near[:2], prefix_kv, 0)
    send = prefix_attention(head_of, usable, far[:2], prefix_kv, 0, keep[0])
    send += prefix_attention(head_of, usable, far[2:], prefix_kv, 2)
    keep += prefix_attention(head_of, usable, near[2:], prefix_kv, 2)
    got = [quarter_step(send[k], *both[k], 3) for k in range(4)]
    parts = [merge(keep[k], got[k]) for k in range(4)]
    keep, send = [p[0] for p in parts], [p[1] for p in parts]
    got = [quarter_step(send[k], *both[k], 2) for k in range(4)]
    parts = [merge(keep[2 * a], got[2 * a], keep[2 * a + 1], got[2 * a + 1]) for a in range(2)]
    keep, send = [p[0] for p in parts], [p[1] for p in parts]
    got = [half_step(send[a], a, 1) for a in range(2)]
    parts = [merge(keep[a], got[a], after=local[2]) for a in range(2)]
    keep, send = [p[0] for p in parts], [p[1] for p in parts]
    got = [half_step(send[a], a, 0) for a in range(2)]
    tiles = []
    for a in range(2):
        tiles += merge_last(keep[a], got[a])
    back = [tiles[0]] + [lax.ppermute(tiles[t], "pre", pre_pairs(t)) for t in range(1, 8)]
    return finish(rel, part * ROWS, local, back)


def solution(mesh):
    placed = (
        P("pre", "req", None),
        P(),
        P("req", None),
        P("req"),
        P("req", None, "pre"),
        P("req", None, "pre"),
        P("req", None, "pre"),
    )
    return jax.shard_map(
        on_device, mesh=mesh, in_specs=placed, out_specs=P("req", None, "pre"), check_vma=False
    )
```

```python
import functools
import math

import jax
import jax.numpy as jnp
from jax import lax
from jax.experimental import pallas as pl
from jax.experimental.pallas import tpu as pltpu
from jax.sharding import PartitionSpec as P

HD = 128
GROUP = 8
STEPS = 4
ROWS = STEPS * GROUP
NEG = -1e30
ROOT = 1.0 / math.sqrt(HD)
LOG2E = math.log2(math.e)
EMPTY = 128.0
LAST = 144
BF = jnp.bfloat16
F32 = jnp.float32


def params(mb=48):
    return pltpu.CompilerParams(vmem_limit_bytes=mb * 1024 * 1024)


FLIPS = (1, 4, 3, 12)


def req_step(x, turns):
    pairs = []
    for i in range(8):
        flip = 0
        for turn in turns:
            flip ^= FLIPS[(2 * (i & 1) + turn) % 4]
        pairs += [(i * 16 + j, i * 16 + (j ^ flip)) for j in range(16)]
    return lax.ppermute(x, ("pre", "req"), pairs)


def quarter_step(x, half, side, turn):
    turn = turn if side == 0 else 5 - turn
    return req_step(x, [half + turn])


def three_ways(xs, half):
    ways = ([half], [half + 1], [half, half + 1])
    return [req_step(x, way) for x, way in zip(xs, ways)]


def split3(x):
    hi = x.astype(BF).astype(F32)
    mid = (x - hi).astype(BF).astype(F32)
    low = (x - hi - mid).astype(BF).astype(F32)
    return hi, mid, low


def pack_kernel(of_ref, q_ref, rows_ref, out_ref, wide_ref, seen_ref, req_ref):
    count = q_ref.shape[0]
    for p in range(16):
        seen_ref[p] = 0
    for slot in range(32):
        req_ref[slot] = -1
    for r in range(count):
        p = of_ref[r]
        rank = seen_ref[p]
        seen_ref[p] = rank + 1
        req_ref[p * 2 + rank] = r
    for g in range(GROUP):
        wide_ref[:, pl.ds(g, STEPS, GROUP), :] = q_ref[:, :, g * HD:(g + 1) * HD].astype(F32)
    rows_ref[...] = wide_ref[...].astype(BF)
    nobody = jnp.full((ROWS, HD), EMPTY, BF)
    for slot in range(32):
        r = req_ref[slot]
        rows = rows_ref[jnp.maximum(r, 0)]
        at = (slot % 4) * ROWS
        out_ref[slot // 4, at:at + ROWS, :] = jnp.where(r >= 0, rows, nobody)


def pack(owners, queries):
    count = queries.shape[0]
    return pl.pallas_call(
        pack_kernel,
        out_shape=[
            jax.ShapeDtypeStruct((count, ROWS, HD), BF),
            jax.ShapeDtypeStruct((8, 128, HD), BF),
        ],
        in_specs=[pl.BlockSpec(memory_space=pltpu.SMEM), pl.BlockSpec(memory_space=pltpu.VMEM)],
        out_specs=[pl.BlockSpec(memory_space=pltpu.VMEM)] * 2,
        scratch_shapes=[
            pltpu.VMEM((count, ROWS, HD), F32),
            pltpu.SMEM((16,), jnp.int32),
            pltpu.SMEM((32,), jnp.int32),
        ],
        compiler_params=params(),
        name="pack_slots",
    )(owners, queries)


def join_kernel(groups, cuts, total, *refs):
    out_refs = refs[-groups * cuts:]
    ins = refs[:total]
    count = total // groups
    each = ins[0].shape[0]
    width = ins[0].shape[1] // cuts
    for g in range(groups):
        for c in range(cuts):
            for n in range(count):
                piece = ins[g * count + n][:, c * width:(c + 1) * width]
                out_refs[g * cuts + c][n * each:(n + 1) * each] = piece


def join(parts, groups=1, cuts=1, after=None):
    extra = [] if after is None else [after]
    first = parts[0].shape
    shape = (len(parts) // groups * first[0], first[1] // cuts) + first[2:]
    return pl.pallas_call(
        functools.partial(join_kernel, groups, cuts, len(parts)),
        out_shape=[jax.ShapeDtypeStruct(shape, BF)] * (groups * cuts),
        in_specs=[pl.BlockSpec(memory_space=pltpu.VMEM)] * len(parts)
        + [pl.BlockSpec(memory_space=pl.ANY)] * len(extra),
        out_specs=[pl.BlockSpec(memory_space=pltpu.VMEM)] * (groups * cuts),
        compiler_params=params(),
        name="join",
    )(*parts, *extra)


def prefix_kernel(count, first, extra, use_ref, *rest):
    q_refs, kv_hbm = rest[:count], rest[count]
    rest = rest[count + 1 + extra:]
    out_refs = rest[:count]
    q_all, kv_all, o_all, sa_ref, sb_ref, bias_ref, lse_ref, item_ref, many_ref, sems = rest[
        count:
    ]
    heads = 2 * count
    positions = kv_all.shape[1]
    blocks = q_all.shape[1]
    rows = blocks * ROWS

    def fetch(m, h):
        at = pl.multiple_of((2 * first + h) * (2 * HD), 2 * HD)
        return pltpu.make_async_copy(
            kv_hbm.at[m, :, pl.ds(at, 2 * HD)], kv_all.at[m * heads + h], sems.at[m * heads + h]
        )

    marks = [
        jnp.min(q_refs[0][:, 0, w * ROWS:w * ROWS + 16, :].astype(F32)) < 100.0 for w in range(4)
    ]
    live = [(use_ref[w // 2] > 0) & marks[w] for w in range(4)]

    many_ref[0] = 0
    for m in range(2):
        for rank in range(2):
            on = live[m * 2 + rank]

            @pl.when(on)
            def _():
                n = many_ref[0]
                for h in range(heads):
                    item_ref[n + h] = (m * 2 + rank) * heads + h
                    if rank == 0:
                        fetch(m, h).start()
                many_ref[0] = n + heads

            @pl.when(jnp.logical_not(on))
            def _():
                for side in range(2):
                    at = m * 128 + side * 64 + rank * ROWS
                    o_all[:, :, at:at + ROWS, :] = jnp.zeros((count, blocks, ROWS, HD), BF)

    for m in range(2):
        pos = lax.broadcasted_iota(jnp.int32, (8, positions), 1)
        bias_ref[m] = jnp.where(pos < use_ref[m], 0.0, NEG)
    lse_ref[...] = jnp.full(lse_ref.shape, NEG, F32)
    for c in range(count):
        for side in range(2):
            q_all[2 * c + side] = q_refs[c][:, side]
    n = many_ref[0]
    shift = heads.bit_length() - 1

    def decode(i):
        code = item_ref[jnp.minimum(i, n - 1)]
        h, which = code & (heads - 1), code >> shift
        return h, which, which >> 1, which & 1

    def score(i, s_ref):
        h, which, m, rank = decode(i)

        @pl.when((rank == 0) & (i < n))
        def _():
            fetch(m, h).wait()

        q = q_all[h, :, pl.ds(pl.multiple_of(which * ROWS, ROWS), ROWS), :].reshape(rows, HD)
        k = kv_all[m * heads + h, :, :HD]
        s = lax.dot_general(q, k, (((1,), (1,)), ((), ())), preferred_element_type=F32)
        s = s.reshape(rows // 8, 8, positions) + bias_ref[m][None]
        s_ref[...] = s.reshape(rows, positions)

    def weigh(i, s_ref):
        h, which, m, rank = decode(i)
        c, side = h >> 1, h & 1
        s = s_ref[...]
        top = jnp.max(s, axis=1, keepdims=True)
        p = jnp.exp2((s - top) * (ROOT * LOG2E)).astype(BF)
        v = kv_all[m * heads + h, :, HD:]
        v1 = jnp.concatenate([v, jnp.ones((positions, HD), BF)], axis=1)
        r = jnp.dot(p, v1, preferred_element_type=F32)
        den = r[:, HD:]
        o = r[:, :HD] / den
        lse = top * ROOT + jnp.log(den)
        at = pl.multiple_of(m * 128 + side * 64 + rank * ROWS, ROWS)
        o_all[c, :, pl.ds(at, ROWS), :] = o.reshape(blocks, ROWS, HD).astype(BF)
        part = side * 2 + rank
        row_id = lax.broadcasted_iota(jnp.int32, (ROWS, HD), 0)
        lane_id = lax.broadcasted_iota(jnp.int32, (ROWS, HD), 1)
        diag = (lane_id - row_id == part * ROWS)[None]
        flat = jnp.sum(jnp.where(diag, lse.reshape(blocks, ROWS, HD), 0.0), axis=1)
        lanes = lax.broadcasted_iota(jnp.int32, (blocks, HD), 1) >> 5
        old = lse_ref[c * 2 + m]
        lse_ref[c * 2 + m] = jnp.where(lanes == part, flat, old)

    @pl.when(n > 0)
    def _():
        score(0, sa_ref)

        def body(j, carry):
            score(2 * j + 1, sb_ref)
            weigh(2 * j, sa_ref)
            score(2 * j + 2, sa_ref)
            weigh(2 * j + 1, sb_ref)
            return carry

        lax.fori_loop(0, (n + 1) // 2, body, 0)

    for c in range(count):
        out_refs[c][:, :256, :] = o_all[c]
        out_refs[c][:, 256:, :] = lse_rows([lse_ref[2 * c + m][:, None, :] for m in range(2)])


def lse_rows(tops):
    shape = (tops[0].shape[0], 16, HD)
    row = lax.broadcasted_iota(jnp.int32, shape, 1)
    out = jnp.zeros(shape, F32)
    at = 0
    for top in tops:
        for piece in split3(top):
            out = jnp.where(row == at, jnp.broadcast_to(piece, shape), out)
            at += 1
    return out.astype(BF)


def prefix_attention(usable, qs, prefix_kv, first, after=None):
    count = len(qs)
    extra = [] if after is None else [after]
    heads = 2 * count
    blocks = qs[0].shape[0]
    positions = prefix_kv.shape[1]
    rows = blocks * ROWS
    work = rows * positions * heads * 3
    return pl.pallas_call(
        functools.partial(prefix_kernel, count, first, len(extra)),
        out_shape=[jax.ShapeDtypeStruct((blocks, 272, HD), BF)] * count,
        in_specs=[pl.BlockSpec(memory_space=pltpu.SMEM)]
        + [pl.BlockSpec(memory_space=pltpu.VMEM)] * count
        + [pl.BlockSpec(memory_space=pl.ANY)] * (1 + len(extra)),
        out_specs=[pl.BlockSpec(memory_space=pltpu.VMEM)] * count,
        scratch_shapes=[
            pltpu.VMEM((heads, blocks, 128, HD), BF),
            pltpu.VMEM((2 * heads, positions, 2 * HD), BF),
            pltpu.VMEM((count, blocks, 256, HD), BF),
            pltpu.VMEM((rows, positions), F32),
            pltpu.VMEM((rows, positions), F32),
            pltpu.VMEM((2, 8, positions), F32),
            pltpu.VMEM((heads, blocks, HD), F32),
            pltpu.SMEM((4 * heads,), jnp.int32),
            pltpu.SMEM((1,), jnp.int32),
            pltpu.SemaphoreType.DMA((2 * heads,)),
        ],
        compiler_params=params(),
        cost_estimate=pl.CostEstimate(
            flops=work * 512, bytes_accessed=heads << 20, transcendentals=work
        ),
        name="prefix_attention",
    )(usable, *qs, prefix_kv, *extra)


def blend_weights(la, lb):
    top = jnp.maximum(la, lb)
    ea, eb = jnp.exp(la - top), jnp.exp(lb - top)
    total = ea + eb
    return ea / total, top + jnp.log(total)


def spread(w):
    return jnp.broadcast_to(w, (HD, HD)).T


def read_lse(rows, m):
    return rows[3 * m:3 * m + 1] + rows[3 * m + 1:3 * m + 2] + rows[3 * m + 2:3 * m + 3]


def merge_line(a_ref, b_ref, idx):
    tiles = a_ref.shape[1] // 128
    ra = a_ref[idx, tiles * 128:, :].astype(F32)
    rb = b_ref[idx, tiles * 128:, :].astype(F32)
    datas, tops = [], []
    for m in range(tiles):
        wa, lse = blend_weights(read_lse(ra, m), read_lse(rb, m))
        oa = a_ref[idx, m * 128:(m + 1) * 128, :].astype(F32)
        ob = b_ref[idx, m * 128:(m + 1) * 128, :].astype(F32)
        datas.append(ob + spread(wa) * (oa - ob))
        tops.append(lse)
    return datas, tops


def merge_kernel(pairs, extra, *refs):
    ins, out_refs = refs[:2 * pairs], refs[2 * pairs + extra:]
    outs = [(ref, b) for ref in out_refs for b in range(ref.shape[0])]
    for spot, (out_ref, b) in reversed(list(enumerate(outs))):
        merged = [merge_line(ins[2 * c], ins[2 * c + 1], spot) for c in range(pairs)]
        datas = [d for row in zip(*[x[0] for x in merged]) for d in row]
        tops = [t for row in zip(*[x[1] for x in merged]) for t in row]
        tiles = len(datas)
        for m in range(tiles):
            out_ref[b, m * 128:(m + 1) * 128, :] = datas[m].astype(BF)
        out_ref[b, tiles * 128:, :] = lse_rows([t[None] for t in tops])[0]


def merge(ins, counts, after=None):
    extra = [] if after is None else [after]
    blocks, line = ins[0].shape[:2]
    pairs = len(ins) // 2
    tiles = (line // 128) * pairs
    return pl.pallas_call(
        functools.partial(merge_kernel, pairs, len(extra)),
        out_shape=[jax.ShapeDtypeStruct((n, tiles * 128 + 16, HD), BF) for n in counts],
        in_specs=[pl.BlockSpec(memory_space=pltpu.VMEM)] * len(ins)
        + [pl.BlockSpec(memory_space=pl.ANY)] * len(extra),
        out_specs=[pl.BlockSpec(memory_space=pltpu.VMEM)] * len(counts),
        compiler_params=params(),
        cost_estimate=pl.CostEstimate(
            flops=blocks * tiles * 128 * 128 * 6,
            bytes_accessed=blocks * tiles * 128 * HD * 6,
            transcendentals=0,
        ),
        name="merge_step",
    )(*ins, *extra)


def last_kernel(*refs):
    ins, out_ref = refs[:8], refs[8]
    low = lax.broadcasted_iota(jnp.int32, (1, HD), 1) < 64
    for a in range(2):
        parts = ins[4 * a:4 * a + 4]
        rows = [p[0, 512:, :].astype(F32) for p in parts]
        datas, tops = [], []
        for t in range(4):
            each = [read_lse(r, t) for r in rows]
            top = functools.reduce(jnp.maximum, each)
            es = [jnp.exp(x - top) for x in each]
            total = es[0] + es[1] + es[2] + es[3]
            data = 0.0
            for p, e in zip(parts, es):
                data = data + spread(e / total) * p[0, t * 128:(t + 1) * 128, :].astype(F32)
            datas.append(data)
            tops.append(top + jnp.log(total))
        rolled = [pltpu.roll(jnp.broadcast_to(t, (8, HD)), 64, 1)[0:1] for t in tops]
        for h in range(4):
            pair, side = h // 2, h % 2
            if side == 0:
                joined = jnp.where(low, tops[pair], rolled[2 + pair])
            else:
                joined = jnp.where(low, rolled[pair], tops[2 + pair])
            for m in range(2):
                piece = datas[2 * m + pair][side * 64:(side + 1) * 64]
                out_ref[4 * a + h, m * 64:(m + 1) * 64, :] = piece.astype(BF)
            out_ref[4 * a + h, 128:LAST, :] = lse_rows([joined[None]])[0]


def merge_last(parts):
    return pl.pallas_call(
        last_kernel,
        out_shape=jax.ShapeDtypeStruct((8, LAST, HD), BF),
        in_specs=[pl.BlockSpec(memory_space=pltpu.VMEM)] * 8,
        out_specs=pl.BlockSpec(memory_space=pltpu.VMEM),
        compiler_params=params(),
        name="merge_last",
    )(*parts)


def suffix_kernel(first, len_ref, q_ref, kv_ref, new_ref, o_ref, lse_ref):
    per = q_ref.shape[0]
    positions = kv_ref.shape[1]
    step_id = lax.broadcasted_iota(jnp.int32, (ROWS, 1), 0) // GROUP
    pos = lax.broadcasted_iota(jnp.int32, (ROWS, positions), 1)
    ones = jnp.ones((positions, HD), BF)
    for e in range(per):
        used = len_ref[first + pl.program_id(0) * per + e]
        q = q_ref[e]
        qf = q.astype(F32)
        fresh = new_ref[e].astype(F32)
        s = lax.dot_general(
            q, kv_ref[e, :, :HD], (((1,), (1,)), ((), ())), preferred_element_type=F32
        )
        s = jnp.where(pos < used, s, NEG)
        top = jnp.max(s, axis=1, keepdims=True)
        extra = []
        for t in range(STEPS):
            f = jnp.sum(qf * fresh[t:t + 1, :HD], axis=1, keepdims=True)
            f = jnp.where(step_id >= t, f, NEG)
            extra.append(f)
            top = jnp.maximum(top, f)
        p = jnp.exp2((s - top) * (ROOT * LOG2E)).astype(BF)
        r = jnp.dot(
            p, jnp.concatenate([kv_ref[e, :, HD:], ones], axis=1), preferred_element_type=F32
        )
        num, den = r[:, :HD], r[:, HD:]
        for t in range(STEPS):
            w = jnp.exp2((extra[t] - top) * (ROOT * LOG2E))
            num = num + w * fresh[t:t + 1, HD:]
            den = den + w
        o_ref[e] = num / den
        lse_ref[e] = top * ROOT + jnp.log(den)


def suffix_attention(suffix_len, q_rows, suffix_kv, new_kv, first, count):
    positions = suffix_kv.shape[1]
    per = 4
    skip = first // per
    one = jax.ShapeDtypeStruct((count, ROWS, HD), F32)
    grid_spec = pltpu.PrefetchScalarGridSpec(
        num_scalar_prefetch=1,
        grid=(count // per,),
        in_specs=[
            pl.BlockSpec((per, ROWS, HD), lambda s, n: (s + skip, 0, 0)),
            pl.BlockSpec((per, positions, 2 * HD), lambda s, n: (s + skip, 0, 0)),
            pl.BlockSpec((per, STEPS, 2 * HD), lambda s, n: (s + skip, 0, 0)),
        ],
        out_specs=[pl.BlockSpec((per, ROWS, HD), lambda s, n: (s, 0, 0))] * 2,
    )
    return pl.pallas_call(
        functools.partial(suffix_kernel, first),
        out_shape=[one, one],
        grid_spec=grid_spec,
        compiler_params=params(),
        cost_estimate=pl.CostEstimate(
            flops=count * 256 * positions * 128 * 4,
            bytes_accessed=count << 19,
            transcendentals=count * ROWS * positions,
        ),
        name="suffix_attention",
    )(suffix_len, q_rows, suffix_kv, new_kv)


def final_kernel(
    own_ref, off_ref, oa_ref, la_ref, ob_ref, lb_ref, part_ref, out_ref, data_ref, top_ref, wide_ref
):
    for t in range(8):
        data_ref[t] = part_ref[t, 0:128, :].astype(F32)
        rows = part_ref[t, 128:LAST, :].astype(F32)
        top_ref[t] = spread(read_lse(rows, 0))
    each = oa_ref.shape[0]
    for r in range(2 * each):
        o_ref, l_ref = (oa_ref, la_ref) if r < each else (ob_ref, lb_ref)
        at = pl.ds(pl.multiple_of(off_ref[r], ROWS), ROWS)
        op, lp = data_ref[own_ref[r], at, :], top_ref[own_ref[r], at, :]
        w, _ = blend_weights(lp, l_ref[r % each])
        ol = o_ref[r % each]
        wide_ref[r] = ol + w * (op - ol)
    for g in range(GROUP):
        out_ref[:, :, g * HD:(g + 1) * HD] = wide_ref[:, pl.ds(g, STEPS, GROUP), :].astype(BF)


def finish(own, off, local, parts):
    count = own.shape[0]
    return pl.pallas_call(
        final_kernel,
        out_shape=jax.ShapeDtypeStruct((count, STEPS, GROUP * HD), BF),
        in_specs=[pl.BlockSpec(memory_space=pltpu.SMEM)] * 2
        + [pl.BlockSpec(memory_space=pltpu.VMEM)] * 5,
        out_specs=pl.BlockSpec(memory_space=pltpu.VMEM),
        scratch_shapes=[
            pltpu.VMEM((8, HD, HD), F32),
            pltpu.VMEM((8, HD, HD), F32),
            pltpu.VMEM((count, ROWS, HD), F32),
        ],
        compiler_params=params(),
        name="finish",
    )(own, off, *local, parts)


def on_device(prefix_kv, prefix_len, prefix_of, suffix_len, suffix_kv, queries, new_kv):
    mine, block = lax.axis_index("pre"), lax.axis_index("req")
    shard = prefix_kv.shape[1]
    count = queries.shape[0]

    owners = prefix_of[:, 0]
    ids = jnp.arange(count, dtype=jnp.int32)
    earlier = (owners[None, :] == owners[:, None]) & (ids[None, :] < ids[:, None])
    rank = jnp.sum(earlier.astype(jnp.int32), axis=1)
    part = (owners & 1) * 2 + rank
    own_len = lax.dynamic_slice_in_dim(prefix_len, mine * 2, 2, 0)
    usable = jnp.clip(own_len - block * shard, 0, shard)

    q_rows, packed = pack(owners, queries)
    heads = lax.all_to_all(packed, "pre", 0, 0, tiled=True)
    local = []
    for first in (0, count // 2):
        local += suffix_attention(suffix_len, q_rows, suffix_kv, new_kv, first, count // 2)

    both = [(a, side) for a in range(2) for side in range(2)]
    have = [heads[None, 4 * a:4 * a + 4] for a in range(2)]
    got = [three_ways([have[a]] * 3, a) for a in range(2)]
    near = join([have[0]] + got[0] + [have[1]] + got[1], 2, 2)
    got = [quarter_step(near[k], *both[k], 2) for k in range(4)]
    near = [
        join([near[k], got[k]], after=local[0] if k == 3 else None)[0] for k in range(4)
    ]
    far = [quarter_step(near[k], *both[k], 3) for k in range(4)]
    keep = prefix_attention(usable, near[:2], prefix_kv, 0)
    send = prefix_attention(usable, far[:2], prefix_kv, 0, keep[0])
    send += prefix_attention(usable, far[2:], prefix_kv, 2)
    keep += prefix_attention(usable, near[2:], prefix_kv, 2)
    got = [quarter_step(send[k], *both[k], 3) for k in range(4)]
    parts = [merge([keep[k], got[k]], [4, 4]) for k in range(4)]
    keep, send = [p[0] for p in parts], [p[1] for p in parts]
    got = [quarter_step(send[k], *both[k], 2) for k in range(4)]
    final = []
    for a in range(2):
        ins = [keep[2 * a], got[2 * a], keep[2 * a + 1], got[2 * a + 1]]
        parts = merge(ins, [1] * 4, local[2] if a else None)
        final += [parts[0]] + three_ways(parts[1:], a)
    back = lax.all_to_all(merge_last(final), "pre", 0, 0, tiled=True)
    return finish(owners >> 1, part * ROWS, local, back)


def solution(mesh):
    placed = (
        P("pre", "req", None),
        P(),
        P("req", None),
        P("req"),
        P("req", None, "pre"),
        P("req", None, "pre"),
        P("req", None, "pre"),
    )
    return jax.shard_map(
        on_device, mesh=mesh, in_specs=placed, out_specs=P("req", None, "pre"), check_vma=False
    )
```

```python
import functools
import math

import jax
import jax.numpy as jnp
from jax import lax
from jax.experimental import pallas as pl
from jax.experimental.pallas import tpu as pltpu
from jax.sharding import PartitionSpec as P

HD = 128
GROUP = 8
STEPS = 4
ROWS = STEPS * GROUP
NEG = -1e30
ROOT = 1.0 / math.sqrt(HD)
LOG2E = math.log2(math.e)
EMPTY = 128.0
LAST = 144
BF = jnp.bfloat16
F32 = jnp.float32


def params(mb=48):
    return pltpu.CompilerParams(vmem_limit_bytes=mb * 1024 * 1024)


FLIPS = (1, 4, 3, 12)


def req_step(x, turns):
    pairs = []
    for i in range(8):
        flip = 0
        for turn in turns:
            flip ^= FLIPS[(2 * (i & 1) + turn) % 4]
        pairs += [(i * 16 + j, i * 16 + (j ^ flip)) for j in range(16)]
    return lax.ppermute(x, ("pre", "req"), pairs)


def quarter_step(x, k, turn):
    return req_step(x, [turn if k % 2 == 0 else 5 - turn])


def three_ways(xs):
    return [req_step(x, way) for x, way in zip(xs, ([0], [1], [0, 1]))]


def split3(x):
    hi = x.astype(BF).astype(F32)
    mid = (x - hi).astype(BF).astype(F32)
    low = (x - hi - mid).astype(BF).astype(F32)
    return hi, mid, low


def pack_kernel(of_ref, q_ref, rows_ref, out_ref, wide_ref, seen_ref, req_ref):
    count = q_ref.shape[0]
    for p in range(16):
        seen_ref[p] = 0
    for slot in range(32):
        req_ref[slot] = -1
    for r in range(count):
        p = of_ref[r]
        rank = seen_ref[p]
        seen_ref[p] = rank + 1
        req_ref[p * 2 + rank] = r
    for g in range(GROUP):
        wide_ref[:, pl.ds(g, STEPS, GROUP), :] = q_ref[:, :, g * HD:(g + 1) * HD].astype(F32)
    rows_ref[...] = wide_ref[...].astype(BF)
    nobody = jnp.full((ROWS, HD), EMPTY, BF)
    for slot in range(32):
        r = req_ref[slot]
        rows = rows_ref[jnp.maximum(r, 0)]
        at = (slot % 4) * ROWS
        out_ref[slot // 4, at:at + ROWS, :] = jnp.where(r >= 0, rows, nobody)


def pack(owners, queries):
    count = queries.shape[0]
    return pl.pallas_call(
        pack_kernel,
        out_shape=[
            jax.ShapeDtypeStruct((count, ROWS, HD), BF),
            jax.ShapeDtypeStruct((8, 128, HD), BF),
        ],
        in_specs=[pl.BlockSpec(memory_space=pltpu.SMEM), pl.BlockSpec(memory_space=pltpu.VMEM)],
        out_specs=[pl.BlockSpec(memory_space=pltpu.VMEM)] * 2,
        scratch_shapes=[
            pltpu.VMEM((count, ROWS, HD), F32),
            pltpu.SMEM((16,), jnp.int32),
            pltpu.SMEM((32,), jnp.int32),
        ],
        compiler_params=params(),
        name="pack_slots",
    )(owners, queries)


def join_kernel(groups, cuts, total, *refs):
    out_refs = refs[-groups * cuts:]
    ins = refs[:total]
    count = total // groups
    each = ins[0].shape[0]
    width = ins[0].shape[1] // cuts
    for g in range(groups):
        for c in range(cuts):
            for n in range(count):
                piece = ins[g * count + n][:, c * width:(c + 1) * width]
                out_refs[g * cuts + c][n * each:(n + 1) * each] = piece


def join(parts, groups=1, cuts=1, after=None):
    extra = [] if after is None else [after]
    first = parts[0].shape
    shape = (len(parts) // groups * first[0], first[1] // cuts) + first[2:]
    return pl.pallas_call(
        functools.partial(join_kernel, groups, cuts, len(parts)),
        out_shape=[jax.ShapeDtypeStruct(shape, BF)] * (groups * cuts),
        in_specs=[pl.BlockSpec(memory_space=pltpu.VMEM)] * len(parts)
        + [pl.BlockSpec(memory_space=pl.ANY)] * len(extra),
        out_specs=[pl.BlockSpec(memory_space=pltpu.VMEM)] * (groups * cuts),
        compiler_params=params(),
        name="join",
    )(*parts, *extra)


def prefix_kernel(count, first, extra, use_ref, *rest):
    q_refs, kv_hbm = rest[:count], rest[count]
    rest = rest[count + 1 + extra:]
    out_refs = rest[:count]
    q_all, kv_all, o_all, sa_ref, sb_ref, bias_ref, lse_ref, item_ref, many_ref, sems = rest[
        count:
    ]
    heads = 2 * count
    positions = kv_all.shape[1]
    blocks = q_all.shape[1]
    rows = blocks * ROWS

    def fetch(m, h):
        at = pl.multiple_of((2 * first + h) * (2 * HD), 2 * HD)
        return pltpu.make_async_copy(
            kv_hbm.at[m, :, pl.ds(at, 2 * HD)], kv_all.at[m * heads + h], sems.at[m * heads + h]
        )

    marks = [
        jnp.min(q_refs[0][:, 0, w * ROWS:w * ROWS + 16, :].astype(F32)) < 100.0 for w in range(4)
    ]
    live = [(use_ref[w // 2] > 0) & marks[w] for w in range(4)]

    many_ref[0] = 0
    for m in range(2):
        for rank in range(2):
            on = live[m * 2 + rank]

            @pl.when(on)
            def _():
                n = many_ref[0]
                for h in range(heads):
                    item_ref[n + h] = (m * 2 + rank) * heads + h
                    if rank == 0:
                        fetch(m, h).start()
                many_ref[0] = n + heads

            @pl.when(jnp.logical_not(on))
            def _():
                for side in range(2):
                    at = m * 128 + side * 64 + rank * ROWS
                    o_all[:, :, at:at + ROWS, :] = jnp.zeros((count, blocks, ROWS, HD), BF)

    for m in range(2):
        pos = lax.broadcasted_iota(jnp.int32, (8, positions), 1)
        bias_ref[m] = jnp.where(pos < use_ref[m], 0.0, NEG)
    lse_ref[...] = jnp.full(lse_ref.shape, NEG, F32)
    for c in range(count):
        for side in range(2):
            q_all[2 * c + side] = q_refs[c][:, side]
    n = many_ref[0]
    shift = heads.bit_length() - 1

    def decode(i):
        code = item_ref[jnp.minimum(i, n - 1)]
        h, which = code & (heads - 1), code >> shift
        return h, which, which >> 1, which & 1

    def score(i, s_ref):
        h, which, m, rank = decode(i)

        @pl.when((rank == 0) & (i < n))
        def _():
            fetch(m, h).wait()

        q = q_all[h, :, pl.ds(pl.multiple_of(which * ROWS, ROWS), ROWS), :].reshape(rows, HD)
        k = kv_all[m * heads + h, :, :HD]
        s = lax.dot_general(q, k, (((1,), (1,)), ((), ())), preferred_element_type=F32)
        s = s.reshape(rows // 8, 8, positions) + bias_ref[m][None]
        s_ref[...] = s.reshape(rows, positions)

    def weigh(i, s_ref):
        h, which, m, rank = decode(i)
        c, side = h >> 1, h & 1
        s = s_ref[...]
        top = jnp.max(s, axis=1, keepdims=True)
        p = jnp.exp2((s - top) * (ROOT * LOG2E)).astype(BF)
        v = kv_all[m * heads + h, :, HD:]
        v1 = jnp.concatenate([v, jnp.ones((positions, HD), BF)], axis=1)
        r = jnp.dot(p, v1, preferred_element_type=F32)
        den = r[:, HD:]
        o = r[:, :HD] / den
        lse = top * ROOT + jnp.log(den)
        at = pl.multiple_of(m * 128 + side * 64 + rank * ROWS, ROWS)
        o_all[c, :, pl.ds(at, ROWS), :] = o.reshape(blocks, ROWS, HD).astype(BF)
        part = side * 2 + rank
        row_id = lax.broadcasted_iota(jnp.int32, (ROWS, HD), 0)
        lane_id = lax.broadcasted_iota(jnp.int32, (ROWS, HD), 1)
        diag = (lane_id - row_id == part * ROWS)[None]
        flat = jnp.sum(jnp.where(diag, lse.reshape(blocks, ROWS, HD), 0.0), axis=1)
        lanes = lax.broadcasted_iota(jnp.int32, (blocks, HD), 1) >> 5
        old = lse_ref[c * 2 + m]
        lse_ref[c * 2 + m] = jnp.where(lanes == part, flat, old)

    @pl.when(n > 0)
    def _():
        score(0, sa_ref)

        def body(j, carry):
            score(2 * j + 1, sb_ref)
            weigh(2 * j, sa_ref)
            score(2 * j + 2, sa_ref)
            weigh(2 * j + 1, sb_ref)
            return carry

        lax.fori_loop(0, (n + 1) // 2, body, 0)

    for c in range(count):
        out_refs[c][:, :256, :] = o_all[c]
        out_refs[c][:, 256:, :] = lse_rows([lse_ref[2 * c + m][:, None, :] for m in range(2)])


def lse_rows(tops):
    shape = (tops[0].shape[0], -(-3 * len(tops) // 16) * 16, HD)
    row = lax.broadcasted_iota(jnp.int32, shape, 1)
    out = jnp.zeros(shape, F32)
    at = 0
    for top in tops:
        for piece in split3(top):
            out = jnp.where(row == at, jnp.broadcast_to(piece, shape), out)
            at += 1
    return out.astype(BF)


def prefix_attention(usable, qs, prefix_kv, first, after=None):
    count = len(qs)
    extra = [] if after is None else [after]
    heads = 2 * count
    blocks = qs[0].shape[0]
    positions = prefix_kv.shape[1]
    rows = blocks * ROWS
    work = rows * positions * heads * 3
    return pl.pallas_call(
        functools.partial(prefix_kernel, count, first, len(extra)),
        out_shape=[jax.ShapeDtypeStruct((blocks, 272, HD), BF)] * count,
        in_specs=[pl.BlockSpec(memory_space=pltpu.SMEM)]
        + [pl.BlockSpec(memory_space=pltpu.VMEM)] * count
        + [pl.BlockSpec(memory_space=pl.ANY)] * (1 + len(extra)),
        out_specs=[pl.BlockSpec(memory_space=pltpu.VMEM)] * count,
        scratch_shapes=[
            pltpu.VMEM((heads, blocks, 128, HD), BF),
            pltpu.VMEM((2 * heads, positions, 2 * HD), BF),
            pltpu.VMEM((count, blocks, 256, HD), BF),
            pltpu.VMEM((rows, positions), F32),
            pltpu.VMEM((rows, positions), F32),
            pltpu.VMEM((2, 8, positions), F32),
            pltpu.VMEM((heads, blocks, HD), F32),
            pltpu.SMEM((4 * heads,), jnp.int32),
            pltpu.SMEM((1,), jnp.int32),
            pltpu.SemaphoreType.DMA((2 * heads,)),
        ],
        compiler_params=params(),
        cost_estimate=pl.CostEstimate(
            flops=work * 512, bytes_accessed=heads << 20, transcendentals=work
        ),
        name="prefix_attention",
    )(usable, *qs, prefix_kv, *extra)


def blend_weights(la, lb):
    top = jnp.maximum(la, lb)
    ea, eb = jnp.exp(la - top), jnp.exp(lb - top)
    total = ea + eb
    return ea / total, top + jnp.log(total)


def spread(w):
    return jnp.broadcast_to(w, (HD, HD)).T


def read_lse(rows, m):
    return rows[3 * m:3 * m + 1] + rows[3 * m + 1:3 * m + 2] + rows[3 * m + 2:3 * m + 3]


def merge_line(a_ref, b_ref, idx):
    tiles = a_ref.shape[1] // 128
    ra = a_ref[idx, tiles * 128:, :].astype(F32)
    rb = b_ref[idx, tiles * 128:, :].astype(F32)
    datas, tops = [], []
    for m in range(tiles):
        wa, lse = blend_weights(read_lse(ra, m), read_lse(rb, m))
        oa = a_ref[idx, m * 128:(m + 1) * 128, :].astype(F32)
        ob = b_ref[idx, m * 128:(m + 1) * 128, :].astype(F32)
        datas.append(ob + spread(wa) * (oa - ob))
        tops.append(lse)
    return datas, tops


def merge_kernel(pairs, extra, *refs):
    ins, out_refs = refs[:2 * pairs], refs[2 * pairs + extra:]
    outs = [(ref, b) for ref in out_refs for b in range(ref.shape[0])]
    for spot, (out_ref, b) in reversed(list(enumerate(outs))):
        merged = [merge_line(ins[2 * c], ins[2 * c + 1], spot) for c in range(pairs)]
        datas = [d for row in zip(*[x[0] for x in merged]) for d in row]
        tops = [t for row in zip(*[x[1] for x in merged]) for t in row]
        tiles = len(datas)
        for m in range(tiles):
            out_ref[b, m * 128:(m + 1) * 128, :] = datas[m].astype(BF)
        out_ref[b, tiles * 128:, :] = lse_rows([t[None] for t in tops])[0]


def merge(ins, counts, after=None):
    extra = [] if after is None else [after]
    blocks, line = ins[0].shape[:2]
    pairs = len(ins) // 2
    tiles = (line // 128) * pairs
    extra_rows = -(-3 * tiles // 16) * 16
    return pl.pallas_call(
        functools.partial(merge_kernel, pairs, len(extra)),
        out_shape=[jax.ShapeDtypeStruct((n, tiles * 128 + extra_rows, HD), BF) for n in counts],
        in_specs=[pl.BlockSpec(memory_space=pltpu.VMEM)] * len(ins)
        + [pl.BlockSpec(memory_space=pl.ANY)] * len(extra),
        out_specs=[pl.BlockSpec(memory_space=pltpu.VMEM)] * len(counts),
        compiler_params=params(),
        cost_estimate=pl.CostEstimate(
            flops=blocks * tiles * 128 * 128 * 6,
            bytes_accessed=blocks * tiles * 128 * HD * 6,
            transcendentals=0,
        ),
        name="merge_step",
    )(*ins, *extra)


def last_kernel(*refs):
    parts, out_ref = refs[:4], refs[4]
    low = lax.broadcasted_iota(jnp.int32, (1, HD), 1) < 64
    rows = [p[0, 1024:, :].astype(F32) for p in parts]
    datas, tops = [], []
    for t in range(8):
        each = [read_lse(r, t) for r in rows]
        top = functools.reduce(jnp.maximum, each)
        es = [jnp.exp(x - top) for x in each]
        total = es[0] + es[1] + es[2] + es[3]
        data = 0.0
        for p, e in zip(parts, es):
            data = data + spread(e / total) * p[0, t * 128:(t + 1) * 128, :].astype(F32)
        datas.append(data)
        tops.append(top + jnp.log(total))
    rolled = [pltpu.roll(jnp.broadcast_to(t, (8, HD)), 64, 1)[0:1] for t in tops]
    for h in range(8):
        k, side = h // 2, h % 2
        if side == 0:
            joined = jnp.where(low, tops[k], rolled[4 + k])
        else:
            joined = jnp.where(low, rolled[k], tops[4 + k])
        for m in range(2):
            piece = datas[4 * m + k][side * 64:(side + 1) * 64]
            out_ref[h, m * 64:(m + 1) * 64, :] = piece.astype(BF)
        out_ref[h, 128:LAST, :] = lse_rows([joined[None]])[0]


def merge_last(parts):
    return pl.pallas_call(
        last_kernel,
        out_shape=jax.ShapeDtypeStruct((8, LAST, HD), BF),
        in_specs=[pl.BlockSpec(memory_space=pltpu.VMEM)] * 4,
        out_specs=pl.BlockSpec(memory_space=pltpu.VMEM),
        compiler_params=params(),
        name="merge_last",
    )(*parts)


def suffix_kernel(first, len_ref, q_ref, kv_ref, new_ref, o_ref, lse_ref):
    per = q_ref.shape[0]
    positions = kv_ref.shape[1]
    step_id = lax.broadcasted_iota(jnp.int32, (ROWS, 1), 0) // GROUP
    pos = lax.broadcasted_iota(jnp.int32, (ROWS, positions), 1)
    ones = jnp.ones((positions, HD), BF)
    for e in range(per):
        used = len_ref[first + pl.program_id(0) * per + e]
        q = q_ref[e]
        qf = q.astype(F32)
        fresh = new_ref[e].astype(F32)
        s = lax.dot_general(
            q, kv_ref[e, :, :HD], (((1,), (1,)), ((), ())), preferred_element_type=F32
        )
        s = jnp.where(pos < used, s, NEG)
        top = jnp.max(s, axis=1, keepdims=True)
        extra = []
        for t in range(STEPS):
            f = jnp.sum(qf * fresh[t:t + 1, :HD], axis=1, keepdims=True)
            f = jnp.where(step_id >= t, f, NEG)
            extra.append(f)
            top = jnp.maximum(top, f)
        p = jnp.exp2((s - top) * (ROOT * LOG2E)).astype(BF)
        r = jnp.dot(
            p, jnp.concatenate([kv_ref[e, :, HD:], ones], axis=1), preferred_element_type=F32
        )
        num, den = r[:, :HD], r[:, HD:]
        for t in range(STEPS):
            w = jnp.exp2((extra[t] - top) * (ROOT * LOG2E))
            num = num + w * fresh[t:t + 1, HD:]
            den = den + w
        o_ref[e] = num / den
        lse_ref[e] = top * ROOT + jnp.log(den)


def suffix_attention(suffix_len, q_rows, suffix_kv, new_kv, first, count):
    positions = suffix_kv.shape[1]
    per = 4
    skip = first // per
    one = jax.ShapeDtypeStruct((count, ROWS, HD), F32)
    grid_spec = pltpu.PrefetchScalarGridSpec(
        num_scalar_prefetch=1,
        grid=(count // per,),
        in_specs=[
            pl.BlockSpec((per, ROWS, HD), lambda s, n: (s + skip, 0, 0)),
            pl.BlockSpec((per, positions, 2 * HD), lambda s, n: (s + skip, 0, 0)),
            pl.BlockSpec((per, STEPS, 2 * HD), lambda s, n: (s + skip, 0, 0)),
        ],
        out_specs=[pl.BlockSpec((per, ROWS, HD), lambda s, n: (s, 0, 0))] * 2,
    )
    return pl.pallas_call(
        functools.partial(suffix_kernel, first),
        out_shape=[one, one],
        grid_spec=grid_spec,
        compiler_params=params(),
        cost_estimate=pl.CostEstimate(
            flops=count * 256 * positions * 128 * 4,
            bytes_accessed=count << 19,
            transcendentals=count * ROWS * positions,
        ),
        name="suffix_attention",
    )(suffix_len, q_rows, suffix_kv, new_kv)


def final_kernel(
    own_ref, off_ref, oa_ref, la_ref, ob_ref, lb_ref, part_ref, out_ref, data_ref, top_ref, wide_ref
):
    for t in range(8):
        data_ref[t] = part_ref[t, 0:128, :].astype(F32)
        rows = part_ref[t, 128:LAST, :].astype(F32)
        top_ref[t] = spread(read_lse(rows, 0))
    each = oa_ref.shape[0]
    for r in range(2 * each):
        o_ref, l_ref = (oa_ref, la_ref) if r < each else (ob_ref, lb_ref)
        at = pl.ds(pl.multiple_of(off_ref[r], ROWS), ROWS)
        op, lp = data_ref[own_ref[r], at, :], top_ref[own_ref[r], at, :]
        w, _ = blend_weights(lp, l_ref[r % each])
        ol = o_ref[r % each]
        wide_ref[r] = ol + w * (op - ol)
    for g in range(GROUP):
        out_ref[:, :, g * HD:(g + 1) * HD] = wide_ref[:, pl.ds(g, STEPS, GROUP), :].astype(BF)


def finish(own, off, local, parts):
    count = own.shape[0]
    return pl.pallas_call(
        final_kernel,
        out_shape=jax.ShapeDtypeStruct((count, STEPS, GROUP * HD), BF),
        in_specs=[pl.BlockSpec(memory_space=pltpu.SMEM)] * 2
        + [pl.BlockSpec(memory_space=pltpu.VMEM)] * 5,
        out_specs=pl.BlockSpec(memory_space=pltpu.VMEM),
        scratch_shapes=[
            pltpu.VMEM((8, HD, HD), F32),
            pltpu.VMEM((8, HD, HD), F32),
            pltpu.VMEM((count, ROWS, HD), F32),
        ],
        compiler_params=params(),
        name="finish",
    )(own, off, *local, parts)


def on_device(prefix_kv, prefix_len, prefix_of, suffix_len, suffix_kv, queries, new_kv):
    mine, block = lax.axis_index("pre"), lax.axis_index("req")
    shard = prefix_kv.shape[1]
    count = queries.shape[0]

    owners = prefix_of[:, 0]
    ids = jnp.arange(count, dtype=jnp.int32)
    earlier = (owners[None, :] == owners[:, None]) & (ids[None, :] < ids[:, None])
    rank = jnp.sum(earlier.astype(jnp.int32), axis=1)
    part = (owners & 1) * 2 + rank
    own_len = lax.dynamic_slice_in_dim(prefix_len, mine * 2, 2, 0)
    usable = jnp.clip(own_len - block * shard, 0, shard)

    q_rows, packed = pack(owners, queries)
    heads = lax.all_to_all(packed, "pre", 0, 0, tiled=True)
    local = []
    for first in (0, count // 2):
        local += suffix_attention(suffix_len, q_rows, suffix_kv, new_kv, first, count // 2)

    near = join([heads[None]] + three_ways([heads[None]] * 3), cuts=4, after=local[0])
    got = [quarter_step(near[k], k, 2) for k in range(4)]
    near = [join([near[k], got[k]])[0] for k in range(4)]
    far = [quarter_step(near[k], k, 3) for k in range(4)]
    keep = prefix_attention(usable, near[:2], prefix_kv, 0)
    send = prefix_attention(usable, far[:2], prefix_kv, 0, keep[0])
    send += prefix_attention(usable, far[2:], prefix_kv, 2)
    keep += prefix_attention(usable, near[2:], prefix_kv, 2)
    got = [quarter_step(send[k], k, 3) for k in range(4)]
    parts = [merge([keep[k], got[k]], [4, 4]) for k in range(4)]
    keep, send = [p[0] for p in parts], [p[1] for p in parts]
    got = [quarter_step(send[k], k, 2) for k in range(4)]
    parts = merge([x for pair in zip(keep, got) for x in pair], [1] * 4)
    final = merge_last([parts[0]] + three_ways(parts[1:]))
    back = lax.all_to_all(final, "pre", 0, 0, tiled=True)
    return finish(owners >> 1, part * ROWS, local, back)


def solution(mesh):
    placed = (
        P("pre", "req", None),
        P(),
        P("req", None),
        P("req"),
        P("req", None, "pre"),
        P("req", None, "pre"),
        P("req", None, "pre"),
    )
    return jax.shard_map(
        on_device, mesh=mesh, in_specs=placed, out_specs=P("req", None, "pre"), check_vma=False
    )
```

```python
import functools
import math

import jax
import jax.numpy as jnp
from jax import lax
from jax.experimental import pallas as pl
from jax.experimental.pallas import tpu as pltpu
from jax.sharding import PartitionSpec as P

HD = 128
GROUP = 8
STEPS = 4
ROWS = STEPS * GROUP
NEG = -1e30
ROOT = 1.0 / math.sqrt(HD)
LOG2E = math.log2(math.e)
EMPTY = 128.0
LAST = 144
BF = jnp.bfloat16
F32 = jnp.float32


def params(mb=48):
    return pltpu.CompilerParams(vmem_limit_bytes=mb * 1024 * 1024)


FLIPS = (1, 4, 3, 12)


def req_step(x, turns):
    pairs = []
    for i in range(8):
        flip = 0
        for turn in turns:
            flip ^= FLIPS[(2 * (i & 1) + turn) % 4]
        pairs += [(i * 16 + j, i * 16 + (j ^ flip)) for j in range(16)]
    return lax.ppermute(x, ("pre", "req"), pairs)


def quarter_step(x, k, turn):
    return req_step(x, [turn if k % 2 == 0 else 5 - turn])


def three_ways(xs):
    return [req_step(x, way) for x, way in zip(xs, ([0], [1], [0, 1]))]


def split3(x):
    hi = x.astype(BF).astype(F32)
    mid = (x - hi).astype(BF).astype(F32)
    low = (x - hi - mid).astype(BF).astype(F32)
    return hi, mid, low


def pack_kernel(of_ref, q_ref, rows_ref, out_ref, wide_ref, seen_ref, req_ref):
    count = q_ref.shape[0]
    for p in range(16):
        seen_ref[p] = 0
    for slot in range(32):
        req_ref[slot] = -1
    for r in range(count):
        p = of_ref[r]
        rank = seen_ref[p]
        seen_ref[p] = rank + 1
        req_ref[p * 2 + rank] = r
    for g in range(GROUP):
        wide_ref[:, pl.ds(g, STEPS, GROUP), :] = q_ref[:, :, g * HD:(g + 1) * HD].astype(F32)
    rows_ref[...] = wide_ref[...].astype(BF)
    nobody = jnp.full((ROWS, HD), EMPTY, BF)
    for slot in range(32):
        r = req_ref[slot]
        rows = rows_ref[jnp.maximum(r, 0)]
        at = (slot % 4) * ROWS
        out_ref[slot // 4, at:at + ROWS, :] = jnp.where(r >= 0, rows, nobody)


def pack(owners, queries):
    count = queries.shape[0]
    return pl.pallas_call(
        pack_kernel,
        out_shape=[
            jax.ShapeDtypeStruct((count, ROWS, HD), BF),
            jax.ShapeDtypeStruct((8, 128, HD), BF),
        ],
        in_specs=[pl.BlockSpec(memory_space=pltpu.SMEM), pl.BlockSpec(memory_space=pltpu.VMEM)],
        out_specs=[pl.BlockSpec(memory_space=pltpu.VMEM)] * 2,
        scratch_shapes=[
            pltpu.VMEM((count, ROWS, HD), F32),
            pltpu.SMEM((16,), jnp.int32),
            pltpu.SMEM((32,), jnp.int32),
        ],
        compiler_params=params(),
        name="pack_slots",
    )(owners, queries)


def join_kernel(groups, cuts, total, *refs):
    out_refs = refs[-groups * cuts:]
    ins = refs[:total]
    count = total // groups
    each = ins[0].shape[0]
    width = ins[0].shape[1] // cuts
    for g in range(groups):
        for c in range(cuts):
            for n in range(count):
                piece = ins[g * count + n][:, c * width:(c + 1) * width]
                out_refs[g * cuts + c][n * each:(n + 1) * each] = piece


def join(parts, groups=1, cuts=1, after=None):
    extra = [] if after is None else [after]
    first = parts[0].shape
    shape = (len(parts) // groups * first[0], first[1] // cuts) + first[2:]
    return pl.pallas_call(
        functools.partial(join_kernel, groups, cuts, len(parts)),
        out_shape=[jax.ShapeDtypeStruct(shape, BF)] * (groups * cuts),
        in_specs=[pl.BlockSpec(memory_space=pltpu.VMEM)] * len(parts)
        + [pl.BlockSpec(memory_space=pl.ANY)] * len(extra),
        out_specs=[pl.BlockSpec(memory_space=pltpu.VMEM)] * (groups * cuts),
        compiler_params=params(),
        name="join",
    )(*parts, *extra)


def prefix_kernel(count, first, extra, use_ref, *rest):
    q_refs, kv_hbm = rest[:count], rest[count]
    rest = rest[count + 1 + extra:]
    out_refs = rest[:count]
    kv_all, sa_ref, sb_ref, bias_ref, lse_ref, group_ref, many_ref, sems = rest[
        count:
    ]
    heads = 2 * count
    positions = kv_all.shape[1]
    blocks = q_refs[0].shape[0]
    rows = blocks * ROWS

    def fetch(m, h):
        at = pl.multiple_of((2 * first + h) * (2 * HD), 2 * HD)
        return pltpu.make_async_copy(
            kv_hbm.at[m, :, pl.ds(at, 2 * HD)], kv_all.at[m * heads + h], sems.at[m * heads + h]
        )

    marks = [
        jnp.min(q_refs[0][:, 0, w * ROWS:w * ROWS + 16, :].astype(F32)) < 100.0 for w in range(4)
    ]
    live = [(use_ref[w // 2] > 0) & marks[w] for w in range(4)]

    many_ref[0] = 0
    for m in range(2):
        for rank in range(2):
            on = live[m * 2 + rank]

            @pl.when(on)
            def _():
                n = many_ref[0]
                group_ref[n] = m * 2 + rank
                if rank == 0:
                    for h in range(heads):
                        fetch(m, h).start()
                many_ref[0] = n + 1

            @pl.when(jnp.logical_not(on))
            def _():
                for side in range(2):
                    at = m * 128 + side * 64 + rank * ROWS
                    for c in range(count):
                        out_refs[c][:, at:at + ROWS, :] = jnp.zeros((blocks, ROWS, HD), BF)

    for m in range(2):
        pos = lax.broadcasted_iota(jnp.int32, (8, positions), 1)
        bias_ref[m] = jnp.where(pos < use_ref[m], 0.0, NEG)
    lse_ref[...] = jnp.full(lse_ref.shape, NEG, F32)
    n = many_ref[0]

    def decode(i):
        which = group_ref[jnp.minimum(i, n - 1)]
        return which, which >> 1, which & 1

    def arrive(i, hs):
        which, m, rank = decode(i)

        @pl.when((rank == 0) & (i < n))
        def _():
            for h in hs:
                fetch(m, h).wait()

    def score(i, h, s_ref):
        which, m, rank = decode(i)
        at = pl.ds(pl.multiple_of(which * ROWS, ROWS), ROWS)
        q = q_refs[h // 2][:, h % 2, at, :].reshape(rows, HD)
        k = kv_all[m * heads + h, :, :HD]
        s = lax.dot_general(q, k, (((1,), (1,)), ((), ())), preferred_element_type=F32)
        s = s.reshape(rows // 8, 8, positions) + bias_ref[m][None]
        s_ref[...] = s.reshape(rows, positions)

    def weigh(i, h, s_ref):
        which, m, rank = decode(i)
        c, side = h // 2, h % 2
        s = s_ref[...]
        top = jnp.max(s, axis=1, keepdims=True)
        p = jnp.exp2((s - top) * (ROOT * LOG2E)).astype(BF)
        v = kv_all[m * heads + h, :, HD:]
        v1 = jnp.concatenate([v, jnp.ones((positions, HD), BF)], axis=1)
        r = jnp.dot(p, v1, preferred_element_type=F32)
        den = r[:, HD:]
        o = r[:, :HD] / den
        lse = top * ROOT + jnp.log(den)
        at = pl.multiple_of(m * 128 + side * 64 + rank * ROWS, ROWS)
        out_refs[c][:, pl.ds(at, ROWS), :] = o.reshape(blocks, ROWS, HD).astype(BF)
        part = side * 2 + rank
        row_id = lax.broadcasted_iota(jnp.int32, (ROWS, HD), 0)
        lane_id = lax.broadcasted_iota(jnp.int32, (ROWS, HD), 1)
        diag = (lane_id - row_id == part * ROWS)[None]
        flat = jnp.sum(jnp.where(diag, lse.reshape(blocks, ROWS, HD), 0.0), axis=1)
        lanes = lax.broadcasted_iota(jnp.int32, (blocks, HD), 1) >> 5
        old = lse_ref[c * 2 + m]
        lse_ref[c * 2 + m] = jnp.where(lanes == part, flat, old)

    @pl.when(n > 0)
    def _():
        arrive(0, [0])
        score(0, 0, sa_ref)

        def body(j, carry):
            arrive(j, range(1, heads))
            arrive(j + 1, [0])
            for h in range(heads):
                now, later = (sa_ref, sb_ref) if h % 2 == 0 else (sb_ref, sa_ref)
                if h + 1 < heads:
                    score(j, h + 1, later)
                else:
                    score(j + 1, 0, later)
                weigh(j, h, now)
            return carry

        lax.fori_loop(0, n, body, 0)

    for c in range(count):
        out_refs[c][:, 256:, :] = lse_rows([lse_ref[2 * c + m][:, None, :] for m in range(2)])


def lse_rows(tops):
    shape = (tops[0].shape[0], -(-3 * len(tops) // 16) * 16, HD)
    row = lax.broadcasted_iota(jnp.int32, shape, 1)
    out = jnp.zeros(shape, F32)
    at = 0
    for top in tops:
        for piece in split3(top):
            out = jnp.where(row == at, jnp.broadcast_to(piece, shape), out)
            at += 1
    return out.astype(BF)


def prefix_attention(usable, qs, prefix_kv, first, after=None):
    count = len(qs)
    extra = [] if after is None else [after]
    heads = 2 * count
    blocks = qs[0].shape[0]
    positions = prefix_kv.shape[1]
    rows = blocks * ROWS
    work = rows * positions * heads * 3
    return pl.pallas_call(
        functools.partial(prefix_kernel, count, first, len(extra)),
        out_shape=[jax.ShapeDtypeStruct((blocks, 272, HD), BF)] * count,
        in_specs=[pl.BlockSpec(memory_space=pltpu.SMEM)]
        + [pl.BlockSpec(memory_space=pltpu.VMEM)] * count
        + [pl.BlockSpec(memory_space=pl.ANY)] * (1 + len(extra)),
        out_specs=[pl.BlockSpec(memory_space=pltpu.VMEM)] * count,
        scratch_shapes=[
            pltpu.VMEM((2 * heads, positions, 2 * HD), BF),
            pltpu.VMEM((rows, positions), F32),
            pltpu.VMEM((rows, positions), F32),
            pltpu.VMEM((2, 8, positions), F32),
            pltpu.VMEM((heads, blocks, HD), F32),
            pltpu.SMEM((4,), jnp.int32),
            pltpu.SMEM((1,), jnp.int32),
            pltpu.SemaphoreType.DMA((2 * heads,)),
        ],
        compiler_params=params(),
        cost_estimate=pl.CostEstimate(
            flops=work * 512, bytes_accessed=heads << 20, transcendentals=work
        ),
        name="prefix_attention",
    )(usable, *qs, prefix_kv, *extra)


def blend_weights(la, lb):
    top = jnp.maximum(la, lb)
    ea, eb = jnp.exp(la - top), jnp.exp(lb - top)
    total = ea + eb
    return ea / total, top + jnp.log(total)


def spread(w):
    return jnp.broadcast_to(w, (HD, HD)).T


def read_lse(rows, m):
    return rows[3 * m:3 * m + 1] + rows[3 * m + 1:3 * m + 2] + rows[3 * m + 2:3 * m + 3]


def merge_line(a_ref, b_ref, idx):
    tiles = a_ref.shape[1] // 128
    ra = a_ref[idx, tiles * 128:, :].astype(F32)
    rb = b_ref[idx, tiles * 128:, :].astype(F32)
    datas, tops = [], []
    for m in range(tiles):
        wa, lse = blend_weights(read_lse(ra, m), read_lse(rb, m))
        oa = a_ref[idx, m * 128:(m + 1) * 128, :].astype(F32)
        ob = b_ref[idx, m * 128:(m + 1) * 128, :].astype(F32)
        datas.append(ob + spread(wa) * (oa - ob))
        tops.append(lse)
    return datas, tops


def merge_kernel(pairs, extra, *refs):
    ins, out_refs = refs[:2 * pairs], refs[2 * pairs + extra:]
    outs = [(ref, b) for ref in out_refs for b in range(ref.shape[0])]
    for spot, (out_ref, b) in reversed(list(enumerate(outs))):
        merged = [merge_line(ins[2 * c], ins[2 * c + 1], spot) for c in range(pairs)]
        datas = [d for row in zip(*[x[0] for x in merged]) for d in row]
        tops = [t for row in zip(*[x[1] for x in merged]) for t in row]
        tiles = len(datas)
        for m in range(tiles):
            out_ref[b, m * 128:(m + 1) * 128, :] = datas[m].astype(BF)
        out_ref[b, tiles * 128:, :] = lse_rows([t[None] for t in tops])[0]


def merge(ins, counts, after=None):
    extra = [] if after is None else [after]
    blocks, line = ins[0].shape[:2]
    pairs = len(ins) // 2
    tiles = (line // 128) * pairs
    extra_rows = -(-3 * tiles // 16) * 16
    return pl.pallas_call(
        functools.partial(merge_kernel, pairs, len(extra)),
        out_shape=[jax.ShapeDtypeStruct((n, tiles * 128 + extra_rows, HD), BF) for n in counts],
        in_specs=[pl.BlockSpec(memory_space=pltpu.VMEM)] * len(ins)
        + [pl.BlockSpec(memory_space=pl.ANY)] * len(extra),
        out_specs=[pl.BlockSpec(memory_space=pltpu.VMEM)] * len(counts),
        compiler_params=params(),
        cost_estimate=pl.CostEstimate(
            flops=blocks * tiles * 128 * 128 * 6,
            bytes_accessed=blocks * tiles * 128 * HD * 6,
            transcendentals=0,
        ),
        name="merge_step",
    )(*ins, *extra)


def last_kernel(*refs):
    parts, out_ref = refs[:4], refs[5]
    low = lax.broadcasted_iota(jnp.int32, (1, HD), 1) < 64
    rows = [p[0, 1024:, :].astype(F32) for p in parts]
    datas, tops = [], []
    for t in range(8):
        each = [read_lse(r, t) for r in rows]
        top = functools.reduce(jnp.maximum, each)
        es = [jnp.exp(x - top) for x in each]
        total = es[0] + es[1] + es[2] + es[3]
        data = 0.0
        for p, e in zip(parts, es):
            data = data + spread(e / total) * p[0, t * 128:(t + 1) * 128, :].astype(F32)
        datas.append(data)
        tops.append(top + jnp.log(total))
    rolled = [pltpu.roll(jnp.broadcast_to(t, (8, HD)), 64, 1)[0:1] for t in tops]
    for h in range(8):
        k, side = h // 2, h % 2
        if side == 0:
            joined = jnp.where(low, tops[k], rolled[4 + k])
        else:
            joined = jnp.where(low, rolled[k], tops[4 + k])
        for m in range(2):
            piece = datas[4 * m + k][side * 64:(side + 1) * 64]
            out_ref[h, m * 64:(m + 1) * 64, :] = piece.astype(BF)
        out_ref[h, 128:LAST, :] = lse_rows([joined[None]])[0]


def merge_last(parts, after):
    return pl.pallas_call(
        last_kernel,
        out_shape=jax.ShapeDtypeStruct((8, LAST, HD), BF),
        in_specs=[pl.BlockSpec(memory_space=pltpu.VMEM)] * 4
        + [pl.BlockSpec(memory_space=pl.ANY)],
        out_specs=pl.BlockSpec(memory_space=pltpu.VMEM),
        compiler_params=params(),
        name="merge_last",
    )(*parts, after)


def suffix_kernel(first, len_ref, q_ref, kv_ref, new_ref, o_ref, lse_ref):
    per = q_ref.shape[0]
    positions = kv_ref.shape[1]
    step_id = lax.broadcasted_iota(jnp.int32, (ROWS, 1), 0) // GROUP
    pos = lax.broadcasted_iota(jnp.int32, (ROWS, positions), 1)
    ones = jnp.ones((positions, HD), BF)
    for e in range(per):
        used = len_ref[first + pl.program_id(0) * per + e]
        q = q_ref[e]
        qf = q.astype(F32)
        fresh = new_ref[e].astype(F32)
        s = lax.dot_general(
            q, kv_ref[e, :, :HD], (((1,), (1,)), ((), ())), preferred_element_type=F32
        )
        s = jnp.where(pos < used, s, NEG)
        top = jnp.max(s, axis=1, keepdims=True)
        extra = []
        for t in range(STEPS):
            f = jnp.sum(qf * fresh[t:t + 1, :HD], axis=1, keepdims=True)
            f = jnp.where(step_id >= t, f, NEG)
            extra.append(f)
            top = jnp.maximum(top, f)
        p = jnp.exp2((s - top) * (ROOT * LOG2E)).astype(BF)
        r = jnp.dot(
            p, jnp.concatenate([kv_ref[e, :, HD:], ones], axis=1), preferred_element_type=F32
        )
        num, den = r[:, :HD], r[:, HD:]
        for t in range(STEPS):
            w = jnp.exp2((extra[t] - top) * (ROOT * LOG2E))
            num = num + w * fresh[t:t + 1, HD:]
            den = den + w
        o_ref[e] = num / den
        lse_ref[e] = top * ROOT + jnp.log(den)


def suffix_attention(suffix_len, q_rows, suffix_kv, new_kv, first, count):
    positions = suffix_kv.shape[1]
    per = 4
    skip = first // per
    one = jax.ShapeDtypeStruct((count, ROWS, HD), F32)
    grid_spec = pltpu.PrefetchScalarGridSpec(
        num_scalar_prefetch=1,
        grid=(count // per,),
        in_specs=[
            pl.BlockSpec((per, ROWS, HD), lambda s, n: (s + skip, 0, 0)),
            pl.BlockSpec((per, positions, 2 * HD), lambda s, n: (s + skip, 0, 0)),
            pl.BlockSpec((per, STEPS, 2 * HD), lambda s, n: (s + skip, 0, 0)),
        ],
        out_specs=[pl.BlockSpec((per, ROWS, HD), lambda s, n: (s, 0, 0))] * 2,
    )
    return pl.pallas_call(
        functools.partial(suffix_kernel, first),
        out_shape=[one, one],
        grid_spec=grid_spec,
        compiler_params=params(),
        cost_estimate=pl.CostEstimate(
            flops=count * 256 * positions * 128 * 4,
            bytes_accessed=count << 19,
            transcendentals=count * ROWS * positions,
        ),
        name="suffix_attention",
    )(suffix_len, q_rows, suffix_kv, new_kv)


def final_kernel(
    own_ref, off_ref, oa_ref, la_ref, ob_ref, lb_ref, part_ref, out_ref, data_ref, top_ref, wide_ref
):
    for t in range(8):
        data_ref[t] = part_ref[t, 0:128, :].astype(F32)
        rows = part_ref[t, 128:LAST, :].astype(F32)
        top_ref[t] = spread(read_lse(rows, 0))
    each = oa_ref.shape[0]
    for r in range(2 * each):
        o_ref, l_ref = (oa_ref, la_ref) if r < each else (ob_ref, lb_ref)
        at = pl.ds(pl.multiple_of(off_ref[r], ROWS), ROWS)
        op, lp = data_ref[own_ref[r], at, :], top_ref[own_ref[r], at, :]
        w, _ = blend_weights(lp, l_ref[r % each])
        ol = o_ref[r % each]
        wide_ref[r] = ol + w * (op - ol)
    for g in range(GROUP):
        out_ref[:, :, g * HD:(g + 1) * HD] = wide_ref[:, pl.ds(g, STEPS, GROUP), :].astype(BF)


def finish(own, off, local, parts):
    count = own.shape[0]
    return pl.pallas_call(
        final_kernel,
        out_shape=jax.ShapeDtypeStruct((count, STEPS, GROUP * HD), BF),
        in_specs=[pl.BlockSpec(memory_space=pltpu.SMEM)] * 2
        + [pl.BlockSpec(memory_space=pltpu.VMEM)] * 5,
        out_specs=pl.BlockSpec(memory_space=pltpu.VMEM),
        scratch_shapes=[
            pltpu.VMEM((8, HD, HD), F32),
            pltpu.VMEM((8, HD, HD), F32),
            pltpu.VMEM((count, ROWS, HD), F32),
        ],
        compiler_params=params(),
        name="finish",
    )(own, off, *local, parts)


def on_device(prefix_kv, prefix_len, prefix_of, suffix_len, suffix_kv, queries, new_kv):
    mine, block = lax.axis_index("pre"), lax.axis_index("req")
    shard = prefix_kv.shape[1]
    count = queries.shape[0]

    owners = prefix_of[:, 0]
    ids = jnp.arange(count, dtype=jnp.int32)
    earlier = (owners[None, :] == owners[:, None]) & (ids[None, :] < ids[:, None])
    rank = jnp.sum(earlier.astype(jnp.int32), axis=1)
    part = (owners & 1) * 2 + rank
    own_len = lax.dynamic_slice_in_dim(prefix_len, mine * 2, 2, 0)
    usable = jnp.clip(own_len - block * shard, 0, shard)

    q_rows, packed = pack(owners, queries)
    heads = lax.all_to_all(packed, "pre", 0, 0, tiled=True)
    local = []
    for first in (0, count // 2):
        local += suffix_attention(suffix_len, q_rows, suffix_kv, new_kv, first, count // 2)

    near = join([heads[None]] + three_ways([heads[None]] * 3), cuts=4, after=local[0])
    got = [quarter_step(near[k], k, 2) for k in range(4)]
    near = [join([near[k], got[k]])[0] for k in range(4)]
    far = [quarter_step(near[k], k, 3) for k in range(4)]
    keep = prefix_attention(usable, near[:2], prefix_kv, 0)
    send = prefix_attention(usable, far[:2], prefix_kv, 0, keep[0])
    send += prefix_attention(usable, far[2:], prefix_kv, 2)
    keep += prefix_attention(usable, near[2:], prefix_kv, 2)
    got = [quarter_step(send[k], k, 3) for k in range(4)]
    parts = [merge([keep[k], got[k]], [4, 4]) for k in range(4)]
    keep, send = [p[0] for p in parts], [p[1] for p in parts]
    got = [quarter_step(send[k], k, 2) for k in range(4)]
    parts = merge([x for pair in zip(keep, got) for x in pair], [1] * 4)
    final = merge_last([parts[0]] + three_ways(parts[1:]), local[2])
    back = lax.all_to_all(final, "pre", 0, 0, tiled=True)
    return finish(owners >> 1, part * ROWS, local, back)


def solution(mesh):
    placed = (
        P("pre", "req", None),
        P(),
        P("req", None),
        P("req"),
        P("req", None, "pre"),
        P("req", None, "pre"),
        P("req", None, "pre"),
    )
    return jax.shard_map(
        on_device, mesh=mesh, in_specs=placed, out_specs=P("req", None, "pre"), check_vma=False
    )
```

```python
import functools
import math

import jax
import jax.numpy as jnp
from jax import lax
from jax.experimental import pallas as pl
from jax.experimental.pallas import tpu as pltpu
from jax.sharding import PartitionSpec as P

HD = 128
GROUP = 8
STEPS = 4
ROWS = STEPS * GROUP
NEG = -1e30
ROOT = 1.0 / math.sqrt(HD)
LOG2E = math.log2(math.e)
EMPTY = 128.0
LAST = 144
BF = jnp.bfloat16
F32 = jnp.float32


def params(mb=48):
    return pltpu.CompilerParams(vmem_limit_bytes=mb * 1024 * 1024)


FLIPS = (1, 4, 3, 12)


def req_step(x, turns):
    pairs = []
    for i in range(8):
        flip = 0
        for turn in turns:
            flip ^= FLIPS[(2 * (i & 1) + turn) % 4]
        pairs += [(i * 16 + j, i * 16 + (j ^ flip)) for j in range(16)]
    return lax.ppermute(x, ("pre", "req"), pairs)


def three_ways(xs, first):
    ways = ([first], [first + 1], [first, first + 1])
    return [req_step(x, way) for x, way in zip(xs, ways)]


def split3(x):
    hi = x.astype(BF).astype(F32)
    mid = (x - hi).astype(BF).astype(F32)
    low = (x - hi - mid).astype(BF).astype(F32)
    return hi, mid, low


def pack_kernel(of_ref, q_ref, rows_ref, out_ref, wide_ref, seen_ref, req_ref):
    count = q_ref.shape[0]
    for p in range(16):
        seen_ref[p] = 0
    for slot in range(32):
        req_ref[slot] = -1
    for r in range(count):
        p = of_ref[r]
        rank = seen_ref[p]
        seen_ref[p] = rank + 1
        req_ref[p * 2 + rank] = r
    for g in range(GROUP):
        wide_ref[:, pl.ds(g, STEPS, GROUP), :] = q_ref[:, :, g * HD:(g + 1) * HD].astype(F32)
    rows_ref[...] = wide_ref[...].astype(BF)
    nobody = jnp.full((ROWS, HD), EMPTY, BF)
    for slot in range(32):
        r = req_ref[slot]
        rows = rows_ref[jnp.maximum(r, 0)]
        at = (slot % 4) * ROWS
        out_ref[slot // 4, at:at + ROWS, :] = jnp.where(r >= 0, rows, nobody)


def pack(owners, queries):
    count = queries.shape[0]
    return pl.pallas_call(
        pack_kernel,
        out_shape=[
            jax.ShapeDtypeStruct((count, ROWS, HD), BF),
            jax.ShapeDtypeStruct((8, 128, HD), BF),
        ],
        in_specs=[pl.BlockSpec(memory_space=pltpu.SMEM), pl.BlockSpec(memory_space=pltpu.VMEM)],
        out_specs=[pl.BlockSpec(memory_space=pltpu.VMEM)] * 2,
        scratch_shapes=[
            pltpu.VMEM((count, ROWS, HD), F32),
            pltpu.SMEM((16,), jnp.int32),
            pltpu.SMEM((32,), jnp.int32),
        ],
        compiler_params=params(),
        name="pack_slots",
    )(owners, queries)


def join_kernel(groups, cuts, total, *refs):
    out_refs = refs[-groups * cuts:]
    ins = refs[:total]
    count = total // groups
    each = ins[0].shape[0]
    width = ins[0].shape[1] // cuts
    for g in range(groups):
        for c in range(cuts):
            for n in range(count):
                piece = ins[g * count + n][:, c * width:(c + 1) * width]
                out_refs[g * cuts + c][n * each:(n + 1) * each] = piece


def join(parts, groups=1, cuts=1, after=None):
    extra = [] if after is None else [after]
    first = parts[0].shape
    shape = (len(parts) // groups * first[0], first[1] // cuts) + first[2:]
    return pl.pallas_call(
        functools.partial(join_kernel, groups, cuts, len(parts)),
        out_shape=[jax.ShapeDtypeStruct(shape, BF)] * (groups * cuts),
        in_specs=[pl.BlockSpec(memory_space=pltpu.VMEM)] * len(parts)
        + [pl.BlockSpec(memory_space=pl.ANY)] * len(extra),
        out_specs=[pl.BlockSpec(memory_space=pltpu.VMEM)] * (groups * cuts),
        compiler_params=params(),
        name="join",
    )(*parts, *extra)


def prefix_kernel(count, first, extra, use_ref, *rest):
    q_refs, kv_hbm = rest[:count], rest[count]
    rest = rest[count + 1 + extra:]
    out_refs = rest[:count]
    kv_all, sa_ref, sb_ref, bias_ref, lse_ref, group_ref, many_ref, sems = rest[
        count:
    ]
    each, heads = q_refs[0].shape[:2]
    positions = kv_all.shape[1]
    blocks = each * count
    rows = blocks * ROWS

    def fetch(m, h):
        at = (first + h) * (2 * HD)
        return pltpu.make_async_copy(
            kv_hbm.at[m, :, pl.ds(at, 2 * HD)], kv_all.at[m * heads + h], sems.at[m * heads + h]
        )

    marks = [
        jnp.min(
            functools.reduce(
                jnp.minimum, [r[:, 0, w * ROWS:w * ROWS + 16, :].astype(F32) for r in q_refs]
            )
        )
        < 100.0
        for w in range(4)
    ]
    live = [(use_ref[w // 2] > 0) & marks[w] for w in range(4)]

    many_ref[0] = 0
    for m in range(2):
        for rank in range(2):
            on = live[m * 2 + rank]

            @pl.when(on)
            def _():
                n = many_ref[0]
                group_ref[n] = m * 2 + rank
                if rank == 0:
                    for h in range(heads):
                        fetch(m, h).start()
                many_ref[0] = n + 1

            @pl.when(jnp.logical_not(on))
            def _():
                for h in range(heads):
                    at = m * 256 + h * 64 + rank * ROWS
                    for c in range(count):
                        out_refs[c][:, at:at + ROWS, :] = jnp.zeros((each, ROWS, HD), BF)

    for m in range(2):
        pos = lax.broadcasted_iota(jnp.int32, (8, positions), 1)
        bias_ref[m] = jnp.where(pos < use_ref[m], 0.0, NEG)
    lse_ref[...] = jnp.full(lse_ref.shape, NEG, F32)
    n = many_ref[0]

    def decode(i):
        which = group_ref[jnp.minimum(i, n - 1)]
        return which, which >> 1, which & 1

    def arrive(i, hs):
        which, m, rank = decode(i)

        @pl.when((rank == 0) & (i < n))
        def _():
            for h in hs:
                fetch(m, h).wait()

    def score(i, h, s_ref):
        which, m, rank = decode(i)
        at = pl.ds(pl.multiple_of(which * ROWS, ROWS), ROWS)
        q = [r[:, h, at, :].reshape(each * ROWS, HD) for r in q_refs]
        q = q[0] if count == 1 else jnp.concatenate(q, axis=0)
        k = kv_all[m * heads + h, :, :HD]
        s = lax.dot_general(q, k, (((1,), (1,)), ((), ())), preferred_element_type=F32)
        s = s.reshape(rows // 8, 8, positions) + bias_ref[m][None]
        s_ref[...] = s.reshape(rows, positions)

    def weigh(i, h, s_ref):
        which, m, rank = decode(i)
        tile, side = m * 2 + h // 2, h % 2
        s = s_ref[...]
        top = jnp.max(s, axis=1, keepdims=True)
        p = jnp.exp2((s - top) * (ROOT * LOG2E)).astype(BF)
        v = kv_all[m * heads + h, :, HD:]
        v1 = jnp.concatenate([v, jnp.ones((positions, HD), BF)], axis=1)
        r = jnp.dot(p, v1, preferred_element_type=F32)
        den = r[:, HD:]
        o = r[:, :HD] / den
        lse = top * ROOT + jnp.log(den)
        at = pl.multiple_of(m * 256 + h * 64 + rank * ROWS, ROWS)
        o = o.reshape(blocks, ROWS, HD).astype(BF)
        for c in range(count):
            out_refs[c][:, pl.ds(at, ROWS), :] = o[c * each:(c + 1) * each]
        part = side * 2 + rank
        row_id = lax.broadcasted_iota(jnp.int32, (ROWS, HD), 0)
        lane_id = lax.broadcasted_iota(jnp.int32, (ROWS, HD), 1)
        diag = (lane_id - row_id == part * ROWS)[None]
        flat = jnp.sum(jnp.where(diag, lse.reshape(blocks, ROWS, HD), 0.0), axis=1)
        lanes = lax.broadcasted_iota(jnp.int32, (blocks, HD), 1) >> 5
        lse_ref[tile] = jnp.where(lanes == part, flat, lse_ref[tile])

    @pl.when(n > 0)
    def _():
        arrive(0, [0])
        score(0, 0, sa_ref)

        def body(j, carry):
            arrive(j, range(1, heads))
            arrive(j + 1, [0])
            for h in range(heads):
                now, later = (sa_ref, sb_ref) if h % 2 == 0 else (sb_ref, sa_ref)
                if h + 1 < heads:
                    score(j, h + 1, later)
                else:
                    score(j + 1, 0, later)
                weigh(j, h, now)
            return carry

        lax.fori_loop(0, n, body, 0)

    for c in range(count):
        tops = [lse_ref[t, c * each:(c + 1) * each, :][:, None, :] for t in range(4)]
        out_refs[c][:, 512:, :] = lse_rows(tops)


def lse_rows(tops):
    shape = (tops[0].shape[0], -(-3 * len(tops) // 16) * 16, HD)
    row = lax.broadcasted_iota(jnp.int32, shape, 1)
    out = jnp.zeros(shape, F32)
    at = 0
    for top in tops:
        for piece in split3(top):
            out = jnp.where(row == at, jnp.broadcast_to(piece, shape), out)
            at += 1
    return out.astype(BF)


def prefix_attention(usable, prefix_kv, qs, first, after=None):
    count = len(qs)
    extra = [] if after is None else [after]
    each, heads = qs[0].shape[:2]
    blocks = each * count
    positions = prefix_kv.shape[1]
    rows = blocks * ROWS
    work = rows * positions * heads * 3
    return pl.pallas_call(
        functools.partial(prefix_kernel, count, first, len(extra)),
        out_shape=[jax.ShapeDtypeStruct((each, 528, HD), BF)] * count,
        in_specs=[pl.BlockSpec(memory_space=pltpu.SMEM)]
        + [pl.BlockSpec(memory_space=pltpu.VMEM)] * count
        + [pl.BlockSpec(memory_space=pl.ANY)] * (1 + len(extra)),
        out_specs=[pl.BlockSpec(memory_space=pltpu.VMEM)] * count,
        scratch_shapes=[
            pltpu.VMEM((2 * heads, positions, 2 * HD), BF),
            pltpu.VMEM((rows, positions), F32),
            pltpu.VMEM((rows, positions), F32),
            pltpu.VMEM((2, 8, positions), F32),
            pltpu.VMEM((4, blocks, HD), F32),
            pltpu.SMEM((4,), jnp.int32),
            pltpu.SMEM((1,), jnp.int32),
            pltpu.SemaphoreType.DMA((2 * heads,)),
        ],
        compiler_params=params(),
        cost_estimate=pl.CostEstimate(
            flops=work * 512, bytes_accessed=heads << 20, transcendentals=work
        ),
        name="prefix_attention",
    )(usable, *qs, prefix_kv, *extra)


def blend_weights(la, lb):
    top = jnp.maximum(la, lb)
    ea, eb = jnp.exp(la - top), jnp.exp(lb - top)
    total = ea + eb
    return ea / total, top + jnp.log(total)


def spread(w):
    return jnp.broadcast_to(w, (HD, HD)).T


def read_lse(rows, m):
    return rows[3 * m:3 * m + 1] + rows[3 * m + 1:3 * m + 2] + rows[3 * m + 2:3 * m + 3]


def merge_line(refs, idx):
    tiles = refs[0].shape[1] // 128
    rows = [r[idx, tiles * 128:, :].astype(F32) for r in refs]
    datas, tops = [], []
    for t in range(tiles):
        lses = [read_lse(r, t) for r in rows]
        top = functools.reduce(jnp.maximum, lses)
        es = [jnp.exp(x - top) for x in lses]
        total = functools.reduce(jnp.add, es)
        blocks = [r[idx, t * 128:(t + 1) * 128, :].astype(F32) for r in refs]
        data = blocks[-1]
        for e, o in zip(es[:-1], blocks[:-1]):
            data = data + spread(e / total) * (o - blocks[-1])
        datas.append(data)
        tops.append(top + jnp.log(total))
    return datas, tops


def merge_kernel(sides, ways, *refs):
    ins, out_refs = refs[:sides * ways], refs[sides * ways:]
    outs = [(ref, b) for ref in out_refs for b in range(ref.shape[0])]
    for spot, (out_ref, b) in reversed(list(enumerate(outs))):
        merged = [merge_line(ins[c * ways:(c + 1) * ways], spot) for c in range(sides)]
        tiles = len(merged[0][0])
        order = [(c, m * 2 + k) for m in range(tiles // 2) for c in range(sides) for k in range(2)]
        for n, (c, t) in enumerate(order):
            out_ref[b, n * 128:(n + 1) * 128, :] = merged[c][0][t].astype(BF)
        out_ref[b, len(order) * 128:, :] = lse_rows([merged[c][1][t][None] for c, t in order])[0]


def merge(sides, counts):
    ins = [x for side in sides for x in side]
    blocks, line = ins[0].shape[:2]
    tiles = (line // 128) * len(sides)
    extra_rows = -(-3 * tiles // 16) * 16
    return pl.pallas_call(
        functools.partial(merge_kernel, len(sides), len(sides[0])),
        out_shape=[jax.ShapeDtypeStruct((n, tiles * 128 + extra_rows, HD), BF) for n in counts],
        in_specs=[pl.BlockSpec(memory_space=pltpu.VMEM)] * len(ins),
        out_specs=[pl.BlockSpec(memory_space=pltpu.VMEM)] * len(counts),
        compiler_params=params(),
        cost_estimate=pl.CostEstimate(
            flops=blocks * tiles * 128 * 128 * 6,
            bytes_accessed=blocks * tiles * 128 * HD * 6,
            transcendentals=0,
        ),
        name="merge_step",
    )(*ins)


def last_kernel(*refs):
    parts, out_ref = refs[:4], refs[5]
    low = lax.broadcasted_iota(jnp.int32, (1, HD), 1) < 64
    datas, tops = merge_line(parts, 0)
    rolled = [pltpu.roll(jnp.broadcast_to(t, (8, HD)), 64, 1)[0:1] for t in tops]
    for h in range(8):
        k, side = h // 2, h % 2
        if side == 0:
            joined = jnp.where(low, tops[k], rolled[4 + k])
        else:
            joined = jnp.where(low, rolled[k], tops[4 + k])
        for m in range(2):
            piece = datas[4 * m + k][side * 64:(side + 1) * 64]
            out_ref[h, m * 64:(m + 1) * 64, :] = piece.astype(BF)
        out_ref[h, 128:LAST, :] = lse_rows([joined[None]])[0]


def merge_last(parts, after):
    return pl.pallas_call(
        last_kernel,
        out_shape=jax.ShapeDtypeStruct((8, LAST, HD), BF),
        in_specs=[pl.BlockSpec(memory_space=pltpu.VMEM)] * 4
        + [pl.BlockSpec(memory_space=pl.ANY)],
        out_specs=pl.BlockSpec(memory_space=pltpu.VMEM),
        compiler_params=params(),
        name="merge_last",
    )(*parts, after)


def suffix_kernel(first, len_ref, q_ref, kv_ref, new_ref, o_ref, lse_ref):
    per = q_ref.shape[0]
    positions = kv_ref.shape[1]
    step_id = lax.broadcasted_iota(jnp.int32, (ROWS, 1), 0) // GROUP
    pos = lax.broadcasted_iota(jnp.int32, (ROWS, positions), 1)
    ones = jnp.ones((positions, HD), BF)
    for e in range(per):
        used = len_ref[first + pl.program_id(0) * per + e]
        q = q_ref[e]
        qf = q.astype(F32)
        fresh = new_ref[e].astype(F32)
        s = lax.dot_general(
            q, kv_ref[e, :, :HD], (((1,), (1,)), ((), ())), preferred_element_type=F32
        )
        s = jnp.where(pos < used, s, NEG)
        top = jnp.max(s, axis=1, keepdims=True)
        extra = []
        for t in range(STEPS):
            f = jnp.sum(qf * fresh[t:t + 1, :HD], axis=1, keepdims=True)
            f = jnp.where(step_id >= t, f, NEG)
            extra.append(f)
            top = jnp.maximum(top, f)
        p = jnp.exp2((s - top) * (ROOT * LOG2E)).astype(BF)
        r = jnp.dot(
            p, jnp.concatenate([kv_ref[e, :, HD:], ones], axis=1), preferred_element_type=F32
        )
        num, den = r[:, :HD], r[:, HD:]
        for t in range(STEPS):
            w = jnp.exp2((extra[t] - top) * (ROOT * LOG2E))
            num = num + w * fresh[t:t + 1, HD:]
            den = den + w
        o_ref[e] = num / den
        lse_ref[e] = top * ROOT + jnp.log(den)


def suffix_attention(suffix_len, q_rows, suffix_kv, new_kv, first, count):
    positions = suffix_kv.shape[1]
    per = 4
    skip = first // per
    one = jax.ShapeDtypeStruct((count, ROWS, HD), F32)
    grid_spec = pltpu.PrefetchScalarGridSpec(
        num_scalar_prefetch=1,
        grid=(count // per,),
        in_specs=[
            pl.BlockSpec((per, ROWS, HD), lambda s, n: (s + skip, 0, 0)),
            pl.BlockSpec((per, positions, 2 * HD), lambda s, n: (s + skip, 0, 0)),
            pl.BlockSpec((per, STEPS, 2 * HD), lambda s, n: (s + skip, 0, 0)),
        ],
        out_specs=[pl.BlockSpec((per, ROWS, HD), lambda s, n: (s, 0, 0))] * 2,
    )
    return pl.pallas_call(
        functools.partial(suffix_kernel, first),
        out_shape=[one, one],
        grid_spec=grid_spec,
        compiler_params=params(),
        cost_estimate=pl.CostEstimate(
            flops=count * 256 * positions * 128 * 4,
            bytes_accessed=count << 19,
            transcendentals=count * ROWS * positions,
        ),
        name="suffix_attention",
    )(suffix_len, q_rows, suffix_kv, new_kv)


def final_kernel(
    own_ref, off_ref, oa_ref, la_ref, ob_ref, lb_ref, part_ref, out_ref, data_ref, top_ref, wide_ref
):
    for t in range(8):
        data_ref[t] = part_ref[t, 0:128, :].astype(F32)
        rows = part_ref[t, 128:LAST, :].astype(F32)
        top_ref[t] = spread(read_lse(rows, 0))
    each = oa_ref.shape[0]
    for r in range(2 * each):
        o_ref, l_ref = (oa_ref, la_ref) if r < each else (ob_ref, lb_ref)
        at = pl.ds(pl.multiple_of(off_ref[r], ROWS), ROWS)
        op, lp = data_ref[own_ref[r], at, :], top_ref[own_ref[r], at, :]
        w, _ = blend_weights(lp, l_ref[r % each])
        ol = o_ref[r % each]
        wide_ref[r] = ol + w * (op - ol)
    for g in range(GROUP):
        out_ref[:, :, g * HD:(g + 1) * HD] = wide_ref[:, pl.ds(g, STEPS, GROUP), :].astype(BF)


def finish(own, off, local, parts):
    count = own.shape[0]
    return pl.pallas_call(
        final_kernel,
        out_shape=jax.ShapeDtypeStruct((count, STEPS, GROUP * HD), BF),
        in_specs=[pl.BlockSpec(memory_space=pltpu.SMEM)] * 2
        + [pl.BlockSpec(memory_space=pltpu.VMEM)] * 5,
        out_specs=pl.BlockSpec(memory_space=pltpu.VMEM),
        scratch_shapes=[
            pltpu.VMEM((8, HD, HD), F32),
            pltpu.VMEM((8, HD, HD), F32),
            pltpu.VMEM((count, ROWS, HD), F32),
        ],
        compiler_params=params(),
        name="finish",
    )(own, off, *local, parts)


def on_device(prefix_kv, prefix_len, prefix_of, suffix_len, suffix_kv, queries, new_kv):
    mine, block = lax.axis_index("pre"), lax.axis_index("req")
    shard = prefix_kv.shape[1]
    count = queries.shape[0]

    owners = prefix_of[:, 0]
    ids = jnp.arange(count, dtype=jnp.int32)
    earlier = (owners[None, :] == owners[:, None]) & (ids[None, :] < ids[:, None])
    rank = jnp.sum(earlier.astype(jnp.int32), axis=1)
    part = (owners & 1) * 2 + rank
    own_len = lax.dynamic_slice_in_dim(prefix_len, mine * 2, 2, 0)
    usable = jnp.clip(own_len - block * shard, 0, shard)

    q_rows, packed = pack(owners, queries)
    heads = lax.all_to_all(packed, "pre", 0, 0, tiled=True)
    local = []
    for first in (0, count // 2):
        local += suffix_attention(suffix_len, q_rows, suffix_kv, new_kv, first, count // 2)

    near = join([heads[None]] + three_ways([heads[None]] * 3, 0), cuts=2, after=local[0])
    got = [three_ways([near[a]] * 3, 2) for a in range(2)]
    attend = functools.partial(prefix_attention, usable, prefix_kv)
    own0 = attend([near[0]], 0)
    mid0 = attend(got[0][:2], 0, own0[0])
    mid1 = attend(got[1][:2], 4, mid0[0])
    far0 = attend(got[0][2:], 0, mid1[0])
    far1 = attend(got[1][2:], 4, far0[0])
    own1 = attend([near[1]], 4, far1[0])
    back = [three_ways(mid0 + far0, 2), three_ways(mid1 + far1, 2)]
    most = [merge([[own[0], back[a][0], back[a][1]]], [4])[0] for a, own in enumerate((own0, own1))]
    parts = merge([[most[a], back[a][2]] for a in range(2)], [1] * 4)
    final = merge_last([parts[0]] + three_ways(parts[1:], 0), local[2])
    back = lax.all_to_all(final, "pre", 0, 0, tiled=True)
    return finish(owners >> 1, part * ROWS, local, back)


def solution(mesh):
    placed = (
        P("pre", "req", None),
        P(),
        P("req", None),
        P("req"),
        P("req", None, "pre"),
        P("req", None, "pre"),
        P("req", None, "pre"),
    )
    return jax.shard_map(
        on_device, mesh=mesh, in_specs=placed, out_specs=P("req", None, "pre"), check_vma=False
    )
```

```python
import functools
import math

import jax
import jax.numpy as jnp
from jax import lax
from jax.experimental import pallas as pl
from jax.experimental.pallas import tpu as pltpu
from jax.sharding import PartitionSpec as P

HD = 128
GROUP = 8
STEPS = 4
ROWS = STEPS * GROUP
NEG = -1e30
ROOT = 1.0 / math.sqrt(HD)
LOG2E = math.log2(math.e)
EMPTY = 128.0
LAST = 144
BF = jnp.bfloat16
F32 = jnp.float32


def params(mb=48):
    return pltpu.CompilerParams(vmem_limit_bytes=mb * 1024 * 1024)


FLIPS = (1, 4, 3, 12)


def req_step(x, turns):
    pairs = []
    for i in range(8):
        flip = 0
        for turn in turns:
            flip ^= FLIPS[(2 * (i & 1) + turn) % 4]
        pairs += [(i * 16 + j, i * 16 + (j ^ flip)) for j in range(16)]
    return lax.ppermute(x, ("pre", "req"), pairs)


def three_ways(xs, first):
    ways = ([first], [first + 1], [first, first + 1])
    return [req_step(x, way) for x, way in zip(xs, ways)]


def split3(x):
    hi = x.astype(BF).astype(F32)
    mid = (x - hi).astype(BF).astype(F32)
    low = (x - hi - mid).astype(BF).astype(F32)
    return hi, mid, low


def pack_kernel(of_ref, q_ref, rows_ref, out_ref, wide_ref, seen_ref, req_ref):
    count = q_ref.shape[0]
    for p in range(16):
        seen_ref[p] = 0
    for slot in range(32):
        req_ref[slot] = -1
    for r in range(count):
        p = of_ref[r]
        rank = seen_ref[p]
        seen_ref[p] = rank + 1
        req_ref[p * 2 + rank] = r
    for g in range(GROUP):
        wide_ref[:, pl.ds(g, STEPS, GROUP), :] = q_ref[:, :, g * HD:(g + 1) * HD].astype(F32)
    rows_ref[...] = wide_ref[...].astype(BF)
    nobody = jnp.full((ROWS, HD), EMPTY, BF)
    for slot in range(32):
        r = req_ref[slot]
        rows = rows_ref[jnp.maximum(r, 0)]
        at = (slot % 4) * ROWS
        out_ref[slot // 4, at:at + ROWS, :] = jnp.where(r >= 0, rows, nobody)


def pack(owners, queries):
    count = queries.shape[0]
    return pl.pallas_call(
        pack_kernel,
        out_shape=[
            jax.ShapeDtypeStruct((count, ROWS, HD), BF),
            jax.ShapeDtypeStruct((8, 128, HD), BF),
        ],
        in_specs=[pl.BlockSpec(memory_space=pltpu.SMEM), pl.BlockSpec(memory_space=pltpu.VMEM)],
        out_specs=[pl.BlockSpec(memory_space=pltpu.VMEM)] * 2,
        scratch_shapes=[
            pltpu.VMEM((count, ROWS, HD), F32),
            pltpu.SMEM((16,), jnp.int32),
            pltpu.SMEM((32,), jnp.int32),
        ],
        compiler_params=params(),
        name="pack_slots",
    )(owners, queries)


def join_kernel(groups, cuts, total, *refs):
    out_refs = refs[-groups * cuts:]
    ins = refs[:total]
    count = total // groups
    each = ins[0].shape[0]
    width = ins[0].shape[1] // cuts
    for g in range(groups):
        for c in range(cuts):
            for n in range(count):
                piece = ins[g * count + n][:, c * width:(c + 1) * width]
                out_refs[g * cuts + c][n * each:(n + 1) * each] = piece


def join(parts, groups=1, cuts=1, after=None):
    extra = [] if after is None else [after]
    first = parts[0].shape
    shape = (len(parts) // groups * first[0], first[1] // cuts) + first[2:]
    return pl.pallas_call(
        functools.partial(join_kernel, groups, cuts, len(parts)),
        out_shape=[jax.ShapeDtypeStruct(shape, BF)] * (groups * cuts),
        in_specs=[pl.BlockSpec(memory_space=pltpu.VMEM)] * len(parts)
        + [pl.BlockSpec(memory_space=pl.ANY)] * len(extra),
        out_specs=[pl.BlockSpec(memory_space=pltpu.VMEM)] * (groups * cuts),
        compiler_params=params(),
        name="join",
    )(*parts, *extra)


def prefix_kernel(count, first, extra, cuts, base, use_ref, *rest):
    q_refs, kv_hbm = rest[:count], rest[count]
    rest = rest[count + 1 + extra:]
    out_refs = rest[:count * cuts]
    kv_all, sa_ref, sb_ref, bias_ref, lse_ref, group_ref, many_ref, sems = rest[
        count * cuts:
    ]
    each, heads = q_refs[0].shape[0], 4
    positions = kv_all.shape[1]
    blocks = each * count
    rows = blocks * ROWS
    part_len = each // cuts

    def fetch(m, h):
        at = (first + h) * (2 * HD)
        return pltpu.make_async_copy(
            kv_hbm.at[m, :, pl.ds(at, 2 * HD)], kv_all.at[m * heads + h], sems.at[m * heads + h]
        )

    marks = [
        jnp.min(
            functools.reduce(
                jnp.minimum, [r[:, base, w * ROWS:w * ROWS + 16, :].astype(F32) for r in q_refs]
            )
        )
        < 100.0
        for w in range(4)
    ]
    live = [(use_ref[w // 2] > 0) & marks[w] for w in range(4)]

    many_ref[0] = 0
    for m in range(2):
        for rank in range(2):
            on = live[m * 2 + rank]

            @pl.when(on)
            def _():
                n = many_ref[0]
                group_ref[n] = m * 2 + rank
                if rank == 0:
                    for h in range(heads):
                        fetch(m, h).start()
                many_ref[0] = n + 1

            @pl.when(jnp.logical_not(on))
            def _():
                for h in range(heads):
                    at = m * 256 + h * 64 + rank * ROWS
                    for out_ref in out_refs:
                        out_ref[:, at:at + ROWS, :] = jnp.zeros((part_len, ROWS, HD), BF)

    for m in range(2):
        pos = lax.broadcasted_iota(jnp.int32, (8, positions), 1)
        bias_ref[m] = jnp.where(pos < use_ref[m], 0.0, NEG)
    lse_ref[...] = jnp.full(lse_ref.shape, NEG, F32)
    n = many_ref[0]

    def decode(i):
        which = group_ref[jnp.minimum(i, n - 1)]
        return which, which >> 1, which & 1

    def arrive(i, hs):
        which, m, rank = decode(i)

        @pl.when((rank == 0) & (i < n))
        def _():
            for h in hs:
                fetch(m, h).wait()

    def score(i, h, s_ref):
        which, m, rank = decode(i)
        at = pl.ds(pl.multiple_of(which * ROWS, ROWS), ROWS)
        q = [r[:, base + h, at, :].reshape(each * ROWS, HD) for r in q_refs]
        q = q[0] if count == 1 else jnp.concatenate(q, axis=0)
        k = kv_all[m * heads + h, :, :HD]
        s = lax.dot_general(q, k, (((1,), (1,)), ((), ())), preferred_element_type=F32)
        s = s.reshape(rows // 8, 8, positions) + bias_ref[m][None]
        s_ref[...] = s.reshape(rows, positions)

    def weigh(i, h, s_ref):
        which, m, rank = decode(i)
        tile, side = m * 2 + h // 2, h % 2
        s = s_ref[...]
        top = jnp.max(s, axis=1, keepdims=True)
        p = jnp.exp2((s - top) * (ROOT * LOG2E)).astype(BF)
        v = kv_all[m * heads + h, :, HD:]
        v1 = jnp.concatenate([v, jnp.ones((positions, HD), BF)], axis=1)
        r = jnp.dot(p, v1, preferred_element_type=F32)
        den = r[:, HD:]
        o = r[:, :HD] / den
        lse = top * ROOT + jnp.log(den)
        at = pl.multiple_of(m * 256 + h * 64 + rank * ROWS, ROWS)
        o = o.reshape(blocks, ROWS, HD).astype(BF)
        for c, out_ref in enumerate(out_refs):
            out_ref[:, pl.ds(at, ROWS), :] = o[c * part_len:(c + 1) * part_len]
        part = side * 2 + rank
        row_id = lax.broadcasted_iota(jnp.int32, (ROWS, HD), 0)
        lane_id = lax.broadcasted_iota(jnp.int32, (ROWS, HD), 1)
        diag = (lane_id - row_id == part * ROWS)[None]
        flat = jnp.sum(jnp.where(diag, lse.reshape(blocks, ROWS, HD), 0.0), axis=1)
        lanes = lax.broadcasted_iota(jnp.int32, (blocks, HD), 1) >> 5
        lse_ref[tile] = jnp.where(lanes == part, flat, lse_ref[tile])

    @pl.when(n > 0)
    def _():
        arrive(0, [0])
        score(0, 0, sa_ref)

        def body(j, carry):
            arrive(j, range(1, heads))
            arrive(j + 1, [0])
            for h in range(heads):
                now, later = (sa_ref, sb_ref) if h % 2 == 0 else (sb_ref, sa_ref)
                if h + 1 < heads:
                    score(j, h + 1, later)
                else:
                    score(j + 1, 0, later)
                weigh(j, h, now)
            return carry

        lax.fori_loop(0, n, body, 0)

    for c, out_ref in enumerate(out_refs):
        tops = [lse_ref[t, c * part_len:(c + 1) * part_len, :][:, None, :] for t in range(4)]
        out_ref[:, 512:, :] = lse_rows(tops)


def lse_rows(tops):
    shape = (tops[0].shape[0], -(-3 * len(tops) // 16) * 16, HD)
    row = lax.broadcasted_iota(jnp.int32, shape, 1)
    out = jnp.zeros(shape, F32)
    at = 0
    for top in tops:
        for piece in split3(top):
            out = jnp.where(row == at, jnp.broadcast_to(piece, shape), out)
            at += 1
    return out.astype(BF)


def prefix_attention(usable, prefix_kv, qs, first, after=None, cuts=1):
    count = len(qs)
    extra = [] if after is None else [after]
    each, heads = qs[0].shape[0], 4
    base = first % qs[0].shape[1]
    blocks = each * count
    positions = prefix_kv.shape[1]
    rows = blocks * ROWS
    work = rows * positions * heads * 3
    return pl.pallas_call(
        functools.partial(prefix_kernel, count, first, len(extra), cuts, base),
        out_shape=[jax.ShapeDtypeStruct((each // cuts, 528, HD), BF)] * (count * cuts),
        in_specs=[pl.BlockSpec(memory_space=pltpu.SMEM)]
        + [pl.BlockSpec(memory_space=pltpu.VMEM)] * count
        + [pl.BlockSpec(memory_space=pl.ANY)] * (1 + len(extra)),
        out_specs=[pl.BlockSpec(memory_space=pltpu.VMEM)] * (count * cuts),
        scratch_shapes=[
            pltpu.VMEM((2 * heads, positions, 2 * HD), BF),
            pltpu.VMEM((rows, positions), F32),
            pltpu.VMEM((rows, positions), F32),
            pltpu.VMEM((2, 8, positions), F32),
            pltpu.VMEM((4, blocks, HD), F32),
            pltpu.SMEM((4,), jnp.int32),
            pltpu.SMEM((1,), jnp.int32),
            pltpu.SemaphoreType.DMA((2 * heads,)),
        ],
        compiler_params=params(),
        cost_estimate=pl.CostEstimate(
            flops=work * 512, bytes_accessed=heads << 20, transcendentals=work
        ),
        name="prefix_attention",
    )(usable, *qs, prefix_kv, *extra)


def blend_weights(la, lb):
    top = jnp.maximum(la, lb)
    ea, eb = jnp.exp(la - top), jnp.exp(lb - top)
    total = ea + eb
    return ea / total, top + jnp.log(total)


def spread(w):
    return jnp.broadcast_to(w, (HD, HD)).T


def read_lse(rows, m):
    return rows[3 * m:3 * m + 1] + rows[3 * m + 1:3 * m + 2] + rows[3 * m + 2:3 * m + 3]


def merge_line(ways, spot):
    tiles = ways[0][0].shape[1] // 128
    at = [(way[spot // way[0].shape[0]], spot % way[0].shape[0]) for way in ways]
    rows = [r[i, tiles * 128:, :].astype(F32) for r, i in at]
    datas, tops = [], []
    for t in range(tiles):
        lses = [read_lse(r, t) for r in rows]
        top = functools.reduce(jnp.maximum, lses)
        es = [jnp.exp(x - top) for x in lses]
        total = functools.reduce(jnp.add, es)
        blocks = [r[i, t * 128:(t + 1) * 128, :].astype(F32) for r, i in at]
        data = blocks[-1]
        for e, o in zip(es[:-1], blocks[:-1]):
            data = data + spread(e / total) * (o - blocks[-1])
        datas.append(data)
        tops.append(top + jnp.log(total))
    return datas, tops


def merge_kernel(shape, *refs):
    refs = list(refs)
    ins = [[[refs.pop(0) for _ in range(n)] for n in side] for side in shape]
    out_refs = refs
    sides = len(shape)
    outs = [(ref, b) for ref in out_refs for b in range(ref.shape[0])]
    for spot, (out_ref, b) in reversed(list(enumerate(outs))):
        merged = [merge_line(side, spot) for side in ins]
        tiles = len(merged[0][0])
        order = [(c, m * 2 + k) for m in range(tiles // 2) for c in range(sides) for k in range(2)]
        for n, (c, t) in enumerate(order):
            out_ref[b, n * 128:(n + 1) * 128, :] = merged[c][0][t].astype(BF)
        out_ref[b, len(order) * 128:, :] = lse_rows([merged[c][1][t][None] for c, t in order])[0]


def merge(sides, counts):
    ins = [x for side in sides for way in side for x in way]
    shape = [[len(way) for way in side] for side in sides]
    blocks, line = sum(counts), ins[0].shape[1]
    tiles = (line // 128) * len(sides)
    extra_rows = -(-3 * tiles // 16) * 16
    return pl.pallas_call(
        functools.partial(merge_kernel, shape),
        out_shape=[jax.ShapeDtypeStruct((n, tiles * 128 + extra_rows, HD), BF) for n in counts],
        in_specs=[pl.BlockSpec(memory_space=pltpu.VMEM)] * len(ins),
        out_specs=[pl.BlockSpec(memory_space=pltpu.VMEM)] * len(counts),
        compiler_params=params(),
        cost_estimate=pl.CostEstimate(
            flops=blocks * tiles * 128 * 128 * 6,
            bytes_accessed=blocks * tiles * 128 * HD * 6,
            transcendentals=0,
        ),
        name="merge_step",
    )(*ins)


def last_kernel(*refs):
    parts, out_ref = refs[:4], refs[5]
    low = lax.broadcasted_iota(jnp.int32, (1, HD), 1) < 64
    datas, tops = merge_line([[p] for p in parts], 0)
    rolled = [pltpu.roll(jnp.broadcast_to(t, (8, HD)), 64, 1)[0:1] for t in tops]
    for h in range(8):
        k, side = h // 2, h % 2
        if side == 0:
            joined = jnp.where(low, tops[k], rolled[4 + k])
        else:
            joined = jnp.where(low, rolled[k], tops[4 + k])
        for m in range(2):
            piece = datas[4 * m + k][side * 64:(side + 1) * 64]
            out_ref[h, m * 64:(m + 1) * 64, :] = piece.astype(BF)
        out_ref[h, 128:LAST, :] = lse_rows([joined[None]])[0]


def merge_last(parts, after):
    return pl.pallas_call(
        last_kernel,
        out_shape=jax.ShapeDtypeStruct((8, LAST, HD), BF),
        in_specs=[pl.BlockSpec(memory_space=pltpu.VMEM)] * 4
        + [pl.BlockSpec(memory_space=pl.ANY)],
        out_specs=pl.BlockSpec(memory_space=pltpu.VMEM),
        compiler_params=params(),
        name="merge_last",
    )(*parts, after)


def suffix_kernel(first, len_ref, q_ref, kv_ref, new_ref, o_ref, lse_ref):
    per = q_ref.shape[0]
    positions = kv_ref.shape[1]
    step_id = lax.broadcasted_iota(jnp.int32, (ROWS, 1), 0) // GROUP
    pos = lax.broadcasted_iota(jnp.int32, (ROWS, positions), 1)
    ones = jnp.ones((positions, HD), BF)
    for e in range(per):
        used = len_ref[first + pl.program_id(0) * per + e]
        q = q_ref[e]
        qf = q.astype(F32)
        fresh = new_ref[e].astype(F32)
        s = lax.dot_general(
            q, kv_ref[e, :, :HD], (((1,), (1,)), ((), ())), preferred_element_type=F32
        )
        s = jnp.where(pos < used, s, NEG)
        top = jnp.max(s, axis=1, keepdims=True)
        extra = []
        for t in range(STEPS):
            f = jnp.sum(qf * fresh[t:t + 1, :HD], axis=1, keepdims=True)
            f = jnp.where(step_id >= t, f, NEG)
            extra.append(f)
            top = jnp.maximum(top, f)
        p = jnp.exp2((s - top) * (ROOT * LOG2E)).astype(BF)
        r = jnp.dot(
            p, jnp.concatenate([kv_ref[e, :, HD:], ones], axis=1), preferred_element_type=F32
        )
        num, den = r[:, :HD], r[:, HD:]
        for t in range(STEPS):
            w = jnp.exp2((extra[t] - top) * (ROOT * LOG2E))
            num = num + w * fresh[t:t + 1, HD:]
            den = den + w
        o_ref[e] = num / den
        lse_ref[e] = top * ROOT + jnp.log(den)


def suffix_attention(suffix_len, q_rows, suffix_kv, new_kv, first, count):
    positions = suffix_kv.shape[1]
    per = 4
    skip = first // per
    one = jax.ShapeDtypeStruct((count, ROWS, HD), F32)
    grid_spec = pltpu.PrefetchScalarGridSpec(
        num_scalar_prefetch=1,
        grid=(count // per,),
        in_specs=[
            pl.BlockSpec((per, ROWS, HD), lambda s, n: (s + skip, 0, 0)),
            pl.BlockSpec((per, positions, 2 * HD), lambda s, n: (s + skip, 0, 0)),
            pl.BlockSpec((per, STEPS, 2 * HD), lambda s, n: (s + skip, 0, 0)),
        ],
        out_specs=[pl.BlockSpec((per, ROWS, HD), lambda s, n: (s, 0, 0))] * 2,
    )
    return pl.pallas_call(
        functools.partial(suffix_kernel, first),
        out_shape=[one, one],
        grid_spec=grid_spec,
        compiler_params=params(),
        cost_estimate=pl.CostEstimate(
            flops=count * 256 * positions * 128 * 4,
            bytes_accessed=count << 19,
            transcendentals=count * ROWS * positions,
        ),
        name="suffix_attention",
    )(suffix_len, q_rows, suffix_kv, new_kv)


def final_kernel(
    own_ref, off_ref, oa_ref, la_ref, ob_ref, lb_ref, part_ref, out_ref, data_ref, top_ref, wide_ref
):
    for t in range(8):
        data_ref[t] = part_ref[t, 0:128, :].astype(F32)
        rows = part_ref[t, 128:LAST, :].astype(F32)
        top_ref[t] = spread(read_lse(rows, 0))
    each = oa_ref.shape[0]
    for r in range(2 * each):
        o_ref, l_ref = (oa_ref, la_ref) if r < each else (ob_ref, lb_ref)
        at = pl.ds(pl.multiple_of(off_ref[r], ROWS), ROWS)
        op, lp = data_ref[own_ref[r], at, :], top_ref[own_ref[r], at, :]
        w, _ = blend_weights(lp, l_ref[r % each])
        ol = o_ref[r % each]
        wide_ref[r] = ol + w * (op - ol)
    for g in range(GROUP):
        out_ref[:, :, g * HD:(g + 1) * HD] = wide_ref[:, pl.ds(g, STEPS, GROUP), :].astype(BF)


def finish(own, off, local, parts):
    count = own.shape[0]
    return pl.pallas_call(
        final_kernel,
        out_shape=jax.ShapeDtypeStruct((count, STEPS, GROUP * HD), BF),
        in_specs=[pl.BlockSpec(memory_space=pltpu.SMEM)] * 2
        + [pl.BlockSpec(memory_space=pltpu.VMEM)] * 5,
        out_specs=pl.BlockSpec(memory_space=pltpu.VMEM),
        scratch_shapes=[
            pltpu.VMEM((8, HD, HD), F32),
            pltpu.VMEM((8, HD, HD), F32),
            pltpu.VMEM((count, ROWS, HD), F32),
        ],
        compiler_params=params(),
        name="finish",
    )(own, off, *local, parts)


def on_device(prefix_kv, prefix_len, prefix_of, suffix_len, suffix_kv, queries, new_kv):
    mine, block = lax.axis_index("pre"), lax.axis_index("req")
    shard = prefix_kv.shape[1]
    count = queries.shape[0]

    owners = prefix_of[:, 0]
    ids = jnp.arange(count, dtype=jnp.int32)
    earlier = (owners[None, :] == owners[:, None]) & (ids[None, :] < ids[:, None])
    rank = jnp.sum(earlier.astype(jnp.int32), axis=1)
    part = (owners & 1) * 2 + rank
    own_len = lax.dynamic_slice_in_dim(prefix_len, mine * 2, 2, 0)
    usable = jnp.clip(own_len - block * shard, 0, shard)

    q_rows, packed = pack(owners, queries)
    heads = lax.all_to_all(packed, "pre", 0, 0, tiled=True)
    local = []
    for first in (0, count // 2):
        local += suffix_attention(suffix_len, q_rows, suffix_kv, new_kv, first, count // 2)

    near = [heads[None]] + three_ways([heads[None]] * 3, 0)
    whole, halves = join(near, after=local[0])[0], join(near, cuts=2, after=local[0])
    attend = functools.partial(prefix_attention, usable, prefix_kv)
    side, other, cross = [2], [3], [2, 3]
    mid = [req_step(whole, way) for way in (side, other)]
    far = [req_step(half, cross) for half in halves]
    own0 = attend([halves[0]], 0)
    own1 = attend([halves[1]], 4, own0[0])
    far0 = attend([far[0]], 0, own1[0])
    far1 = attend([far[1]], 4, far0[0])
    mid0 = attend(mid, 0, far1[0])
    mid1 = attend(mid, 4, mid0[0], 2)
    back_far = [req_step(x[0], cross) for x in (far0, far1)]
    back0 = [[req_step(mid0[n], way)] for n, way in enumerate((side, other))]
    back1 = [
        [req_step(x, way) for x in mid1[2 * n:2 * n + 2]] for n, way in enumerate((side, other))
    ]
    most0 = merge([[own0, [back_far[0]]] + back0], [4])
    most1 = merge([[own1, [back_far[1]]]], [4])
    parts = merge([[most0], [most1] + back1], [1] * 4)
    final = merge_last([parts[0]] + three_ways(parts[1:], 0), local[2])
    back = lax.all_to_all(final, "pre", 0, 0, tiled=True)
    return finish(owners >> 1, part * ROWS, local, back)


def solution(mesh):
    placed = (
        P("pre", "req", None),
        P(),
        P("req", None),
        P("req"),
        P("req", None, "pre"),
        P("req", None, "pre"),
        P("req", None, "pre"),
    )
    return jax.shard_map(
        on_device, mesh=mesh, in_specs=placed, out_specs=P("req", None, "pre"), check_vma=False
    )
```

```python
import functools
import math

import jax
import jax.numpy as jnp
from jax import lax
from jax.experimental import pallas as pl
from jax.experimental.pallas import tpu as pltpu
from jax.sharding import PartitionSpec as P

HD = 128
GROUP = 8
STEPS = 4
ROWS = STEPS * GROUP
NEG = -1e30
ROOT = 1.0 / math.sqrt(HD)
LOG2E = math.log2(math.e)
EMPTY = 128.0
LAST = 144
BF = jnp.bfloat16
F32 = jnp.float32


def params(mb=48):
    return pltpu.CompilerParams(vmem_limit_bytes=mb * 1024 * 1024)


FLIPS = (1, 4, 3, 12)


def req_step(x, turns):
    pairs = []
    for i in range(8):
        flip = 0
        for turn in turns:
            flip ^= FLIPS[(2 * (i & 1) + turn) % 4]
        pairs += [(i * 16 + j, i * 16 + (j ^ flip)) for j in range(16)]
    return lax.ppermute(x, ("pre", "req"), pairs)


def quarter_step(x, k, turn):
    return req_step(x, [turn if k < 2 else 5 - turn])


def three_ways(xs):
    return [req_step(x, way) for x, way in zip(xs, ([0], [1], [0, 1]))]


def split3(x):
    hi = x.astype(BF).astype(F32)
    mid = (x - hi).astype(BF).astype(F32)
    low = (x - hi - mid).astype(BF).astype(F32)
    return hi, mid, low


def pack_kernel(of_ref, q_ref, rows_ref, out_ref, wide_ref, seen_ref, req_ref):
    count = q_ref.shape[0]
    for p in range(16):
        seen_ref[p] = 0
    for slot in range(32):
        req_ref[slot] = -1
    for r in range(count):
        p = of_ref[r]
        rank = seen_ref[p]
        seen_ref[p] = rank + 1
        req_ref[p * 2 + rank] = r
    for g in range(GROUP):
        wide_ref[:, pl.ds(g, STEPS, GROUP), :] = q_ref[:, :, g * HD:(g + 1) * HD].astype(F32)
    rows_ref[...] = wide_ref[...].astype(BF)
    nobody = jnp.full((ROWS, HD), EMPTY, BF)
    for slot in range(32):
        r = req_ref[slot]
        rows = rows_ref[jnp.maximum(r, 0)]
        at = (slot % 4) * ROWS
        out_ref[slot // 4, at:at + ROWS, :] = jnp.where(r >= 0, rows, nobody)


def pack(owners, queries):
    count = queries.shape[0]
    return pl.pallas_call(
        pack_kernel,
        out_shape=[
            jax.ShapeDtypeStruct((count, ROWS, HD), BF),
            jax.ShapeDtypeStruct((8, 128, HD), BF),
        ],
        in_specs=[pl.BlockSpec(memory_space=pltpu.SMEM), pl.BlockSpec(memory_space=pltpu.VMEM)],
        out_specs=[pl.BlockSpec(memory_space=pltpu.VMEM)] * 2,
        scratch_shapes=[
            pltpu.VMEM((count, ROWS, HD), F32),
            pltpu.SMEM((16,), jnp.int32),
            pltpu.SMEM((32,), jnp.int32),
        ],
        compiler_params=params(),
        name="pack_slots",
    )(owners, queries)


def join_kernel(groups, cuts, total, *refs):
    out_refs = refs[-groups * cuts:]
    ins = refs[:total]
    count = total // groups
    each = ins[0].shape[0]
    width = ins[0].shape[1] // cuts
    for g in range(groups):
        for c in range(cuts):
            for n in range(count):
                piece = ins[g * count + n][:, c * width:(c + 1) * width]
                out_refs[g * cuts + c][n * each:(n + 1) * each] = piece


def join(parts, groups=1, cuts=1, after=None):
    extra = [] if after is None else [after]
    first = parts[0].shape
    shape = (len(parts) // groups * first[0], first[1] // cuts) + first[2:]
    return pl.pallas_call(
        functools.partial(join_kernel, groups, cuts, len(parts)),
        out_shape=[jax.ShapeDtypeStruct(shape, BF)] * (groups * cuts),
        in_specs=[pl.BlockSpec(memory_space=pltpu.VMEM)] * len(parts)
        + [pl.BlockSpec(memory_space=pl.ANY)] * len(extra),
        out_specs=[pl.BlockSpec(memory_space=pltpu.VMEM)] * (groups * cuts),
        compiler_params=params(),
        name="join",
    )(*parts, *extra)


def prefix_kernel(first, extra, use_ref, *rest):
    count = 2
    q_refs, kv_hbm = rest[:count], rest[count]
    rest = rest[count + 1 + extra:]
    out_refs = rest[:-8]
    kv_all, sa_ref, sb_ref, bias_ref, lse_ref, group_ref, many_ref, sems = rest[-8:]
    heads = 2 * count
    positions = kv_all.shape[1]
    blocks = q_refs[0].shape[0]
    rows = blocks * ROWS

    def fetch(m, h):
        at = (first + h) * (2 * HD)
        return pltpu.make_async_copy(
            kv_hbm.at[m, :, pl.ds(at, 2 * HD)], kv_all.at[m * heads + h], sems.at[m * heads + h]
        )

    marks = [
        jnp.min(q_refs[0][:, 0, w * ROWS:w * ROWS + 16, :].astype(F32)) < 100.0 for w in range(4)
    ]
    live = [(use_ref[w // 2] > 0) & marks[w] for w in range(4)]

    many_ref[0] = 0
    for m in range(2):
        for rank in range(2):
            on = live[m * 2 + rank]

            @pl.when(on)
            def _():
                n = many_ref[0]
                group_ref[n] = m * 2 + rank
                if rank == 0:
                    for h in range(heads):
                        fetch(m, h).start()
                many_ref[0] = n + 1

            @pl.when(jnp.logical_not(on))
            def _():
                for h in range(heads):
                    for ref in out_refs:
                        at = m * 256 + h * 64 + rank * ROWS
                        ref[:, at:at + ROWS, :] = jnp.zeros((ref.shape[0], ROWS, HD), BF)

    for m in range(2):
        pos = lax.broadcasted_iota(jnp.int32, (8, positions), 1)
        bias_ref[m] = jnp.where(pos < use_ref[m], 0.0, NEG)
    lse_ref[...] = jnp.full(lse_ref.shape, NEG, F32)
    n = many_ref[0]

    def decode(i):
        which = group_ref[jnp.minimum(i, n - 1)]
        return which, which >> 1, which & 1

    def arrive(i, hs):
        which, m, rank = decode(i)

        @pl.when((rank == 0) & (i < n))
        def _():
            for h in hs:
                fetch(m, h).wait()

    def score(i, h, s_ref):
        which, m, rank = decode(i)
        at = pl.ds(pl.multiple_of(which * ROWS, ROWS), ROWS)
        q = q_refs[h // 2][:, h % 2, at, :].reshape(rows, HD)
        k = kv_all[m * heads + h, :, :HD]
        s = lax.dot_general(q, k, (((1,), (1,)), ((), ())), preferred_element_type=F32)
        s = s.reshape(rows // 8, 8, positions) + bias_ref[m][None]
        s_ref[...] = s.reshape(rows, positions)

    def weigh(i, h, s_ref):
        which, m, rank = decode(i)
        c, side = h // 2, h % 2
        s = s_ref[...]
        top = jnp.max(s, axis=1, keepdims=True)
        p = jnp.exp2((s - top) * (ROOT * LOG2E)).astype(BF)
        v = kv_all[m * heads + h, :, HD:]
        v1 = jnp.concatenate([v, jnp.ones((positions, HD), BF)], axis=1)
        r = jnp.dot(p, v1, preferred_element_type=F32)
        den = r[:, HD:]
        o = r[:, :HD] / den
        lse = top * ROOT + jnp.log(den)
        at = pl.multiple_of(m * 256 + h * 64 + rank * ROWS, ROWS)
        o = o.reshape(blocks, ROWS, HD).astype(BF)
        spot = 0
        for ref in out_refs:
            ref[:, pl.ds(at, ROWS), :] = o[spot:spot + ref.shape[0]]
            spot += ref.shape[0]
        part = side * 2 + rank
        row_id = lax.broadcasted_iota(jnp.int32, (ROWS, HD), 0)
        lane_id = lax.broadcasted_iota(jnp.int32, (ROWS, HD), 1)
        diag = (lane_id - row_id == part * ROWS)[None]
        flat = jnp.sum(jnp.where(diag, lse.reshape(blocks, ROWS, HD), 0.0), axis=1)
        lanes = lax.broadcasted_iota(jnp.int32, (blocks, HD), 1) >> 5
        old = lse_ref[c * 2 + m]
        lse_ref[c * 2 + m] = jnp.where(lanes == part, flat, old)

    @pl.when(n > 0)
    def _():
        arrive(0, [0])
        score(0, 0, sa_ref)

        def body(j, carry):
            arrive(j, range(1, heads))
            arrive(j + 1, [0])
            for h in range(heads):
                now, later = (sa_ref, sb_ref) if h % 2 == 0 else (sb_ref, sa_ref)
                if h + 1 < heads:
                    score(j, h + 1, later)
                else:
                    score(j + 1, 0, later)
                weigh(j, h, now)
            return carry

        lax.fori_loop(0, n, body, 0)

    spot = 0
    for ref in out_refs:
        span = slice(spot, spot + ref.shape[0])
        tops = [lse_ref[2 * c + m, span, :][:, None, :] for m in range(2) for c in range(2)]
        ref[:, 512:, :] = lse_rows(tops)
        spot += ref.shape[0]


def lse_rows(tops):
    shape = (tops[0].shape[0], -(-3 * len(tops) // 16) * 16, HD)
    row = lax.broadcasted_iota(jnp.int32, shape, 1)
    out = jnp.zeros(shape, F32)
    at = 0
    for top in tops:
        for piece in split3(top):
            out = jnp.where(row == at, jnp.broadcast_to(piece, shape), out)
            at += 1
    return out.astype(BF)


def prefix_attention(usable, prefix_kv, qs, first, after=None, cuts=(4, 4)):
    count = len(qs)
    extra = [] if after is None else [after]
    heads = 2 * count
    blocks = qs[0].shape[0]
    positions = prefix_kv.shape[1]
    rows = blocks * ROWS
    work = rows * positions * heads * 3
    return pl.pallas_call(
        functools.partial(prefix_kernel, first, len(extra)),
        out_shape=[jax.ShapeDtypeStruct((n, 528, HD), BF) for n in cuts],
        in_specs=[pl.BlockSpec(memory_space=pltpu.SMEM)]
        + [pl.BlockSpec(memory_space=pltpu.VMEM)] * count
        + [pl.BlockSpec(memory_space=pl.ANY)] * (1 + len(extra)),
        out_specs=[pl.BlockSpec(memory_space=pltpu.VMEM)] * len(cuts),
        scratch_shapes=[
            pltpu.VMEM((2 * heads, positions, 2 * HD), BF),
            pltpu.VMEM((rows, positions), F32),
            pltpu.VMEM((rows, positions), F32),
            pltpu.VMEM((2, 8, positions), F32),
            pltpu.VMEM((heads, blocks, HD), F32),
            pltpu.SMEM((4,), jnp.int32),
            pltpu.SMEM((1,), jnp.int32),
            pltpu.SemaphoreType.DMA((2 * heads,)),
        ],
        compiler_params=params(),
        cost_estimate=pl.CostEstimate(
            flops=work * 512, bytes_accessed=heads << 20, transcendentals=work
        ),
        name="prefix_attention",
    )(usable, *qs, prefix_kv, *extra)


def blend_weights(la, lb):
    top = jnp.maximum(la, lb)
    ea, eb = jnp.exp(la - top), jnp.exp(lb - top)
    total = ea + eb
    return ea / total, top + jnp.log(total)


def spread(w):
    return jnp.broadcast_to(w, (HD, HD)).T


def read_lse(rows, m):
    return rows[3 * m:3 * m + 1] + rows[3 * m + 1:3 * m + 2] + rows[3 * m + 2:3 * m + 3]


def merge_line(ways, spot):
    tiles = ways[0][0].shape[1] // 128
    at = [(way[spot // way[0].shape[0]], spot % way[0].shape[0]) for way in ways]
    rows = [r[i, tiles * 128:, :].astype(F32) for r, i in at]
    datas, tops = [], []
    for t in range(tiles):
        lses = [read_lse(r, t) for r in rows]
        top = functools.reduce(jnp.maximum, lses)
        es = [jnp.exp(x - top) for x in lses]
        total = functools.reduce(jnp.add, es)
        blocks = [r[i, t * 128:(t + 1) * 128, :].astype(F32) for r, i in at]
        data = blocks[-1]
        for e, o in zip(es[:-1], blocks[:-1]):
            data = data + spread(e / total) * (o - blocks[-1])
        datas.append(data)
        tops.append(top + jnp.log(total))
    return datas, tops


def merge_kernel(shape, *refs):
    refs = list(refs)
    ins = [[[refs.pop(0) for _ in range(n)] for n in side] for side in shape]
    out_refs = refs
    sides = len(shape)
    outs = [(ref, b) for ref in out_refs for b in range(ref.shape[0])]
    for spot, (out_ref, b) in reversed(list(enumerate(outs))):
        merged = [merge_line(side, spot) for side in ins]
        tiles = len(merged[0][0])
        order = [(c, m * 2 + k) for m in range(tiles // 2) for c in range(sides) for k in range(2)]
        for n, (c, t) in enumerate(order):
            out_ref[b, n * 128:(n + 1) * 128, :] = merged[c][0][t].astype(BF)
        out_ref[b, len(order) * 128:, :] = lse_rows([merged[c][1][t][None] for c, t in order])[0]


def merge(sides, counts):
    ins = [x for side in sides for way in side for x in way]
    shape = [[len(way) for way in side] for side in sides]
    blocks, line = sum(counts), ins[0].shape[1]
    tiles = (line // 128) * len(sides)
    extra_rows = -(-3 * tiles // 16) * 16
    return pl.pallas_call(
        functools.partial(merge_kernel, shape),
        out_shape=[jax.ShapeDtypeStruct((n, tiles * 128 + extra_rows, HD), BF) for n in counts],
        in_specs=[pl.BlockSpec(memory_space=pltpu.VMEM)] * len(ins),
        out_specs=[pl.BlockSpec(memory_space=pltpu.VMEM)] * len(counts),
        compiler_params=params(),
        cost_estimate=pl.CostEstimate(
            flops=blocks * tiles * 128 * 128 * 6,
            bytes_accessed=blocks * tiles * 128 * HD * 6,
            transcendentals=0,
        ),
        name="merge_step",
    )(*ins)


def last_kernel(*refs):
    parts, out_ref = refs[:4], refs[5]
    low = lax.broadcasted_iota(jnp.int32, (1, HD), 1) < 64
    datas, tops = merge_line([[p] for p in parts], 0)
    rolled = [pltpu.roll(jnp.broadcast_to(t, (8, HD)), 64, 1)[0:1] for t in tops]
    for h in range(8):
        k, side = h // 2, h % 2
        if side == 0:
            joined = jnp.where(low, tops[k], rolled[4 + k])
        else:
            joined = jnp.where(low, rolled[k], tops[4 + k])
        for m in range(2):
            piece = datas[4 * m + k][side * 64:(side + 1) * 64]
            out_ref[h, m * 64:(m + 1) * 64, :] = piece.astype(BF)
        out_ref[h, 128:LAST, :] = lse_rows([joined[None]])[0]


def merge_last(parts, after):
    return pl.pallas_call(
        last_kernel,
        out_shape=jax.ShapeDtypeStruct((8, LAST, HD), BF),
        in_specs=[pl.BlockSpec(memory_space=pltpu.VMEM)] * 4
        + [pl.BlockSpec(memory_space=pl.ANY)],
        out_specs=pl.BlockSpec(memory_space=pltpu.VMEM),
        compiler_params=params(),
        name="merge_last",
    )(*parts, after)


def suffix_kernel(first, len_ref, q_ref, kv_ref, new_ref, o_ref, lse_ref):
    per = q_ref.shape[0]
    positions = kv_ref.shape[1]
    step_id = lax.broadcasted_iota(jnp.int32, (ROWS, 1), 0) // GROUP
    pos = lax.broadcasted_iota(jnp.int32, (ROWS, positions), 1)
    ones = jnp.ones((positions, HD), BF)
    for e in range(per):
        used = len_ref[first + pl.program_id(0) * per + e]
        q = q_ref[e]
        qf = q.astype(F32)
        fresh = new_ref[e].astype(F32)
        s = lax.dot_general(
            q, kv_ref[e, :, :HD], (((1,), (1,)), ((), ())), preferred_element_type=F32
        )
        s = jnp.where(pos < used, s, NEG)
        top = jnp.max(s, axis=1, keepdims=True)
        extra = []
        for t in range(STEPS):
            f = jnp.sum(qf * fresh[t:t + 1, :HD], axis=1, keepdims=True)
            f = jnp.where(step_id >= t, f, NEG)
            extra.append(f)
            top = jnp.maximum(top, f)
        p = jnp.exp2((s - top) * (ROOT * LOG2E)).astype(BF)
        r = jnp.dot(
            p, jnp.concatenate([kv_ref[e, :, HD:], ones], axis=1), preferred_element_type=F32
        )
        num, den = r[:, :HD], r[:, HD:]
        for t in range(STEPS):
            w = jnp.exp2((extra[t] - top) * (ROOT * LOG2E))
            num = num + w * fresh[t:t + 1, HD:]
            den = den + w
        o_ref[e] = num / den
        lse_ref[e] = top * ROOT + jnp.log(den)


def suffix_attention(suffix_len, q_rows, suffix_kv, new_kv, first, count):
    positions = suffix_kv.shape[1]
    per = 4
    skip = first // per
    one = jax.ShapeDtypeStruct((count, ROWS, HD), F32)
    grid_spec = pltpu.PrefetchScalarGridSpec(
        num_scalar_prefetch=1,
        grid=(count // per,),
        in_specs=[
            pl.BlockSpec((per, ROWS, HD), lambda s, n: (s + skip, 0, 0)),
            pl.BlockSpec((per, positions, 2 * HD), lambda s, n: (s + skip, 0, 0)),
            pl.BlockSpec((per, STEPS, 2 * HD), lambda s, n: (s + skip, 0, 0)),
        ],
        out_specs=[pl.BlockSpec((per, ROWS, HD), lambda s, n: (s, 0, 0))] * 2,
    )
    return pl.pallas_call(
        functools.partial(suffix_kernel, first),
        out_shape=[one, one],
        grid_spec=grid_spec,
        compiler_params=params(),
        cost_estimate=pl.CostEstimate(
            flops=count * 256 * positions * 128 * 4,
            bytes_accessed=count << 19,
            transcendentals=count * ROWS * positions,
        ),
        name="suffix_attention",
    )(suffix_len, q_rows, suffix_kv, new_kv)


def final_kernel(
    own_ref, off_ref, oa_ref, la_ref, ob_ref, lb_ref, part_ref, out_ref, data_ref, top_ref, wide_ref
):
    for t in range(8):
        data_ref[t] = part_ref[t, 0:128, :].astype(F32)
        rows = part_ref[t, 128:LAST, :].astype(F32)
        top_ref[t] = spread(read_lse(rows, 0))
    each = oa_ref.shape[0]
    for r in range(2 * each):
        o_ref, l_ref = (oa_ref, la_ref) if r < each else (ob_ref, lb_ref)
        at = pl.ds(pl.multiple_of(off_ref[r], ROWS), ROWS)
        op, lp = data_ref[own_ref[r], at, :], top_ref[own_ref[r], at, :]
        w, _ = blend_weights(lp, l_ref[r % each])
        ol = o_ref[r % each]
        wide_ref[r] = ol + w * (op - ol)
    for g in range(GROUP):
        out_ref[:, :, g * HD:(g + 1) * HD] = wide_ref[:, pl.ds(g, STEPS, GROUP), :].astype(BF)


def finish(own, off, local, parts):
    count = own.shape[0]
    return pl.pallas_call(
        final_kernel,
        out_shape=jax.ShapeDtypeStruct((count, STEPS, GROUP * HD), BF),
        in_specs=[pl.BlockSpec(memory_space=pltpu.SMEM)] * 2
        + [pl.BlockSpec(memory_space=pltpu.VMEM)] * 5,
        out_specs=pl.BlockSpec(memory_space=pltpu.VMEM),
        scratch_shapes=[
            pltpu.VMEM((8, HD, HD), F32),
            pltpu.VMEM((8, HD, HD), F32),
            pltpu.VMEM((count, ROWS, HD), F32),
        ],
        compiler_params=params(),
        name="finish",
    )(own, off, *local, parts)


def on_device(prefix_kv, prefix_len, prefix_of, suffix_len, suffix_kv, queries, new_kv):
    mine, block = lax.axis_index("pre"), lax.axis_index("req")
    shard = prefix_kv.shape[1]
    count = queries.shape[0]

    owners = prefix_of[:, 0]
    ids = jnp.arange(count, dtype=jnp.int32)
    earlier = (owners[None, :] == owners[:, None]) & (ids[None, :] < ids[:, None])
    rank = jnp.sum(earlier.astype(jnp.int32), axis=1)
    part = (owners & 1) * 2 + rank
    own_len = lax.dynamic_slice_in_dim(prefix_len, mine * 2, 2, 0)
    usable = jnp.clip(own_len - block * shard, 0, shard)

    q_rows, packed = pack(owners, queries)
    heads = lax.all_to_all(packed, "pre", 0, 0, tiled=True)
    local = []
    for first in (0, count // 2):
        local += suffix_attention(suffix_len, q_rows, suffix_kv, new_kv, first, count // 2)

    near = join([heads[None]] + three_ways([heads[None]] * 3), cuts=4, after=local[0])
    got = [quarter_step(near[k], k, 2) for k in range(4)]
    near = [join([near[k], got[k]])[0] for k in range(4)]
    far = [quarter_step(near[k], k, 3) for k in range(4)]
    attend = functools.partial(prefix_attention, usable, prefix_kv)
    near0 = attend(near[:2], 0)
    far0 = attend(far[:2], 0, near0[0])
    far1 = attend(far[2:], 4, far0[0])
    near1 = attend(near[2:], 4, far1[0], (4, 2, 2))
    ways = [[[2], [3], [2, 3]], [[3], [2], [2, 3]]]
    back = []
    for a, (close, away) in enumerate(((near0, far0), (near1, far1))):
        back.append([[req_step(x, ways[a][0]) for x in close[1:]]])
        back[a] += [[req_step(away[n], ways[a][n + 1])] for n in range(2)]
    most0 = merge([[near0[:1]] + back[0]], [4])
    most1 = merge([[near1[:1]] + back[1][1:]], [4])
    parts = merge([[most0], [most1, back[1][0]]], [1] * 4)
    final = merge_last([parts[0]] + three_ways(parts[1:]), local[2])
    back = lax.all_to_all(final, "pre", 0, 0, tiled=True)
    return finish(owners >> 1, part * ROWS, local, back)


def solution(mesh):
    placed = (
        P("pre", "req", None),
        P(),
        P("req", None),
        P("req"),
        P("req", None, "pre"),
        P("req", None, "pre"),
        P("req", None, "pre"),
    )
    return jax.shard_map(
        on_device, mesh=mesh, in_specs=placed, out_specs=P("req", None, "pre"), check_vma=False
    )
```

```python
import functools
import math

import jax
import jax.numpy as jnp
from jax import lax
from jax.experimental import pallas as pl
from jax.experimental.pallas import tpu as pltpu
from jax.sharding import PartitionSpec as P

HD = 128
GROUP = 8
STEPS = 4
ROWS = STEPS * GROUP
NEG = -1e30
ROOT = 1.0 / math.sqrt(HD)
LOG2E = math.log2(math.e)
EMPTY = 128.0
LAST = 144
BF = jnp.bfloat16
F32 = jnp.float32


def params(mb=48):
    return pltpu.CompilerParams(vmem_limit_bytes=mb * 1024 * 1024)


FLIPS = (1, 4, 3, 12)


def req_step(x, turns):
    pairs = []
    for i in range(8):
        flip = 0
        for turn in turns:
            flip ^= FLIPS[(2 * (i & 1) + turn) % 4]
        pairs += [(i * 16 + j, i * 16 + (j ^ flip)) for j in range(16)]
    return lax.ppermute(x, ("pre", "req"), pairs)


def three_ways(xs):
    return [req_step(x, way) for x, way in zip(xs, ([0], [1], [0, 1]))]


def split3(x):
    hi = x.astype(BF).astype(F32)
    mid = (x - hi).astype(BF).astype(F32)
    low = (x - hi - mid).astype(BF).astype(F32)
    return hi, mid, low


def pack_kernel(of_ref, q_ref, rows_ref, out_ref, wide_ref, seen_ref, req_ref):
    count = q_ref.shape[0]
    for p in range(16):
        seen_ref[p] = 0
    for slot in range(32):
        req_ref[slot] = -1
    for r in range(count):
        p = of_ref[r]
        rank = seen_ref[p]
        seen_ref[p] = rank + 1
        req_ref[p * 2 + rank] = r
    for g in range(GROUP):
        wide_ref[:, pl.ds(g, STEPS, GROUP), :] = q_ref[:, :, g * HD:(g + 1) * HD].astype(F32)
    rows_ref[...] = wide_ref[...].astype(BF)
    nobody = jnp.full((ROWS, HD), EMPTY, BF)
    for slot in range(32):
        r = req_ref[slot]
        rows = rows_ref[jnp.maximum(r, 0)]
        at = (slot % 4) * ROWS
        out_ref[slot // 4, at:at + ROWS, :] = jnp.where(r >= 0, rows, nobody)


def pack(owners, queries):
    count = queries.shape[0]
    return pl.pallas_call(
        pack_kernel,
        out_shape=[
            jax.ShapeDtypeStruct((count, ROWS, HD), BF),
            jax.ShapeDtypeStruct((8, 128, HD), BF),
        ],
        in_specs=[pl.BlockSpec(memory_space=pltpu.SMEM), pl.BlockSpec(memory_space=pltpu.VMEM)],
        out_specs=[pl.BlockSpec(memory_space=pltpu.VMEM)] * 2,
        scratch_shapes=[
            pltpu.VMEM((count, ROWS, HD), F32),
            pltpu.SMEM((16,), jnp.int32),
            pltpu.SMEM((32,), jnp.int32),
        ],
        compiler_params=params(),
        name="pack_slots",
    )(owners, queries)


def join_kernel(groups, cuts, total, *refs):
    out_refs = refs[-groups * cuts:]
    ins = refs[:total]
    count = total // groups
    each = ins[0].shape[0]
    width = ins[0].shape[1] // cuts
    for g in range(groups):
        for c in range(cuts):
            for n in range(count):
                piece = ins[g * count + n][:, c * width:(c + 1) * width]
                out_refs[g * cuts + c][n * each:(n + 1) * each] = piece


def join(parts, groups=1, cuts=1, after=None):
    extra = [] if after is None else [after]
    first = parts[0].shape
    shape = (len(parts) // groups * first[0], first[1] // cuts) + first[2:]
    return pl.pallas_call(
        functools.partial(join_kernel, groups, cuts, len(parts)),
        out_shape=[jax.ShapeDtypeStruct(shape, BF)] * (groups * cuts),
        in_specs=[pl.BlockSpec(memory_space=pltpu.VMEM)] * len(parts)
        + [pl.BlockSpec(memory_space=pl.ANY)] * len(extra),
        out_specs=[pl.BlockSpec(memory_space=pltpu.VMEM)] * (groups * cuts),
        compiler_params=params(),
        name="join",
    )(*parts, *extra)


def halves_kernel(*refs):
    ins, (first, low, high, second) = refs[:4], refs[5:]
    for n in range(4):
        first[n] = ins[n][0, :4]
        second[n] = ins[n][0, 4:]
        part = low if n < 2 else high
        part[n % 2] = ins[n][0, :4]


def to_halves(parts, after):
    return pl.pallas_call(
        halves_kernel,
        out_shape=[jax.ShapeDtypeStruct((n, 4, 128, HD), BF) for n in (4, 2, 2, 4)],
        in_specs=[pl.BlockSpec(memory_space=pltpu.VMEM)] * 4
        + [pl.BlockSpec(memory_space=pl.ANY)],
        out_specs=[pl.BlockSpec(memory_space=pltpu.VMEM)] * 4,
        compiler_params=params(),
        name="to_halves",
    )(*parts, after)


def prefix_kernel(first, extra, count, use_ref, *rest):
    q_refs, kv_hbm = rest[:count], rest[count]
    rest = rest[count + 1 + extra:]
    out_refs = rest[:-8]
    kv_all, sa_ref, sb_ref, bias_ref, lse_ref, group_ref, many_ref, sems = rest[-8:]
    heads = 4
    positions = kv_all.shape[1]
    blocks = sum(r.shape[0] for r in q_refs)
    rows = blocks * ROWS

    def fetch(m, h):
        at = (first + h) * (2 * HD)
        return pltpu.make_async_copy(
            kv_hbm.at[m, :, pl.ds(at, 2 * HD)], kv_all.at[m * heads + h], sems.at[m * heads + h]
        )

    for m in range(2):

        @pl.when(use_ref[m] > 0)
        def _():
            for h in range(heads):
                fetch(m, h).start()

    marks = []
    for w in range(4):
        each = [jnp.min(r[:, 0, w * ROWS:w * ROWS + 16, :].astype(F32), axis=0) for r in q_refs]
        marks.append(jnp.min(functools.reduce(jnp.minimum, each)) < 100.0)
    live = [(use_ref[w // 2] > 0) & marks[w] for w in range(4)]

    many_ref[0] = 0
    for m in range(2):
        for rank in range(2):
            on = live[m * 2 + rank]

            @pl.when(on)
            def _():
                n = many_ref[0]
                group_ref[n] = m * 2 + rank
                many_ref[0] = n + 1

            @pl.when(jnp.logical_not(on))
            def _():
                for h in range(heads):
                    for ref in out_refs:
                        at = m * 256 + h * 64 + rank * ROWS
                        ref[:, at:at + ROWS, :] = jnp.zeros((ref.shape[0], ROWS, HD), BF)

    for m in range(2):
        pos = lax.broadcasted_iota(jnp.int32, (8, positions), 1)
        bias_ref[m] = jnp.where(pos < use_ref[m], 0.0, NEG)
    lse_ref[...] = jnp.full(lse_ref.shape, NEG, F32)
    n = many_ref[0]

    def decode(i):
        which = group_ref[jnp.minimum(i, n - 1)]
        return which, which >> 1, which & 1

    def arrive(i, hs):
        which, m, rank = decode(i)

        @pl.when((rank == 0) & (i < n))
        def _():
            for h in hs:
                fetch(m, h).wait()

    def score(i, h, s_ref):
        which, m, rank = decode(i)
        at = pl.ds(pl.multiple_of(which * ROWS, ROWS), ROWS)
        q = jnp.concatenate(
            [r[:, h, at, :].reshape(r.shape[0] * ROWS, HD) for r in q_refs], axis=0
        )
        k = kv_all[m * heads + h, :, :HD]
        s = lax.dot_general(q, k, (((1,), (1,)), ((), ())), preferred_element_type=F32)
        s = s.reshape(rows // 8, 8, positions) + bias_ref[m][None]
        s_ref[...] = s.reshape(rows, positions)

    def weigh(i, h, s_ref):
        which, m, rank = decode(i)
        c, side = h // 2, h % 2
        s = s_ref[...]
        top = jnp.max(s, axis=1, keepdims=True)
        p = jnp.exp2((s - top) * (ROOT * LOG2E)).astype(BF)
        v = kv_all[m * heads + h, :, HD:]
        v1 = jnp.concatenate([v, jnp.ones((positions, HD), BF)], axis=1)
        r = jnp.dot(p, v1, preferred_element_type=F32)
        den = r[:, HD:]
        o = r[:, :HD] / den
        lse = top * ROOT + jnp.log(den)
        at = pl.multiple_of(m * 256 + h * 64 + rank * ROWS, ROWS)
        o = o.reshape(blocks, ROWS, HD).astype(BF)
        spot = 0
        for ref in out_refs:
            ref[:, pl.ds(at, ROWS), :] = o[spot:spot + ref.shape[0]]
            spot += ref.shape[0]
        part = side * 2 + rank
        row_id = lax.broadcasted_iota(jnp.int32, (ROWS, HD), 0)
        lane_id = lax.broadcasted_iota(jnp.int32, (ROWS, HD), 1)
        diag = (lane_id - row_id == part * ROWS)[None]
        flat = jnp.sum(jnp.where(diag, lse.reshape(blocks, ROWS, HD), 0.0), axis=1)
        lanes = lax.broadcasted_iota(jnp.int32, (blocks, HD), 1) >> 5
        old = lse_ref[c * 2 + m]
        lse_ref[c * 2 + m] = jnp.where(lanes == part, flat, old)

    for m in range(2):

        @pl.when((use_ref[m] > 0) & jnp.logical_not(live[2 * m]))
        def _():
            for h in range(heads):
                fetch(m, h).wait()

    @pl.when(n > 0)
    def _():
        arrive(0, [0])
        score(0, 0, sa_ref)

        def body(j, carry):
            arrive(j, range(1, heads))
            arrive(j + 1, [0])
            for h in range(heads):
                now, later = (sa_ref, sb_ref) if h % 2 == 0 else (sb_ref, sa_ref)
                if h + 1 < heads:
                    score(j, h + 1, later)
                else:
                    score(j + 1, 0, later)
                weigh(j, h, now)
            return carry

        lax.fori_loop(0, n, body, 0)

    spot = 0
    for ref in out_refs:
        span = slice(spot, spot + ref.shape[0])
        tops = [lse_ref[2 * c + m, span, :][:, None, :] for m in range(2) for c in range(2)]
        ref[:, 512:, :] = lse_rows(tops)
        spot += ref.shape[0]


def lse_rows(tops):
    shape = (tops[0].shape[0], -(-3 * len(tops) // 16) * 16, HD)
    row = lax.broadcasted_iota(jnp.int32, shape, 1)
    out = jnp.zeros(shape, F32)
    at = 0
    for top in tops:
        for piece in split3(top):
            out = jnp.where(row == at, jnp.broadcast_to(piece, shape), out)
            at += 1
    return out.astype(BF)


def prefix_attention(usable, prefix_kv, qs, first, after=None, cuts=(4, 4)):
    count = len(qs)
    extra = [] if after is None else [after]
    heads = 4
    blocks = sum(q.shape[0] for q in qs)
    positions = prefix_kv.shape[1]
    rows = blocks * ROWS
    work = rows * positions * heads * 3
    return pl.pallas_call(
        functools.partial(prefix_kernel, first, len(extra), count),
        out_shape=[jax.ShapeDtypeStruct((n, 528, HD), BF) for n in cuts],
        in_specs=[pl.BlockSpec(memory_space=pltpu.SMEM)]
        + [pl.BlockSpec(memory_space=pltpu.VMEM)] * count
        + [pl.BlockSpec(memory_space=pl.ANY)] * (1 + len(extra)),
        out_specs=[pl.BlockSpec(memory_space=pltpu.VMEM)] * len(cuts),
        scratch_shapes=[
            pltpu.VMEM((2 * heads, positions, 2 * HD), BF),
            pltpu.VMEM((rows, positions), F32),
            pltpu.VMEM((rows, positions), F32),
            pltpu.VMEM((2, 8, positions), F32),
            pltpu.VMEM((heads, blocks, HD), F32),
            pltpu.SMEM((4,), jnp.int32),
            pltpu.SMEM((1,), jnp.int32),
            pltpu.SemaphoreType.DMA((2 * heads,)),
        ],
        compiler_params=params(),
        cost_estimate=pl.CostEstimate(
            flops=work * 512, bytes_accessed=heads << 20, transcendentals=work
        ),
        name="prefix_attention",
    )(usable, *qs, prefix_kv, *extra)


def blend_weights(la, lb):
    top = jnp.maximum(la, lb)
    ea, eb = jnp.exp(la - top), jnp.exp(lb - top)
    total = ea + eb
    return ea / total, top + jnp.log(total)


def spread(w):
    return jnp.broadcast_to(w, (HD, HD)).T


def read_lse(rows, m):
    return rows[3 * m:3 * m + 1] + rows[3 * m + 1:3 * m + 2] + rows[3 * m + 2:3 * m + 3]


def merge_line(ways, spot):
    tiles = ways[0][0].shape[1] // 128
    at = [(way[spot // way[0].shape[0]], spot % way[0].shape[0]) for way in ways]
    rows = [r[i, tiles * 128:, :].astype(F32) for r, i in at]
    datas, tops = [], []
    for t in range(tiles):
        lses = [read_lse(r, t) for r in rows]
        top = functools.reduce(jnp.maximum, lses)
        es = [jnp.exp(x - top) for x in lses]
        total = functools.reduce(jnp.add, es)
        blocks = [r[i, t * 128:(t + 1) * 128, :].astype(F32) for r, i in at]
        data = blocks[-1]
        for e, o in zip(es[:-1], blocks[:-1]):
            data = data + spread(e / total) * (o - blocks[-1])
        datas.append(data)
        tops.append(top + jnp.log(total))
    return datas, tops


def merge_kernel(shape, *refs):
    refs = list(refs)
    ins = [[[refs.pop(0) for _ in range(n)] for n in side] for side in shape]
    out_refs = refs
    sides = len(shape)
    outs = [(ref, b) for ref in out_refs for b in range(ref.shape[0])]
    for spot, (out_ref, b) in reversed(list(enumerate(outs))):
        merged = [merge_line(side, spot) for side in ins]
        tiles = len(merged[0][0])
        order = [(c, m * 2 + k) for m in range(tiles // 2) for c in range(sides) for k in range(2)]
        for n, (c, t) in enumerate(order):
            out_ref[b, n * 128:(n + 1) * 128, :] = merged[c][0][t].astype(BF)
        out_ref[b, len(order) * 128:, :] = lse_rows([merged[c][1][t][None] for c, t in order])[0]


def merge(sides, counts):
    ins = [x for side in sides for way in side for x in way]
    shape = [[len(way) for way in side] for side in sides]
    blocks, line = sum(counts), ins[0].shape[1]
    tiles = (line // 128) * len(sides)
    extra_rows = -(-3 * tiles // 16) * 16
    return pl.pallas_call(
        functools.partial(merge_kernel, shape),
        out_shape=[jax.ShapeDtypeStruct((n, tiles * 128 + extra_rows, HD), BF) for n in counts],
        in_specs=[pl.BlockSpec(memory_space=pltpu.VMEM)] * len(ins),
        out_specs=[pl.BlockSpec(memory_space=pltpu.VMEM)] * len(counts),
        compiler_params=params(),
        cost_estimate=pl.CostEstimate(
            flops=blocks * tiles * 128 * 128 * 6,
            bytes_accessed=blocks * tiles * 128 * HD * 6,
            transcendentals=0,
        ),
        name="merge_step",
    )(*ins)


def last_kernel(*refs):
    parts, out_ref = refs[:4], refs[5]
    low = lax.broadcasted_iota(jnp.int32, (1, HD), 1) < 64
    datas, tops = merge_line([[p] for p in parts], 0)
    rolled = [pltpu.roll(jnp.broadcast_to(t, (8, HD)), 64, 1)[0:1] for t in tops]
    for h in range(8):
        k, side = h // 2, h % 2
        if side == 0:
            joined = jnp.where(low, tops[k], rolled[4 + k])
        else:
            joined = jnp.where(low, rolled[k], tops[4 + k])
        for m in range(2):
            piece = datas[4 * m + k][side * 64:(side + 1) * 64]
            out_ref[h, m * 64:(m + 1) * 64, :] = piece.astype(BF)
        out_ref[h, 128:LAST, :] = lse_rows([joined[None]])[0]


def merge_last(parts, after):
    return pl.pallas_call(
        last_kernel,
        out_shape=jax.ShapeDtypeStruct((8, LAST, HD), BF),
        in_specs=[pl.BlockSpec(memory_space=pltpu.VMEM)] * 4
        + [pl.BlockSpec(memory_space=pl.ANY)],
        out_specs=pl.BlockSpec(memory_space=pltpu.VMEM),
        compiler_params=params(),
        name="merge_last",
    )(*parts, after)


def suffix_kernel(first, len_ref, q_ref, kv_ref, new_ref, o_ref, lse_ref):
    per = q_ref.shape[0]
    positions = kv_ref.shape[1]
    step_id = lax.broadcasted_iota(jnp.int32, (ROWS, 1), 0) // GROUP
    pos = lax.broadcasted_iota(jnp.int32, (ROWS, positions), 1)
    ones = jnp.ones((positions, HD), BF)
    for e in range(per):
        used = len_ref[first + pl.program_id(0) * per + e]
        q = q_ref[e]
        qf = q.astype(F32)
        fresh = new_ref[e].astype(F32)
        s = lax.dot_general(
            q, kv_ref[e, :, :HD], (((1,), (1,)), ((), ())), preferred_element_type=F32
        )
        s = jnp.where(pos < used, s, NEG)
        top = jnp.max(s, axis=1, keepdims=True)
        extra = []
        for t in range(STEPS):
            f = jnp.sum(qf * fresh[t:t + 1, :HD], axis=1, keepdims=True)
            f = jnp.where(step_id >= t, f, NEG)
            extra.append(f)
            top = jnp.maximum(top, f)
        p = jnp.exp2((s - top) * (ROOT * LOG2E)).astype(BF)
        r = jnp.dot(
            p, jnp.concatenate([kv_ref[e, :, HD:], ones], axis=1), preferred_element_type=F32
        )
        num, den = r[:, :HD], r[:, HD:]
        for t in range(STEPS):
            w = jnp.exp2((extra[t] - top) * (ROOT * LOG2E))
            num = num + w * fresh[t:t + 1, HD:]
            den = den + w
        o_ref[e] = num / den
        lse_ref[e] = top * ROOT + jnp.log(den)


def suffix_attention(suffix_len, q_rows, suffix_kv, new_kv, first, count):
    positions = suffix_kv.shape[1]
    per = 4
    skip = first // per
    one = jax.ShapeDtypeStruct((count, ROWS, HD), F32)
    grid_spec = pltpu.PrefetchScalarGridSpec(
        num_scalar_prefetch=1,
        grid=(count // per,),
        in_specs=[
            pl.BlockSpec((per, ROWS, HD), lambda s, n: (s + skip, 0, 0)),
            pl.BlockSpec((per, positions, 2 * HD), lambda s, n: (s + skip, 0, 0)),
            pl.BlockSpec((per, STEPS, 2 * HD), lambda s, n: (s + skip, 0, 0)),
        ],
        out_specs=[pl.BlockSpec((per, ROWS, HD), lambda s, n: (s, 0, 0))] * 2,
    )
    return pl.pallas_call(
        functools.partial(suffix_kernel, first),
        out_shape=[one, one],
        grid_spec=grid_spec,
        compiler_params=params(),
        cost_estimate=pl.CostEstimate(
            flops=count * 256 * positions * 128 * 4,
            bytes_accessed=count << 19,
            transcendentals=count * ROWS * positions,
        ),
        name="suffix_attention",
    )(suffix_len, q_rows, suffix_kv, new_kv)


def final_kernel(
    own_ref, off_ref, oa_ref, la_ref, ob_ref, lb_ref, part_ref, out_ref, data_ref, top_ref, wide_ref
):
    for t in range(8):
        data_ref[t] = part_ref[t, 0:128, :].astype(F32)
        rows = part_ref[t, 128:LAST, :].astype(F32)
        top_ref[t] = spread(read_lse(rows, 0))
    each = oa_ref.shape[0]
    for r in range(2 * each):
        o_ref, l_ref = (oa_ref, la_ref) if r < each else (ob_ref, lb_ref)
        at = pl.ds(pl.multiple_of(off_ref[r], ROWS), ROWS)
        op, lp = data_ref[own_ref[r], at, :], top_ref[own_ref[r], at, :]
        w, _ = blend_weights(lp, l_ref[r % each])
        ol = o_ref[r % each]
        wide_ref[r] = ol + w * (op - ol)
    for g in range(GROUP):
        out_ref[:, :, g * HD:(g + 1) * HD] = wide_ref[:, pl.ds(g, STEPS, GROUP), :].astype(BF)


def finish(own, off, local, parts):
    count = own.shape[0]
    return pl.pallas_call(
        final_kernel,
        out_shape=jax.ShapeDtypeStruct((count, STEPS, GROUP * HD), BF),
        in_specs=[pl.BlockSpec(memory_space=pltpu.SMEM)] * 2
        + [pl.BlockSpec(memory_space=pltpu.VMEM)] * 5,
        out_specs=pl.BlockSpec(memory_space=pltpu.VMEM),
        scratch_shapes=[
            pltpu.VMEM((8, HD, HD), F32),
            pltpu.VMEM((8, HD, HD), F32),
            pltpu.VMEM((count, ROWS, HD), F32),
        ],
        compiler_params=params(),
        name="finish",
    )(own, off, *local, parts)


def on_device(prefix_kv, prefix_len, prefix_of, suffix_len, suffix_kv, queries, new_kv):
    mine, block = lax.axis_index("pre"), lax.axis_index("req")
    shard = prefix_kv.shape[1]
    count = queries.shape[0]

    owners = prefix_of[:, 0]
    ids = jnp.arange(count, dtype=jnp.int32)
    earlier = (owners[None, :] == owners[:, None]) & (ids[None, :] < ids[:, None])
    rank = jnp.sum(earlier.astype(jnp.int32), axis=1)
    part = (owners & 1) * 2 + rank
    own_len = lax.dynamic_slice_in_dim(prefix_len, mine * 2, 2, 0)
    usable = jnp.clip(own_len - block * shard, 0, shard)

    q_rows, packed = pack(owners, queries)
    heads = lax.all_to_all(packed, "pre", 0, 0, tiled=True)
    local = []
    for first in (0, count // 2):
        local += suffix_attention(suffix_len, q_rows, suffix_kv, new_kv, first, count // 2)

    parts = [heads[None]] + three_ways([heads[None]] * 3)
    half0, low0, high0, half1 = to_halves(parts, local[0])
    ways = [[[2], [3], [2, 3]], [[3], [2], [2, 3]]]
    close0 = [req_step(x, ways[0][0]) for x in (low0, high0)]
    far = [req_step(half0, way) for way in ways[0][1:]]
    far += [req_step(half1, way) for way in ways[1][1:]]
    close1 = [req_step(half1, ways[1][0])]
    attend = functools.partial(prefix_attention, usable, prefix_kv)
    near0 = attend([half0] + close0, 0)
    far0 = attend(far[:2], 0, near0[0])
    far1 = attend(far[2:], 4, far0[0])
    near1 = attend([half1] + close1, 4, far1[0], (4, 2, 2))
    sent0 = join([near0[1]], after=far0[0])
    back = []
    for a, (close, away) in enumerate(((sent0, far0), (near1[1:], far1))):
        back.append([[req_step(x, ways[a][0]) for x in close]])
        back[a] += [[req_step(away[n], ways[a][n + 1])] for n in range(2)]
    most0 = merge([[near0[:1]] + back[0]], [4])
    most1 = merge([[near1[:1]] + back[1][1:]], [4])
    parts = merge([[most0], [most1, back[1][0]]], [1] * 4)
    final = merge_last([parts[0]] + three_ways(parts[1:]), local[2])
    back = lax.all_to_all(final, "pre", 0, 0, tiled=True)
    return finish(owners >> 1, part * ROWS, local, back)


def solution(mesh):
    placed = (
        P("pre", "req", None),
        P(),
        P("req", None),
        P("req"),
        P("req", None, "pre"),
        P("req", None, "pre"),
        P("req", None, "pre"),
    )
    return jax.shard_map(
        on_device, mesh=mesh, in_specs=placed, out_specs=P("req", None, "pre"), check_vma=False
    )
```

```python
import functools
import math

import jax
import jax.numpy as jnp
from jax import lax
from jax.experimental import pallas as pl
from jax.experimental.pallas import tpu as pltpu
from jax.sharding import PartitionSpec as P

HD = 128
GROUP = 8
STEPS = 4
ROWS = STEPS * GROUP
NEG = -1e30
ROOT = 1.0 / math.sqrt(HD)
LOG2E = math.log2(math.e)
EMPTY = 128.0
LAST = 144
BF = jnp.bfloat16
F32 = jnp.float32


def params(mb=48):
    return pltpu.CompilerParams(vmem_limit_bytes=mb * 1024 * 1024)


FLIPS = (1, 4, 3, 12)
APART = (1, 4, 2, 8)


def req_step(x, turns, flips=FLIPS):
    pairs = []
    for i in range(8):
        flip = 0
        for turn in turns:
            flip ^= flips[(2 * (i & 1) + turn) % 4]
        pairs += [(i * 16 + j, i * 16 + (j ^ flip)) for j in range(16)]
    return lax.ppermute(x, ("pre", "req"), pairs)


def quarter_step(x, k, turn):
    return req_step(x, [turn if k % 2 == 0 else 5 - turn], APART if k in (1, 2) else FLIPS)


def three_ways(xs):
    return [req_step(x, way) for x, way in zip(xs, ([0], [1], [0, 1]))]


def split3(x):
    hi = x.astype(BF).astype(F32)
    mid = (x - hi).astype(BF).astype(F32)
    low = (x - hi - mid).astype(BF).astype(F32)
    return hi, mid, low


def pack_kernel(of_ref, q_ref, rows_ref, out_ref, wide_ref, seen_ref, req_ref):
    count = q_ref.shape[0]
    for p in range(16):
        seen_ref[p] = 0
    for slot in range(32):
        req_ref[slot] = -1
    for r in range(count):
        p = of_ref[r]
        rank = seen_ref[p]
        seen_ref[p] = rank + 1
        req_ref[p * 2 + rank] = r
    for g in range(GROUP):
        wide_ref[:, pl.ds(g, STEPS, GROUP), :] = q_ref[:, :, g * HD:(g + 1) * HD].astype(F32)
    rows_ref[...] = wide_ref[...].astype(BF)
    nobody = jnp.full((ROWS, HD), EMPTY, BF)
    for slot in range(32):
        r = req_ref[slot]
        rows = rows_ref[jnp.maximum(r, 0)]
        at = (slot % 4) * ROWS
        out_ref[slot // 4, at:at + ROWS, :] = jnp.where(r >= 0, rows, nobody)


def pack(owners, queries):
    count = queries.shape[0]
    return pl.pallas_call(
        pack_kernel,
        out_shape=[
            jax.ShapeDtypeStruct((count, ROWS, HD), BF),
            jax.ShapeDtypeStruct((8, 128, HD), BF),
        ],
        in_specs=[pl.BlockSpec(memory_space=pltpu.SMEM), pl.BlockSpec(memory_space=pltpu.VMEM)],
        out_specs=[pl.BlockSpec(memory_space=pltpu.VMEM)] * 2,
        scratch_shapes=[
            pltpu.VMEM((count, ROWS, HD), F32),
            pltpu.SMEM((16,), jnp.int32),
            pltpu.SMEM((32,), jnp.int32),
        ],
        compiler_params=params(),
        name="pack_slots",
    )(owners, queries)


def join_kernel(groups, cuts, total, *refs):
    out_refs = refs[-groups * cuts:]
    ins = refs[:total]
    count = total // groups
    each = ins[0].shape[0]
    width = ins[0].shape[1] // cuts
    for g in range(groups):
        for c in range(cuts):
            for n in range(count):
                piece = ins[g * count + n][:, c * width:(c + 1) * width]
                out_refs[g * cuts + c][n * each:(n + 1) * each] = piece


def join(parts, groups=1, cuts=1, after=None):
    extra = [] if after is None else [after]
    first = parts[0].shape
    shape = (len(parts) // groups * first[0], first[1] // cuts) + first[2:]
    return pl.pallas_call(
        functools.partial(join_kernel, groups, cuts, len(parts)),
        out_shape=[jax.ShapeDtypeStruct(shape, BF)] * (groups * cuts),
        in_specs=[pl.BlockSpec(memory_space=pltpu.VMEM)] * len(parts)
        + [pl.BlockSpec(memory_space=pl.ANY)] * len(extra),
        out_specs=[pl.BlockSpec(memory_space=pltpu.VMEM)] * (groups * cuts),
        compiler_params=params(),
        name="join",
    )(*parts, *extra)


def prefix_kernel(count, first, extra, use_ref, *rest):
    q_refs, kv_hbm = rest[:count], rest[count]
    rest = rest[count + 1 + extra:]
    out_refs = rest[:count]
    kv_all, sa_ref, sb_ref, bias_ref, lse_ref, group_ref, many_ref, sems = rest[
        count:
    ]
    heads = 2 * count
    positions = kv_all.shape[1]
    blocks = q_refs[0].shape[0]
    rows = blocks * ROWS

    def fetch(m, h):
        at = pl.multiple_of((2 * first + h) * (2 * HD), 2 * HD)
        return pltpu.make_async_copy(
            kv_hbm.at[m, :, pl.ds(at, 2 * HD)], kv_all.at[m * heads + h], sems.at[m * heads + h]
        )

    marks = [
        jnp.min(q_refs[0][:, 0, w * ROWS:w * ROWS + 16, :].astype(F32)) < 100.0 for w in range(4)
    ]
    live = [(use_ref[w // 2] > 0) & marks[w] for w in range(4)]

    many_ref[0] = 0
    for m in range(2):
        for rank in range(2):
            on = live[m * 2 + rank]

            @pl.when(on)
            def _():
                n = many_ref[0]
                group_ref[n] = m * 2 + rank
                if rank == 0:
                    for h in range(heads):
                        fetch(m, h).start()
                many_ref[0] = n + 1

            @pl.when(jnp.logical_not(on))
            def _():
                for side in range(2):
                    at = m * 128 + side * 64 + rank * ROWS
                    for c in range(count):
                        out_refs[c][:, at:at + ROWS, :] = jnp.zeros((blocks, ROWS, HD), BF)

    for m in range(2):
        pos = lax.broadcasted_iota(jnp.int32, (8, positions), 1)
        bias_ref[m] = jnp.where(pos < use_ref[m], 0.0, NEG)
    lse_ref[...] = jnp.full(lse_ref.shape, NEG, F32)
    n = many_ref[0]

    def decode(i):
        which = group_ref[jnp.minimum(i, n - 1)]
        return which, which >> 1, which & 1

    def arrive(i, hs):
        which, m, rank = decode(i)

        @pl.when((rank == 0) & (i < n))
        def _():
            for h in hs:
                fetch(m, h).wait()

    def score(i, h, s_ref):
        which, m, rank = decode(i)
        at = pl.ds(pl.multiple_of(which * ROWS, ROWS), ROWS)
        q = q_refs[h // 2][:, h % 2, at, :].reshape(rows, HD)
        k = kv_all[m * heads + h, :, :HD]
        s = lax.dot_general(q, k, (((1,), (1,)), ((), ())), preferred_element_type=F32)
        s = s.reshape(rows // 8, 8, positions) + bias_ref[m][None]
        s_ref[...] = s.reshape(rows, positions)

    def weigh(i, h, s_ref):
        which, m, rank = decode(i)
        c, side = h // 2, h % 2
        s = s_ref[...]
        top = jnp.max(s, axis=1, keepdims=True)
        p = jnp.exp2((s - top) * (ROOT * LOG2E)).astype(BF)
        v = kv_all[m * heads + h, :, HD:]
        v1 = jnp.concatenate([v, jnp.ones((positions, HD), BF)], axis=1)
        r = jnp.dot(p, v1, preferred_element_type=F32)
        den = r[:, HD:]
        o = r[:, :HD] / den
        lse = top * ROOT + jnp.log(den)
        at = pl.multiple_of(m * 128 + side * 64 + rank * ROWS, ROWS)
        out_refs[c][:, pl.ds(at, ROWS), :] = o.reshape(blocks, ROWS, HD).astype(BF)
        part = side * 2 + rank
        row_id = lax.broadcasted_iota(jnp.int32, (ROWS, HD), 0)
        lane_id = lax.broadcasted_iota(jnp.int32, (ROWS, HD), 1)
        diag = (lane_id - row_id == part * ROWS)[None]
        flat = jnp.sum(jnp.where(diag, lse.reshape(blocks, ROWS, HD), 0.0), axis=1)
        lanes = lax.broadcasted_iota(jnp.int32, (blocks, HD), 1) >> 5
        old = lse_ref[c * 2 + m]
        lse_ref[c * 2 + m] = jnp.where(lanes == part, flat, old)

    @pl.when(n > 0)
    def _():
        arrive(0, [0])
        score(0, 0, sa_ref)

        def body(j, carry):
            arrive(j, range(1, heads))
            arrive(j + 1, [0])
            for h in range(heads):
                now, later = (sa_ref, sb_ref) if h % 2 == 0 else (sb_ref, sa_ref)
                if h + 1 < heads:
                    score(j, h + 1, later)
                else:
                    score(j + 1, 0, later)
                weigh(j, h, now)
            return carry

        lax.fori_loop(0, n, body, 0)

    for c in range(count):
        out_refs[c][:, 256:, :] = lse_rows([lse_ref[2 * c + m][:, None, :] for m in range(2)])


def lse_rows(tops):
    shape = (tops[0].shape[0], -(-3 * len(tops) // 16) * 16, HD)
    row = lax.broadcasted_iota(jnp.int32, shape, 1)
    out = jnp.zeros(shape, F32)
    at = 0
    for top in tops:
        for piece in split3(top):
            out = jnp.where(row == at, jnp.broadcast_to(piece, shape), out)
            at += 1
    return out.astype(BF)


def prefix_attention(usable, qs, prefix_kv, first, after=None):
    count = len(qs)
    extra = [] if after is None else [after]
    heads = 2 * count
    blocks = qs[0].shape[0]
    positions = prefix_kv.shape[1]
    rows = blocks * ROWS
    work = rows * positions * heads * 3
    return pl.pallas_call(
        functools.partial(prefix_kernel, count, first, len(extra)),
        out_shape=[jax.ShapeDtypeStruct((blocks, 272, HD), BF)] * count,
        in_specs=[pl.BlockSpec(memory_space=pltpu.SMEM)]
        + [pl.BlockSpec(memory_space=pltpu.VMEM)] * count
        + [pl.BlockSpec(memory_space=pl.ANY)] * (1 + len(extra)),
        out_specs=[pl.BlockSpec(memory_space=pltpu.VMEM)] * count,
        scratch_shapes=[
            pltpu.VMEM((2 * heads, positions, 2 * HD), BF),
            pltpu.VMEM((rows, positions), F32),
            pltpu.VMEM((rows, positions), F32),
            pltpu.VMEM((2, 8, positions), F32),
            pltpu.VMEM((heads, blocks, HD), F32),
            pltpu.SMEM((4,), jnp.int32),
            pltpu.SMEM((1,), jnp.int32),
            pltpu.SemaphoreType.DMA((2 * heads,)),
        ],
        compiler_params=params(),
        cost_estimate=pl.CostEstimate(
            flops=work * 512, bytes_accessed=heads << 20, transcendentals=work
        ),
        name="prefix_attention",
    )(usable, *qs, prefix_kv, *extra)


def blend_weights(la, lb):
    top = jnp.maximum(la, lb)
    ea, eb = jnp.exp(la - top), jnp.exp(lb - top)
    total = ea + eb
    return ea / total, top + jnp.log(total)


def spread(w):
    return jnp.broadcast_to(w, (HD, HD)).T


def read_lse(rows, m):
    return rows[3 * m:3 * m + 1] + rows[3 * m + 1:3 * m + 2] + rows[3 * m + 2:3 * m + 3]


def merge_line(a_ref, b_ref, idx):
    tiles = a_ref.shape[1] // 128
    ra = a_ref[idx, tiles * 128:, :].astype(F32)
    rb = b_ref[idx, tiles * 128:, :].astype(F32)
    datas, tops = [], []
    for m in range(tiles):
        wa, lse = blend_weights(read_lse(ra, m), read_lse(rb, m))
        oa = a_ref[idx, m * 128:(m + 1) * 128, :].astype(F32)
        ob = b_ref[idx, m * 128:(m + 1) * 128, :].astype(F32)
        datas.append(ob + spread(wa) * (oa - ob))
        tops.append(lse)
    return datas, tops


def merge_kernel(pairs, extra, *refs):
    ins, out_refs = refs[:2 * pairs], refs[2 * pairs + extra:]
    outs = [(ref, b) for ref in out_refs for b in range(ref.shape[0])]
    for spot, (out_ref, b) in reversed(list(enumerate(outs))):
        merged = [merge_line(ins[2 * c], ins[2 * c + 1], spot) for c in range(pairs)]
        datas = [d for row in zip(*[x[0] for x in merged]) for d in row]
        tops = [t for row in zip(*[x[1] for x in merged]) for t in row]
        tiles = len(datas)
        for m in range(tiles):
            out_ref[b, m * 128:(m + 1) * 128, :] = datas[m].astype(BF)
        out_ref[b, tiles * 128:, :] = lse_rows([t[None] for t in tops])[0]


def merge(ins, counts, after=None):
    extra = [] if after is None else [after]
    blocks, line = ins[0].shape[:2]
    pairs = len(ins) // 2
    tiles = (line // 128) * pairs
    extra_rows = -(-3 * tiles // 16) * 16
    return pl.pallas_call(
        functools.partial(merge_kernel, pairs, len(extra)),
        out_shape=[jax.ShapeDtypeStruct((n, tiles * 128 + extra_rows, HD), BF) for n in counts],
        in_specs=[pl.BlockSpec(memory_space=pltpu.VMEM)] * len(ins)
        + [pl.BlockSpec(memory_space=pl.ANY)] * len(extra),
        out_specs=[pl.BlockSpec(memory_space=pltpu.VMEM)] * len(counts),
        compiler_params=params(),
        cost_estimate=pl.CostEstimate(
            flops=blocks * tiles * 128 * 128 * 6,
            bytes_accessed=blocks * tiles * 128 * HD * 6,
            transcendentals=0,
        ),
        name="merge_step",
    )(*ins, *extra)


def last_kernel(*refs):
    parts, out_ref = refs[:4], refs[5]
    low = lax.broadcasted_iota(jnp.int32, (1, HD), 1) < 64
    rows = [p[0, 1024:, :].astype(F32) for p in parts]
    datas, tops = [], []
    for t in range(8):
        each = [read_lse(r, t) for r in rows]
        top = functools.reduce(jnp.maximum, each)
        es = [jnp.exp(x - top) for x in each]
        total = es[0] + es[1] + es[2] + es[3]
        data = 0.0
        for p, e in zip(parts, es):
            data = data + spread(e / total) * p[0, t * 128:(t + 1) * 128, :].astype(F32)
        datas.append(data)
        tops.append(top + jnp.log(total))
    rolled = [pltpu.roll(jnp.broadcast_to(t, (8, HD)), 64, 1)[0:1] for t in tops]
    for h in range(8):
        k, side = h // 2, h % 2
        if side == 0:
            joined = jnp.where(low, tops[k], rolled[4 + k])
        else:
            joined = jnp.where(low, rolled[k], tops[4 + k])
        for m in range(2):
            piece = datas[4 * m + k][side * 64:(side + 1) * 64]
            out_ref[h, m * 64:(m + 1) * 64, :] = piece.astype(BF)
        out_ref[h, 128:LAST, :] = lse_rows([joined[None]])[0]


def merge_last(parts, after):
    return pl.pallas_call(
        last_kernel,
        out_shape=jax.ShapeDtypeStruct((8, LAST, HD), BF),
        in_specs=[pl.BlockSpec(memory_space=pltpu.VMEM)] * 4
        + [pl.BlockSpec(memory_space=pl.ANY)],
        out_specs=pl.BlockSpec(memory_space=pltpu.VMEM),
        compiler_params=params(),
        name="merge_last",
    )(*parts, after)


def suffix_kernel(first, len_ref, q_ref, kv_ref, new_ref, o_ref, lse_ref):
    per = q_ref.shape[0]
    positions = kv_ref.shape[1]
    step_id = lax.broadcasted_iota(jnp.int32, (ROWS, 1), 0) // GROUP
    pos = lax.broadcasted_iota(jnp.int32, (ROWS, positions), 1)
    ones = jnp.ones((positions, HD), BF)
    for e in range(per):
        used = len_ref[first + pl.program_id(0) * per + e]
        q = q_ref[e]
        qf = q.astype(F32)
        fresh = new_ref[e].astype(F32)
        s = lax.dot_general(
            q, kv_ref[e, :, :HD], (((1,), (1,)), ((), ())), preferred_element_type=F32
        )
        s = jnp.where(pos < used, s, NEG)
        top = jnp.max(s, axis=1, keepdims=True)
        extra = []
        for t in range(STEPS):
            f = jnp.sum(qf * fresh[t:t + 1, :HD], axis=1, keepdims=True)
            f = jnp.where(step_id >= t, f, NEG)
            extra.append(f)
            top = jnp.maximum(top, f)
        p = jnp.exp2((s - top) * (ROOT * LOG2E)).astype(BF)
        r = jnp.dot(
            p, jnp.concatenate([kv_ref[e, :, HD:], ones], axis=1), preferred_element_type=F32
        )
        num, den = r[:, :HD], r[:, HD:]
        for t in range(STEPS):
            w = jnp.exp2((extra[t] - top) * (ROOT * LOG2E))
            num = num + w * fresh[t:t + 1, HD:]
            den = den + w
        o_ref[e] = num / den
        lse_ref[e] = top * ROOT + jnp.log(den)


def suffix_attention(suffix_len, q_rows, suffix_kv, new_kv, first, count):
    positions = suffix_kv.shape[1]
    per = 4
    skip = first // per
    one = jax.ShapeDtypeStruct((count, ROWS, HD), F32)
    grid_spec = pltpu.PrefetchScalarGridSpec(
        num_scalar_prefetch=1,
        grid=(count // per,),
        in_specs=[
            pl.BlockSpec((per, ROWS, HD), lambda s, n: (s + skip, 0, 0)),
            pl.BlockSpec((per, positions, 2 * HD), lambda s, n: (s + skip, 0, 0)),
            pl.BlockSpec((per, STEPS, 2 * HD), lambda s, n: (s + skip, 0, 0)),
        ],
        out_specs=[pl.BlockSpec((per, ROWS, HD), lambda s, n: (s, 0, 0))] * 2,
    )
    return pl.pallas_call(
        functools.partial(suffix_kernel, first),
        out_shape=[one, one],
        grid_spec=grid_spec,
        compiler_params=params(),
        cost_estimate=pl.CostEstimate(
            flops=count * 256 * positions * 128 * 4,
            bytes_accessed=count << 19,
            transcendentals=count * ROWS * positions,
        ),
        name="suffix_attention",
    )(suffix_len, q_rows, suffix_kv, new_kv)


def final_kernel(
    own_ref, off_ref, oa_ref, la_ref, ob_ref, lb_ref, part_ref, out_ref, data_ref, top_ref, wide_ref
):
    for t in range(8):
        data_ref[t] = part_ref[t, 0:128, :].astype(F32)
        rows = part_ref[t, 128:LAST, :].astype(F32)
        top_ref[t] = spread(read_lse(rows, 0))
    each = oa_ref.shape[0]
    for r in range(2 * each):
        o_ref, l_ref = (oa_ref, la_ref) if r < each else (ob_ref, lb_ref)
        at = pl.ds(pl.multiple_of(off_ref[r], ROWS), ROWS)
        op, lp = data_ref[own_ref[r], at, :], top_ref[own_ref[r], at, :]
        w, _ = blend_weights(lp, l_ref[r % each])
        ol = o_ref[r % each]
        wide_ref[r] = ol + w * (op - ol)
    for g in range(GROUP):
        out_ref[:, :, g * HD:(g + 1) * HD] = wide_ref[:, pl.ds(g, STEPS, GROUP), :].astype(BF)


def finish(own, off, local, parts):
    count = own.shape[0]
    return pl.pallas_call(
        final_kernel,
        out_shape=jax.ShapeDtypeStruct((count, STEPS, GROUP * HD), BF),
        in_specs=[pl.BlockSpec(memory_space=pltpu.SMEM)] * 2
        + [pl.BlockSpec(memory_space=pltpu.VMEM)] * 5,
        out_specs=pl.BlockSpec(memory_space=pltpu.VMEM),
        scratch_shapes=[
            pltpu.VMEM((8, HD, HD), F32),
            pltpu.VMEM((8, HD, HD), F32),
            pltpu.VMEM((count, ROWS, HD), F32),
        ],
        compiler_params=params(),
        name="finish",
    )(own, off, *local, parts)


def on_device(prefix_kv, prefix_len, prefix_of, suffix_len, suffix_kv, queries, new_kv):
    mine, block = lax.axis_index("pre"), lax.axis_index("req")
    shard = prefix_kv.shape[1]
    count = queries.shape[0]

    owners = prefix_of[:, 0]
    ids = jnp.arange(count, dtype=jnp.int32)
    earlier = (owners[None, :] == owners[:, None]) & (ids[None, :] < ids[:, None])
    rank = jnp.sum(earlier.astype(jnp.int32), axis=1)
    part = (owners & 1) * 2 + rank
    own_len = lax.dynamic_slice_in_dim(prefix_len, mine * 2, 2, 0)
    usable = jnp.clip(own_len - block * shard, 0, shard)

    q_rows, packed = pack(owners, queries)
    heads = lax.all_to_all(packed, "pre", 0, 0, tiled=True)
    local = []
    for first in (0, count // 2):
        local += suffix_attention(suffix_len, q_rows, suffix_kv, new_kv, first, count // 2)

    near = join([heads[None]] + three_ways([heads[None]] * 3), cuts=4, after=local[0])
    got = [quarter_step(near[k], k, 2) for k in range(4)]
    near = [join([near[k], got[k]])[0] for k in range(4)]
    far = [quarter_step(near[k], k, 3) for k in range(4)]
    keep = prefix_attention(usable, near[:2], prefix_kv, 0)
    send = prefix_attention(usable, far[:2], prefix_kv, 0, keep[0])
    send += prefix_attention(usable, far[2:], prefix_kv, 2)
    keep += prefix_attention(usable, near[2:], prefix_kv, 2)
    got = [quarter_step(send[k], k, 3) for k in range(4)]
    parts = [merge([keep[k], got[k]], [4, 4]) for k in range(4)]
    keep, send = [p[0] for p in parts], [p[1] for p in parts]
    got = [quarter_step(send[k], k, 2) for k in range(4)]
    parts = merge([x for pair in zip(keep, got) for x in pair], [1] * 4)
    final = merge_last([parts[0]] + three_ways(parts[1:]), local[2])
    back = lax.all_to_all(final, "pre", 0, 0, tiled=True)
    return finish(owners >> 1, part * ROWS, local, back)


def solution(mesh):
    placed = (
        P("pre", "req", None),
        P(),
        P("req", None),
        P("req"),
        P("req", None, "pre"),
        P("req", None, "pre"),
        P("req", None, "pre"),
    )
    return jax.shard_map(
        on_device, mesh=mesh, in_specs=placed, out_specs=P("req", None, "pre"), check_vma=False
    )
```

```python
import functools
import math

import jax
import jax.numpy as jnp
from jax import lax
from jax.experimental import pallas as pl
from jax.experimental.pallas import tpu as pltpu
from jax.sharding import PartitionSpec as P

HD = 128
GROUP = 8
STEPS = 4
ROWS = STEPS * GROUP
NEG = -1e30
ROOT = 1.0 / math.sqrt(HD)
LOG2E = math.log2(math.e)
EMPTY = 128.0
LAST = 144
BF = jnp.bfloat16
F32 = jnp.float32


def params(mb=48):
    return pltpu.CompilerParams(vmem_limit_bytes=mb * 1024 * 1024)


FLIPS = (1, 4, 3, 12)


def req_step(x, turns):
    pairs = []
    for i in range(8):
        flip = 0
        for turn in turns:
            flip ^= FLIPS[(2 * (i & 1) + turn) % 4]
        pairs += [(i * 16 + j, i * 16 + (j ^ flip)) for j in range(16)]
    return lax.ppermute(x, ("pre", "req"), pairs)


def quarter_step(x, k, turn):
    return req_step(x, [turn if k % 2 == 0 else 5 - turn])


def three_ways(xs):
    return [req_step(x, way) for x, way in zip(xs, ([0], [1], [0, 1]))]


def split3(x):
    hi = x.astype(BF).astype(F32)
    mid = (x - hi).astype(BF).astype(F32)
    low = (x - hi - mid).astype(BF).astype(F32)
    return hi, mid, low


def pack_kernel(of_ref, q_ref, rows_ref, out_ref, wide_ref, seen_ref, req_ref):
    count = q_ref.shape[0]
    for p in range(16):
        seen_ref[p] = 0
    for slot in range(32):
        req_ref[slot] = -1
    for r in range(count):
        p = of_ref[r]
        rank = seen_ref[p]
        seen_ref[p] = rank + 1
        req_ref[p * 2 + rank] = r
    for g in range(GROUP):
        wide_ref[:, pl.ds(g, STEPS, GROUP), :] = q_ref[:, :, g * HD:(g + 1) * HD].astype(F32)
    rows_ref[...] = wide_ref[...].astype(BF)
    nobody = jnp.full((ROWS, HD), EMPTY, BF)
    for slot in range(32):
        r = req_ref[slot]
        rows = rows_ref[jnp.maximum(r, 0)]
        at = (slot % 4) * ROWS
        out_ref[slot // 4, at:at + ROWS, :] = jnp.where(r >= 0, rows, nobody)


def pack(owners, queries):
    count = queries.shape[0]
    return pl.pallas_call(
        pack_kernel,
        out_shape=[
            jax.ShapeDtypeStruct((count, ROWS, HD), BF),
            jax.ShapeDtypeStruct((8, 128, HD), BF),
        ],
        in_specs=[pl.BlockSpec(memory_space=pltpu.SMEM), pl.BlockSpec(memory_space=pltpu.VMEM)],
        out_specs=[pl.BlockSpec(memory_space=pltpu.VMEM)] * 2,
        scratch_shapes=[
            pltpu.VMEM((count, ROWS, HD), F32),
            pltpu.SMEM((16,), jnp.int32),
            pltpu.SMEM((32,), jnp.int32),
        ],
        compiler_params=params(),
        name="pack_slots",
    )(owners, queries)


def join_kernel(groups, cuts, total, *refs):
    out_refs = refs[-groups * cuts:]
    ins = refs[:total]
    count = total // groups
    each = ins[0].shape[0]
    width = ins[0].shape[1] // cuts
    for g in range(groups):
        for c in range(cuts):
            for n in range(count):
                piece = ins[g * count + n][:, c * width:(c + 1) * width]
                out_refs[g * cuts + c][n * each:(n + 1) * each] = piece


def join(parts, groups=1, cuts=1, after=None):
    extra = [] if after is None else [after]
    first = parts[0].shape
    shape = (len(parts) // groups * first[0], first[1] // cuts) + first[2:]
    return pl.pallas_call(
        functools.partial(join_kernel, groups, cuts, len(parts)),
        out_shape=[jax.ShapeDtypeStruct(shape, BF)] * (groups * cuts),
        in_specs=[pl.BlockSpec(memory_space=pltpu.VMEM)] * len(parts)
        + [pl.BlockSpec(memory_space=pl.ANY)] * len(extra),
        out_specs=[pl.BlockSpec(memory_space=pltpu.VMEM)] * (groups * cuts),
        compiler_params=params(),
        name="join",
    )(*parts, *extra)


def prefix_kernel(count, first, extra, use_ref, *rest):
    q_refs, kv_hbm = rest[:count], rest[count]
    rest = rest[count + 1 + extra:]
    out_refs = rest[:count]
    kv_all, sa_ref, sb_ref, bias_ref, lse_ref, group_ref, many_ref, sems = rest[
        count:
    ]
    heads = 2 * count
    positions = kv_all.shape[1]
    blocks = q_refs[0].shape[0]
    rows = blocks * ROWS

    def fetch(m, h):
        at = pl.multiple_of((2 * first + h) * (2 * HD), 2 * HD)
        return pltpu.make_async_copy(
            kv_hbm.at[m, :, pl.ds(at, 2 * HD)], kv_all.at[m * heads + h], sems.at[m * heads + h]
        )

    for m in range(2):

        @pl.when(use_ref[m] > 0)
        def _():
            for h in range(heads):
                fetch(m, h).start()

    marks = [
        jnp.min(q_refs[0][:, 0, w * ROWS:w * ROWS + 16, :].astype(F32)) < 100.0 for w in range(4)
    ]
    live = [(use_ref[w // 2] > 0) & marks[w] for w in range(4)]

    many_ref[0] = 0
    for m in range(2):
        for rank in range(2):
            on = live[m * 2 + rank]

            @pl.when(on)
            def _():
                n = many_ref[0]
                group_ref[n] = m * 2 + rank
                many_ref[0] = n + 1

            @pl.when(jnp.logical_not(on))
            def _():
                for side in range(2):
                    at = m * 128 + side * 64 + rank * ROWS
                    for c in range(count):
                        out_refs[c][:, at:at + ROWS, :] = jnp.zeros((blocks, ROWS, HD), BF)

    for m in range(2):
        pos = lax.broadcasted_iota(jnp.int32, (8, positions), 1)
        bias_ref[m] = jnp.where(pos < use_ref[m], 0.0, NEG)
    lse_ref[...] = jnp.full(lse_ref.shape, NEG, F32)
    n = many_ref[0]

    def decode(i):
        which = group_ref[jnp.minimum(i, n - 1)]
        return which, which >> 1, which & 1

    def arrive(i, hs):
        which, m, rank = decode(i)

        @pl.when((rank == 0) & (i < n))
        def _():
            for h in hs:
                fetch(m, h).wait()

    def score(i, h, s_ref):
        which, m, rank = decode(i)
        at = pl.ds(pl.multiple_of(which * ROWS, ROWS), ROWS)
        q = q_refs[h // 2][:, h % 2, at, :].reshape(rows, HD)
        k = kv_all[m * heads + h, :, :HD]
        s = lax.dot_general(q, k, (((1,), (1,)), ((), ())), preferred_element_type=F32)
        s = s.reshape(rows // 8, 8, positions) + bias_ref[m][None]
        s_ref[...] = s.reshape(rows, positions)

    def weigh(i, h, s_ref):
        which, m, rank = decode(i)
        c, side = h // 2, h % 2
        s = s_ref[...]
        top = jnp.max(s, axis=1, keepdims=True)
        p = jnp.exp2((s - top) * (ROOT * LOG2E)).astype(BF)
        v = kv_all[m * heads + h, :, HD:]
        v1 = jnp.concatenate([v, jnp.ones((positions, HD), BF)], axis=1)
        r = jnp.dot(p, v1, preferred_element_type=F32)
        den = r[:, HD:]
        o = r[:, :HD] / den
        lse = top * ROOT + jnp.log(den)
        at = pl.multiple_of(m * 128 + side * 64 + rank * ROWS, ROWS)
        out_refs[c][:, pl.ds(at, ROWS), :] = o.reshape(blocks, ROWS, HD).astype(BF)
        part = side * 2 + rank
        row_id = lax.broadcasted_iota(jnp.int32, (ROWS, HD), 0)
        lane_id = lax.broadcasted_iota(jnp.int32, (ROWS, HD), 1)
        diag = (lane_id - row_id == part * ROWS)[None]
        flat = jnp.sum(jnp.where(diag, lse.reshape(blocks, ROWS, HD), 0.0), axis=1)
        lanes = lax.broadcasted_iota(jnp.int32, (blocks, HD), 1) >> 5
        old = lse_ref[c * 2 + m]
        lse_ref[c * 2 + m] = jnp.where(lanes == part, flat, old)

    for m in range(2):

        @pl.when((use_ref[m] > 0) & jnp.logical_not(live[2 * m]))
        def _():
            for h in range(heads):
                fetch(m, h).wait()

    @pl.when(n > 0)
    def _():
        arrive(0, [0])
        score(0, 0, sa_ref)

        def body(j, carry):
            arrive(j, range(1, heads))
            arrive(j + 1, [0])
            for h in range(heads):
                now, later = (sa_ref, sb_ref) if h % 2 == 0 else (sb_ref, sa_ref)
                if h + 1 < heads:
                    score(j, h + 1, later)
                else:
                    score(j + 1, 0, later)
                weigh(j, h, now)
            return carry

        lax.fori_loop(0, n, body, 0)

    for c in range(count):
        out_refs[c][:, 256:, :] = lse_rows([lse_ref[2 * c + m][:, None, :] for m in range(2)])


def lse_rows(tops):
    shape = (tops[0].shape[0], -(-3 * len(tops) // 16) * 16, HD)
    row = lax.broadcasted_iota(jnp.int32, shape, 1)
    out = jnp.zeros(shape, F32)
    at = 0
    for top in tops:
        for piece in split3(top):
            out = jnp.where(row == at, jnp.broadcast_to(piece, shape), out)
            at += 1
    return out.astype(BF)


def prefix_attention(usable, qs, prefix_kv, first, after=None):
    count = len(qs)
    extra = [] if after is None else [after]
    heads = 2 * count
    blocks = qs[0].shape[0]
    positions = prefix_kv.shape[1]
    rows = blocks * ROWS
    work = rows * positions * heads * 3
    return pl.pallas_call(
        functools.partial(prefix_kernel, count, first, len(extra)),
        out_shape=[jax.ShapeDtypeStruct((blocks, 272, HD), BF)] * count,
        in_specs=[pl.BlockSpec(memory_space=pltpu.SMEM)]
        + [pl.BlockSpec(memory_space=pltpu.VMEM)] * count
        + [pl.BlockSpec(memory_space=pl.ANY)] * (1 + len(extra)),
        out_specs=[pl.BlockSpec(memory_space=pltpu.VMEM)] * count,
        scratch_shapes=[
            pltpu.VMEM((2 * heads, positions, 2 * HD), BF),
            pltpu.VMEM((rows, positions), F32),
            pltpu.VMEM((rows, positions), F32),
            pltpu.VMEM((2, 8, positions), F32),
            pltpu.VMEM((heads, blocks, HD), F32),
            pltpu.SMEM((4,), jnp.int32),
            pltpu.SMEM((1,), jnp.int32),
            pltpu.SemaphoreType.DMA((2 * heads,)),
        ],
        compiler_params=params(),
        cost_estimate=pl.CostEstimate(
            flops=work * 512, bytes_accessed=heads << 20, transcendentals=work
        ),
        name="prefix_attention",
    )(usable, *qs, prefix_kv, *extra)


def blend_weights(la, lb):
    top = jnp.maximum(la, lb)
    ea, eb = jnp.exp(la - top), jnp.exp(lb - top)
    total = ea + eb
    return ea / total, top + jnp.log(total)


def spread(w):
    return jnp.broadcast_to(w, (HD, HD)).T


def read_lse(rows, m):
    return rows[3 * m:3 * m + 1] + rows[3 * m + 1:3 * m + 2] + rows[3 * m + 2:3 * m + 3]


def merge_line(a_ref, b_ref, idx):
    tiles = a_ref.shape[1] // 128
    ra = a_ref[idx, tiles * 128:, :].astype(F32)
    rb = b_ref[idx, tiles * 128:, :].astype(F32)
    datas, tops = [], []
    for m in range(tiles):
        wa, lse = blend_weights(read_lse(ra, m), read_lse(rb, m))
        oa = a_ref[idx, m * 128:(m + 1) * 128, :].astype(F32)
        ob = b_ref[idx, m * 128:(m + 1) * 128, :].astype(F32)
        datas.append(ob + spread(wa) * (oa - ob))
        tops.append(lse)
    return datas, tops


def merge_kernel(pairs, extra, *refs):
    ins, out_refs = refs[:2 * pairs], refs[2 * pairs + extra:]
    outs = [(ref, b) for ref in out_refs for b in range(ref.shape[0])]
    for spot, (out_ref, b) in reversed(list(enumerate(outs))):
        merged = [merge_line(ins[2 * c], ins[2 * c + 1], spot) for c in range(pairs)]
        datas = [d for row in zip(*[x[0] for x in merged]) for d in row]
        tops = [t for row in zip(*[x[1] for x in merged]) for t in row]
        tiles = len(datas)
        for m in range(tiles):
            out_ref[b, m * 128:(m + 1) * 128, :] = datas[m].astype(BF)
        out_ref[b, tiles * 128:, :] = lse_rows([t[None] for t in tops])[0]


def merge(ins, counts, after=None):
    extra = [] if after is None else [after]
    blocks, line = ins[0].shape[:2]
    pairs = len(ins) // 2
    tiles = (line // 128) * pairs
    extra_rows = -(-3 * tiles // 16) * 16
    return pl.pallas_call(
        functools.partial(merge_kernel, pairs, len(extra)),
        out_shape=[jax.ShapeDtypeStruct((n, tiles * 128 + extra_rows, HD), BF) for n in counts],
        in_specs=[pl.BlockSpec(memory_space=pltpu.VMEM)] * len(ins)
        + [pl.BlockSpec(memory_space=pl.ANY)] * len(extra),
        out_specs=[pl.BlockSpec(memory_space=pltpu.VMEM)] * len(counts),
        compiler_params=params(),
        cost_estimate=pl.CostEstimate(
            flops=blocks * tiles * 128 * 128 * 6,
            bytes_accessed=blocks * tiles * 128 * HD * 6,
            transcendentals=0,
        ),
        name="merge_step",
    )(*ins, *extra)


def last_kernel(*refs):
    parts, out_ref = refs[:4], refs[5]
    low = lax.broadcasted_iota(jnp.int32, (1, HD), 1) < 64
    rows = [p[0, 1024:, :].astype(F32) for p in parts]
    datas, tops = [], []
    for t in range(8):
        each = [read_lse(r, t) for r in rows]
        top = functools.reduce(jnp.maximum, each)
        es = [jnp.exp(x - top) for x in each]
        total = es[0] + es[1] + es[2] + es[3]
        blocks = [p[0, t * 128:(t + 1) * 128, :].astype(F32) for p in parts]
        data = blocks[3]
        for block, e in zip(blocks[:3], es):
            data = data + spread(e / total) * (block - blocks[3])
        datas.append(data)
        tops.append(top + jnp.log(total))
    rolled = [pltpu.roll(jnp.broadcast_to(t, (8, HD)), 64, 1)[0:1] for t in tops]
    for h in range(8):
        k, side = h // 2, h % 2
        if side == 0:
            joined = jnp.where(low, tops[k], rolled[4 + k])
        else:
            joined = jnp.where(low, rolled[k], tops[4 + k])
        for m in range(2):
            piece = datas[4 * m + k][side * 64:(side + 1) * 64]
            out_ref[h, m * 64:(m + 1) * 64, :] = piece.astype(BF)
        out_ref[h, 128:LAST, :] = lse_rows([joined[None]])[0]


def merge_last(parts, after):
    return pl.pallas_call(
        last_kernel,
        out_shape=jax.ShapeDtypeStruct((8, LAST, HD), BF),
        in_specs=[pl.BlockSpec(memory_space=pltpu.VMEM)] * 4
        + [pl.BlockSpec(memory_space=pl.ANY)],
        out_specs=pl.BlockSpec(memory_space=pltpu.VMEM),
        compiler_params=params(),
        name="merge_last",
    )(*parts, after)


def suffix_kernel(first, len_ref, q_ref, kv_ref, new_ref, o_ref, lse_ref):
    per = q_ref.shape[0]
    positions = kv_ref.shape[1]
    step_id = lax.broadcasted_iota(jnp.int32, (ROWS, 1), 0) // GROUP
    pos = lax.broadcasted_iota(jnp.int32, (ROWS, positions), 1)
    ones = jnp.ones((positions, HD), BF)
    for e in range(per):
        used = len_ref[first + pl.program_id(0) * per + e]
        q = q_ref[e]
        qf = q.astype(F32)
        fresh = new_ref[e].astype(F32)
        s = lax.dot_general(
            q, kv_ref[e, :, :HD], (((1,), (1,)), ((), ())), preferred_element_type=F32
        )
        s = jnp.where(pos < used, s, NEG)
        top = jnp.max(s, axis=1, keepdims=True)
        extra = []
        for t in range(STEPS):
            f = jnp.sum(qf * fresh[t:t + 1, :HD], axis=1, keepdims=True)
            f = jnp.where(step_id >= t, f, NEG)
            extra.append(f)
            top = jnp.maximum(top, f)
        p = jnp.exp2((s - top) * (ROOT * LOG2E)).astype(BF)
        r = jnp.dot(
            p, jnp.concatenate([kv_ref[e, :, HD:], ones], axis=1), preferred_element_type=F32
        )
        num, den = r[:, :HD], r[:, HD:]
        for t in range(STEPS):
            w = jnp.exp2((extra[t] - top) * (ROOT * LOG2E))
            num = num + w * fresh[t:t + 1, HD:]
            den = den + w
        o_ref[e] = num / den
        lse_ref[e] = top * ROOT + jnp.log(den)


def suffix_attention(suffix_len, q_rows, suffix_kv, new_kv, first, count):
    positions = suffix_kv.shape[1]
    per = 4
    skip = first // per
    one = jax.ShapeDtypeStruct((count, ROWS, HD), F32)
    grid_spec = pltpu.PrefetchScalarGridSpec(
        num_scalar_prefetch=1,
        grid=(count // per,),
        in_specs=[
            pl.BlockSpec((per, ROWS, HD), lambda s, n: (s + skip, 0, 0)),
            pl.BlockSpec((per, positions, 2 * HD), lambda s, n: (s + skip, 0, 0)),
            pl.BlockSpec((per, STEPS, 2 * HD), lambda s, n: (s + skip, 0, 0)),
        ],
        out_specs=[pl.BlockSpec((per, ROWS, HD), lambda s, n: (s, 0, 0))] * 2,
    )
    return pl.pallas_call(
        functools.partial(suffix_kernel, first),
        out_shape=[one, one],
        grid_spec=grid_spec,
        compiler_params=params(),
        cost_estimate=pl.CostEstimate(
            flops=count * 256 * positions * 128 * 4,
            bytes_accessed=count << 19,
            transcendentals=count * ROWS * positions,
        ),
        name="suffix_attention",
    )(suffix_len, q_rows, suffix_kv, new_kv)


def final_kernel(
    own_ref, off_ref, oa_ref, la_ref, ob_ref, lb_ref, part_ref, out_ref, data_ref, top_ref, wide_ref
):
    for t in range(8):
        data_ref[t] = part_ref[t, 0:128, :].astype(F32)
        rows = part_ref[t, 128:LAST, :].astype(F32)
        top_ref[t] = spread(read_lse(rows, 0))
    each = oa_ref.shape[0]
    for r in range(2 * each):
        o_ref, l_ref = (oa_ref, la_ref) if r < each else (ob_ref, lb_ref)
        at = pl.ds(pl.multiple_of(off_ref[r], ROWS), ROWS)
        op, lp = data_ref[own_ref[r], at, :], top_ref[own_ref[r], at, :]
        w, _ = blend_weights(lp, l_ref[r % each])
        ol = o_ref[r % each]
        wide_ref[r] = ol + w * (op - ol)
    for g in range(GROUP):
        out_ref[:, :, g * HD:(g + 1) * HD] = wide_ref[:, pl.ds(g, STEPS, GROUP), :].astype(BF)


def finish(own, off, local, parts):
    count = own.shape[0]
    return pl.pallas_call(
        final_kernel,
        out_shape=jax.ShapeDtypeStruct((count, STEPS, GROUP * HD), BF),
        in_specs=[pl.BlockSpec(memory_space=pltpu.SMEM)] * 2
        + [pl.BlockSpec(memory_space=pltpu.VMEM)] * 5,
        out_specs=pl.BlockSpec(memory_space=pltpu.VMEM),
        scratch_shapes=[
            pltpu.VMEM((8, HD, HD), F32),
            pltpu.VMEM((8, HD, HD), F32),
            pltpu.VMEM((count, ROWS, HD), F32),
        ],
        compiler_params=params(),
        name="finish",
    )(own, off, *local, parts)


def on_device(prefix_kv, prefix_len, prefix_of, suffix_len, suffix_kv, queries, new_kv):
    mine, block = lax.axis_index("pre"), lax.axis_index("req")
    shard = prefix_kv.shape[1]
    count = queries.shape[0]

    owners = prefix_of[:, 0]
    ids = jnp.arange(count, dtype=jnp.int32)
    earlier = (owners[None, :] == owners[:, None]) & (ids[None, :] < ids[:, None])
    rank = jnp.sum(earlier.astype(jnp.int32), axis=1)
    part = (owners & 1) * 2 + rank
    own_len = lax.dynamic_slice_in_dim(prefix_len, mine * 2, 2, 0)
    usable = jnp.clip(own_len - block * shard, 0, shard)

    q_rows, packed = pack(owners, queries)
    heads = lax.all_to_all(packed, "pre", 0, 0, tiled=True)
    local = []
    for first in (0, count // 2):
        local += suffix_attention(suffix_len, q_rows, suffix_kv, new_kv, first, count // 2)

    near = join([heads[None]] + three_ways([heads[None]] * 3), cuts=4, after=local[0])
    got = [quarter_step(near[k], k, 2) for k in range(4)]
    near = [join([near[k], got[k]])[0] for k in range(4)]
    far = [quarter_step(near[k], k, 3) for k in range(4)]
    keep = prefix_attention(usable, near[:2], prefix_kv, 0)
    send = prefix_attention(usable, far[:2], prefix_kv, 0, keep[0])
    send += prefix_attention(usable, far[2:], prefix_kv, 2)
    keep += prefix_attention(usable, near[2:], prefix_kv, 2)
    got = [quarter_step(send[k], k, 3) for k in range(4)]
    parts = [merge([keep[k], got[k]], [4, 4]) for k in range(4)]
    keep, send = [p[0] for p in parts], [p[1] for p in parts]
    got = [quarter_step(send[k], k, 2) for k in range(4)]
    parts = merge([x for pair in zip(keep, got) for x in pair], [1] * 4)
    final = merge_last([parts[0]] + three_ways(parts[1:]), local[2])
    back = lax.all_to_all(final, "pre", 0, 0, tiled=True)
    return finish(owners >> 1, part * ROWS, local, back)


def solution(mesh):
    placed = (
        P("pre", "req", None),
        P(),
        P("req", None),
        P("req"),
        P("req", None, "pre"),
        P("req", None, "pre"),
        P("req", None, "pre"),
    )
    return jax.shard_map(
        on_device, mesh=mesh, in_specs=placed, out_specs=P("req", None, "pre"), check_vma=False
    )
```
